32 devices in a mesh: row: 2 (over y), chan: 4 (over z), dp: 4 (over x, core).
Axes of the slice: x: 2, y: 2, z: 4, core: 2. Of those that a mesh axis runs over, the one named last changes fastest.
Arguments:
- features_in: bfloat16 [4, 36, 64, 2048], P('dp', 'row', None, 'chan'), may hold values from -6 to 6
- depth_weights: bfloat16 [3, 3, 3, 2048], P(None, None, None, 'chan'), may hold values from -2 to 2
- point_weights: bfloat16 [4, 2048, 256], P(None, 'chan'), may hold values from -0.125 to 0.125
- proj_weights: bfloat16 [4, 256, 256], replicated, may hold values from -0.1875 to 0.1875
- cotangent: bfloat16 [4, 36, 64, 256], P('dp', 'row', 'chan'), may hold values from -18 to 18
Outputs:
- output: bfloat16 [4, 36, 64, 256], P('dp', 'row', 'chan')
- grad_input: bfloat16 [4, 36, 64, 2048], P('dp', 'row', None, 'chan')
- grad_depth: float32 [3, 3, 3, 2048], P(None, None, None, 'chan')
- grad_point: float32 [4, 2048, 256], P(None, 'chan')
- grad_proj: float32 [4, 256, 256], replicated
The draws below stay inside these ranges and needn't reach their ends.
All inputs are finite; a program needn't handle non-finite values.
Results may differ from the reference program's by a relative error of at most 0.0059.
Values may be sent and summed in bfloat16 or wider, within the bound.
No kernel may reach another device: no remote copies, remote signals or barrier semaphores. Data moves between devices by JAX's collectives and lax.ppermute only.
A program may use at most 64 MiB of HBM per device.

```python
import math
import jax
import jax.numpy as jnp
from jax import lax

C = 2048
F = 256
BASE_DILATION = 12
COLS = 64
H = 36
SAMPLES = 4


def block_levels(key, shape, pieces, low, largest):
    def one(dim, shards_of):
        draws = jax.random.uniform(jax.random.fold_in(jax.random.fold_in(key, 6), dim), (shards_of,), jnp.float32, low / len(pieces), largest / len(pieces))
        return jnp.repeat(jnp.exp(draws), shape[dim] // shards_of).reshape((-1,) + (1,) * (len(shape) - dim - 1))

    factor_of = one(*pieces[0])
    for cut in pieces[1:]:
        factor_of = factor_of * one(*cut)
    return factor_of


def bell_draw(stream_key, shape, deviation, reach, shards=(), kind=jnp.bfloat16):
    loudness = block_levels(stream_key, shape, shards, -0.22, 0.18) if shards else 1.0
    result = jax.random.normal(stream_key, shape, jnp.float32) * deviation * loudness
    return jnp.minimum(jnp.maximum(result, -reach), reach).astype(kind)


def setup_inputs(seed: int = 0) -> dict:
    key_of = jax.random.split(jax.random.key(seed), 6)
    return {
        "features_in": bell_draw(key_of[0], (SAMPLES, H, COLS, C), 1.0, 6.0, ((0, 4), (1, 2), (3, 4))),
        "depth_weights": bell_draw(key_of[1], (3, 3, 3, C), 9 ** -0.5, 2.0, ((3, 4),)),
        "point_weights": bell_draw(key_of[2], (4, C, F), C ** -0.5, 0.125, ((1, 4),)),
        "proj_weights": bell_draw(key_of[3], (4, F, F), (4 * F) ** -0.5, 0.1875),
        "cotangent": bell_draw(key_of[4], (SAMPLES, H, COLS, F), 3.0, 18.0, ((0, 4), (1, 2), (2, 4))),
    }


def shifted(padded, top, left, band_rows, band_cols):
    return lax.slice(padded, (top, left, 0), (top + band_rows, left + band_cols, padded.shape[2]))

def per_sample(sample_in, sample_cot, depth_weights, point_weights, proj_weights):
    band_rows, band_cols, channels = sample_in.shape
    largest_reach = 3 * BASE_DILATION
    padded = jnp.pad(sample_in, ((largest_reach, largest_reach), (largest_reach, largest_reach), (0, 0)))
    branch_maps = [sample_in]
    for branch_level in range(3):
        tap_spacing = (branch_level + 1) * BASE_DILATION
        summed = jnp.zeros((band_rows, band_cols, channels), jnp.float32)
        for row_tap in range(3):
            for col_tap in range(3):
                input_kernel_tap = shifted(padded, largest_reach + (row_tap - 1) * tap_spacing, largest_reach + (col_tap - 1) * tap_spacing, band_rows, band_cols)
                summed = summed + input_kernel_tap.astype(jnp.float32) * depth_weights[branch_level, row_tap, col_tap].astype(jnp.float32)
        branch_maps.append(summed.astype(jnp.bfloat16))
    spread = jnp.stack(branch_maps)
    point32 = point_weights.astype(jnp.float32)
    proj32 = proj_weights.astype(jnp.float32)
    preact = jnp.einsum('brwc,bcf->brwf', spread.astype(jnp.float32), point32)
    activation = jax.nn.silu(preact).astype(jnp.bfloat16)
    output = jnp.einsum('brwf,bfg->rwg', activation.astype(jnp.float32), proj32).astype(jnp.bfloat16)
    cot32 = sample_cot.astype(jnp.float32)
    silu_gradient = jnp.einsum('rwg,bfg->brwf', cot32, proj32)
    logistic = jax.nn.sigmoid(preact)
    pre_grad = (silu_gradient * logistic * (1.0 + preact * (1.0 - logistic))).astype(jnp.bfloat16)
    grad_proj = jnp.einsum('brwf,rwg->bfg', activation.astype(jnp.float32), cot32)
    spread_grad = jnp.einsum('brwf,bcf->brwc', pre_grad.astype(jnp.float32), point32).astype(jnp.bfloat16)
    grad_point = jnp.einsum('brwc,brwf->bcf', spread.astype(jnp.float32), pre_grad.astype(jnp.float32))
    grad_in = spread_grad[0].astype(jnp.float32)
    depth_rows = []
    for branch_level in range(3):
        tap_spacing = (branch_level + 1) * BASE_DILATION
        branch_grad = spread_grad[branch_level + 1]
        grad_padded = jnp.pad(branch_grad, ((largest_reach, largest_reach), (largest_reach, largest_reach), (0, 0)))
        gathered = []
        for row_tap in range(3):
            for col_tap in range(3):
                grad_tap = shifted(grad_padded, largest_reach - (row_tap - 1) * tap_spacing, largest_reach - (col_tap - 1) * tap_spacing, band_rows, band_cols)
                grad_in = grad_in + grad_tap.astype(jnp.float32) * depth_weights[branch_level, row_tap, col_tap].astype(jnp.float32)
                input_kernel_tap = shifted(padded, largest_reach + (row_tap - 1) * tap_spacing, largest_reach + (col_tap - 1) * tap_spacing, band_rows, band_cols)
                gathered.append(lax.optimization_barrier(jnp.sum(input_kernel_tap.astype(jnp.float32) * branch_grad.astype(jnp.float32), axis=(0, 1))))
        depth_rows.append(jnp.stack(gathered).reshape(3, 3, channels))
    grad_depth = jnp.stack(depth_rows)
    return (output, grad_in.astype(jnp.bfloat16), grad_depth, grad_point, grad_proj)

def reference(features_in, depth_weights, point_weights, proj_weights, cotangent):

    def apply_one(pair):
        return per_sample(pair[0], pair[1], depth_weights, point_weights, proj_weights)
    results = lax.map(apply_one, (features_in, cotangent))
    weight_scale = 1.0 / math.sqrt(SAMPLES * H * COLS)
    output = results[0]
    grad_input = results[1]
    grad_depth = lax.optimization_barrier(jnp.sum(results[2], axis=0)) * weight_scale
    grad_point = lax.optimization_barrier(jnp.sum(results[3], axis=0)) * weight_scale
    grad_proj = lax.optimization_barrier(jnp.sum(results[4], axis=0)) * weight_scale
    return (output, grad_input, grad_depth, grad_point, grad_proj)
```

```python
import functools
import math

import jax
import jax.numpy as jnp
from jax import lax
from jax.experimental import pallas as pl
from jax.experimental.pallas import tpu as pltpu
from jax.sharding import PartitionSpec as P

BASE_DILATION = 12
F32 = jnp.float32
BF16 = jnp.bfloat16


def swap(value, axis, flip):
    count = lax.axis_size(axis)
    return lax.ppermute(value, axis, [(i, i ^ flip) for i in range(count)])


def swap_diagonal(value):
    dp = lax.axis_size("dp")
    pairs = [(r * dp + d, (r ^ 1) * dp + (d ^ 2)) for r in range(2) for d in range(dp)]
    return lax.ppermute(value, ("row", "dp"), pairs)


def moved(value, steps):
    if steps == 0:
        return value
    count = value.shape[0]
    rolled = pltpu.roll(value, (-steps) % count, 0)
    place = lax.broadcasted_iota(jnp.int32, value.shape, 0)
    inside = place < count - steps if steps > 0 else place >= -steps
    return jnp.where(inside, rolled, 0.0)


def row_pairs(branch, classes):
    return [
        (q, i, q + (i - 1) * branch)
        for q in range(classes)
        for i in range(3)
        if 0 <= q + (i - 1) * branch < classes
    ]


def forward_kernel(branch, half_ref, x_ref, taps_ref, point_ref, *outs):
    classes, _, cols, channels = x_ref.shape
    if branch:
        spread_ref, keep_ref, send_ref = outs
        spacing = branch * BASE_DILATION
        rows = [x_ref[q, 0].astype(F32) for q in range(classes)]
        for q in range(classes):
            total = None
            for j in range(3):
                part = None
                for out, i, source in row_pairs(branch, classes):
                    if out == q:
                        term = rows[source] * taps_ref[i * 3 + j, :][None, :]
                        part = term if part is None else part + term
                part = moved(part, (j - 1) * spacing)
                total = part if total is None else total + part
            spread_ref[q, 0] = total.astype(BF16)
        source_ref = spread_ref
    else:
        keep_ref, send_ref = outs
        source_ref = x_ref
    cells = source_ref[...].reshape(classes * cols, channels)
    partial = jnp.dot(cells, point_ref[...], preferred_element_type=F32)
    split = partial.reshape(classes * 2, 2, cols // 4, partial.shape[-1])
    first = half_ref[0] == 0
    keep = jnp.where(first, split[:, 0], split[:, 1])
    send = jnp.where(first, split[:, 1], split[:, 0])
    keep_ref[...] = keep.reshape(keep_ref.shape)
    send_ref[...] = send.reshape(send_ref.shape).astype(BF16)


def forward(branch, half, x, taps, point):
    classes, residues, cols, channels = x.shape
    filters = point.shape[1]
    block = lambda r, h: (0, r, 0, 0)
    part = lambda r, h: (0, r, 0, 0, 0)
    part_spec = pl.BlockSpec((classes, 1, 2, cols // 4, filters), part)
    part_shape = (classes, residues, 2, cols // 4, filters)
    out_specs = [part_spec, part_spec]
    out_shape = [jax.ShapeDtypeStruct(part_shape, F32), jax.ShapeDtypeStruct(part_shape, BF16)]
    if branch:
        out_specs = [pl.BlockSpec((classes, 1, cols, channels), block)] + out_specs
        out_shape = [jax.ShapeDtypeStruct(x.shape, BF16)] + out_shape
    return pl.pallas_call(
        functools.partial(forward_kernel, branch),
        grid_spec=pltpu.PrefetchScalarGridSpec(
            num_scalar_prefetch=1,
            grid=(residues,),
            in_specs=[
                pl.BlockSpec((classes, 1, cols, channels), block),
                pl.BlockSpec(taps.shape, lambda r, h: (0, 0)),
                pl.BlockSpec(point.shape, lambda r, h: (0, 0)),
            ],
            out_specs=out_specs,
        ),
        out_shape=out_shape,
        compiler_params=pltpu.CompilerParams(vmem_limit_bytes=48 * 2**20),
        cost_estimate=pl.CostEstimate(
            flops=2 * x.size * filters, bytes_accessed=6 * x.size, transcendentals=0
        ),
        name=f"forward_{branch}",
    )(half, x, taps, point)


def whole_columns(half_ref, own, other):
    first = half_ref[0] == 0
    low = jnp.where(first, own, other)
    high = jnp.where(first, other, own)
    both = jnp.concatenate([low[:, None], high[:, None]], axis=1)
    return both.reshape(-1, own.shape[-1])


def backward_kernel(
    branch, half_ref, own_ref, other_ref, x_ref, spread_ref, taps_ref, point_ref, before_ref,
    input_ref, point_grad_ref, depth_ref,
):
    classes, _, cols, channels = x_ref.shape
    step = pl.program_id(0)
    spacing = branch * BASE_DILATION
    thin = (classes * 2, cols // 4, own_ref.shape[-1])
    pre = whole_columns(half_ref, own_ref[...].reshape(thin), other_ref[...].reshape(thin))
    grads = lax.dot_general(pre, point_ref[...], (((1,), (1,)), ((), ())), preferred_element_type=F32)
    grads = grads.astype(BF16).astype(F32).reshape(classes, cols, channels)
    cells = spread_ref[...].reshape(classes * cols, channels)
    product = lax.dot_general(cells, pre, (((0,), (0,)), ((), ())), preferred_element_type=F32)

    @pl.when(step == 0)
    def _():
        point_grad_ref[...] = jnp.zeros_like(point_grad_ref)
        depth_ref[...] = jnp.zeros_like(depth_ref)

    point_grad_ref[...] += product
    pairs = row_pairs(branch, classes)
    rows = [x_ref[q, 0].astype(F32) for q in range(classes)]
    for j in range(3):
        near = [moved(row, (j - 1) * spacing) for row in rows]
        for i in range(3):
            part = None
            for q, tap, source in pairs:
                if tap == i:
                    term = (near[source] * grads[q]).reshape(cols // 8, 8, channels).sum(axis=0)
                    part = term if part is None else part + term
            if part is not None:
                depth_ref[i * 3 + j] += part
    for target in range(classes):
        total = before_ref[target, 0]
        for j in range(3):
            part = None
            for q, i, source in pairs:
                if source == target:
                    term = grads[q] * taps_ref[i * 3 + j, :][None, :]
                    part = term if part is None else part + term
            total = total + moved(part, -(j - 1) * spacing)
        input_ref[target, 0] = total


def backward(branch, half, own, other, x, spread, taps, point, before):
    classes, residues, cols, channels = x.shape
    filters = point.shape[1]
    block = lambda r, h: (0, r, 0, 0)
    part = lambda r, h: (0, r, 0, 0, 0)
    whole = lambda r, h: (0, 0)
    part_spec = pl.BlockSpec((classes, 1, 2, cols // 4, filters), part)
    cell_spec = pl.BlockSpec((classes, 1, cols, channels), block)
    return pl.pallas_call(
        functools.partial(backward_kernel, branch),
        grid_spec=pltpu.PrefetchScalarGridSpec(
            num_scalar_prefetch=1,
            grid=(residues,),
            in_specs=[
                part_spec,
                part_spec,
                cell_spec,
                cell_spec,
                pl.BlockSpec(taps.shape, whole),
                pl.BlockSpec(point.shape, whole),
                cell_spec,
            ],
            out_specs=[
                cell_spec,
                pl.BlockSpec(point.shape, whole),
                pl.BlockSpec((9, 8, channels), lambda r, h: (0, 0, 0)),
            ],
        ),
        out_shape=[
            jax.ShapeDtypeStruct(x.shape, F32),
            jax.ShapeDtypeStruct(point.shape, F32),
            jax.ShapeDtypeStruct((9, 8, channels), F32),
        ],
        compiler_params=pltpu.CompilerParams(vmem_limit_bytes=48 * 2**20),
        cost_estimate=pl.CostEstimate(
            flops=4 * x.size * filters, bytes_accessed=12 * x.size, transcendentals=0
        ),
        name=f"backward_{branch}",
    )(half, own, other, x, spread, taps, point, before)


def plane_sum(value, scale, over_pair=False):
    half = value.shape[0] // 2
    core = lax.axis_index("dp") % 2
    keep = lax.dynamic_slice_in_dim(value, core * half, half)
    send = lax.dynamic_slice_in_dim(value, (1 - core) * half, half)
    mine = (keep + swap(send, "dp", 1)).astype(BF16)
    if over_pair:
        mine = (mine.astype(F32) + swap(mine, "chan", 1).astype(F32)).astype(BF16)
    x, y, diagonal = swap(mine, "dp", 2), swap(mine, "row", 1), swap_diagonal(mine)
    total = (mine.astype(F32) + x.astype(F32)) + (y.astype(F32) + diagonal.astype(F32))
    total = total * scale
    other = swap(total, "dp", 1)
    return jnp.where(
        core == 0, jnp.concatenate([total, other]), jnp.concatenate([other, total])
    )


def by_classes(features_in, depth_weights, point_weights, proj_weights, cotangent):
    _, band_rows, cols, channels = features_in.shape
    filters = point_weights.shape[2]
    classes, residues = 3, band_rows // 3
    weight_scale = 1.0 / math.sqrt(
        lax.axis_size("dp") * band_rows * lax.axis_size("row") * cols
    )
    row, chan = lax.axis_index("row"), lax.axis_index("chan")
    upper = row == 0
    half_index, side = chan % 2, chan // 2
    half = half_index.astype(jnp.int32).reshape(1)
    x = features_in[0]
    n = residues

    def to_classes(first, last, arrived):
        return jnp.where(
            upper, jnp.stack([first, last, arrived]), jnp.stack([arrived, first, last])
        )

    x_arrived = swap(x[n : 2 * n], "row", 1)
    cot = cotangent[0]
    cot_rows = jnp.concatenate([cot, swap(cot[n : 2 * n], "row", 1)])
    cot_far = swap(cot_rows, "chan", 2)
    cot_half = jnp.where(
        side == 0, jnp.stack([cot_rows, cot_far], 1), jnp.stack([cot_far, cot_rows], 1)
    )
    cot_band = cot_half[:band_rows]
    cot_class = to_classes(cot_half[:n], cot_half[2 * n : 3 * n], cot_half[band_rows:])

    taps = depth_weights.astype(F32).reshape(3, 9, channels)
    split = band_rows // 2
    low = x[:split].reshape(3, split // 3, cols, channels)
    high = x[split:].reshape(3, split // 3, cols, channels)

    def reduce(keep, send):
        near = (keep + swap(send, "chan", 1).astype(F32)).astype(BF16)
        far = swap(near, "chan", 2)
        return near.astype(F32) + far.astype(F32)

    def gate(preact, cots, branch):
        cells = cots.reshape(-1, filters)
        act_grad = lax.dot_general(
            cells, proj_weights[branch], (((1,), (1,)), ((), ())), preferred_element_type=F32
        ).reshape(preact.shape)
        logistic = jax.nn.sigmoid(preact)
        pre_grad = (act_grad * logistic * (1.0 + preact * (1.0 - logistic))).astype(BF16)
        return pre_grad, (preact * logistic).astype(BF16)

    def project(activation, branch):
        mine = jnp.where(side == 0, activation[..., 0, :, :], activation[..., 1, :, :])
        return jnp.einsum(
            "...f,fg->...g", mine, proj_weights[branch], preferred_element_type=F32
        )

    def proj_product(activation, cots):
        return lax.dot_general(
            activation.reshape(-1, filters), cots.reshape(-1, filters),
            (((0,), (0,)), ((), ())), preferred_element_type=F32,
        )

    keep0a, send0a = forward(0, half, low, taps[0], point_weights[0])
    pre0a = reduce(keep0a, send0a)
    x_class = to_classes(x[:n], x[2 * n : 3 * n], x_arrived)
    spreads, preacts = [], []
    for b in (1, 2, 3):
        spread, keep, send = forward(b, half, x_class, taps[b - 1], point_weights[b])
        spreads.append(spread)
        preacts.append(reduce(keep, send))
    keep0b, send0b = forward(0, half, high, taps[0], point_weights[0])
    pre0b = reduce(keep0b, send0b)

    cots0 = cot_band.reshape((2, 3, split // 3) + cot_band.shape[1:])
    grad0a, act0a = gate(pre0a, cots0[0], 0)
    other0a = swap(grad0a, "chan", 1)
    grads, acts, others = [], [], []
    for b in (1, 2, 3):
        grad, act = gate(preacts[b - 1], cot_class, b)
        grads.append(grad)
        acts.append(act)
        others.append(swap(grad, "chan", 1))
    grad0b, act0b = gate(pre0b, cots0[1], 0)
    other0b = swap(grad0b, "chan", 1)

    total = jnp.zeros(x_class.shape, F32)
    point_grads, depth_grads = [], []
    for b in (1, 2, 3):
        total, point_grad, depth_grad = backward(
            b, half, grads[b - 1], others[b - 1], x_class, spreads[b - 1], taps[b - 1],
            point_weights[b], total,
        )
        point_grads.append(point_grad)
        depth_grads.append(depth_grad.sum(axis=1))
    leaving = jnp.where(upper, total[2], total[0]).astype(BF16)
    first = jnp.where(upper, total[0], total[1])
    last = jnp.where(upper, total[1], total[2])
    arrived = swap(leaving, "row", 1)

    mixed = sum(project(acts[b - 1], b) for b in (1, 2, 3))
    mixed_leaving = jnp.where(upper, mixed[2], mixed[0]).astype(BF16)
    mixed_arrived = swap(mixed_leaving, "row", 1)
    mixed_band = jnp.concatenate([
        jnp.where(upper, mixed[0], mixed[1]),
        mixed_arrived.astype(F32),
        jnp.where(upper, mixed[1], mixed[2]),
    ])
    act0 = jnp.concatenate([
        act0a.reshape((split,) + act0a.shape[2:]), act0b.reshape((split,) + act0b.shape[2:])
    ])
    output = (mixed_band + project(act0, 0)).astype(BF16)

    proj_later = jnp.concatenate([proj_product(acts[b - 1], cot_class) for b in (1, 2, 3)])
    proj_later = plane_sum(proj_later, weight_scale, over_pair=True)
    proj_first = plane_sum(proj_product(act0, cot_band), weight_scale, over_pair=True)
    grad_proj = jnp.concatenate([proj_first, proj_later]).reshape(4, filters, filters)

    depth_rows = 27 * channels // filters
    padded = -(-depth_rows // 32) * 32
    depth = jnp.concatenate(depth_grads).reshape(depth_rows, filters)
    depth = jnp.pad(depth, ((0, padded - depth_rows), (0, 0)))
    early = plane_sum(jnp.concatenate(point_grads[:2]), weight_scale)
    late = plane_sum(jnp.concatenate([point_grads[2], depth]), weight_scale)

    def joined(own, other):
        own = own.reshape((split,) + own.shape[2:])
        other = other.reshape((split,) + other.shape[2:])
        both = jnp.where(
            half_index == 0, jnp.stack([own, other], 2), jnp.stack([other, own], 2)
        )
        return both.reshape(split, cols, filters)

    pre0 = jnp.concatenate([joined(grad0a, other0a), joined(grad0b, other0b)])
    grad0 = lax.dot_general(
        pre0, point_weights[0], (((2,), (1,)), ((), ())), preferred_element_type=F32
    ).astype(BF16)
    point0 = lax.dot_general(
        x.reshape(-1, channels), pre0.reshape(-1, filters), (((0,), (0,)), ((), ())),
        preferred_element_type=F32,
    )
    others_band = jnp.concatenate([first, arrived.astype(F32), last])
    grad_input = (grad0.astype(F32) + others_band).astype(BF16)[None]
    point0 = plane_sum(point0, weight_scale)
    grad_point = jnp.concatenate([point0, early, late[:channels]])
    grad_point = grad_point.reshape(4, channels, filters)
    grad_depth = late[channels : channels + depth_rows].reshape(3, 3, 3, channels)
    return (output[None], grad_input, grad_depth, grad_point, grad_proj)


def shifted(value, axis, steps):
    count = lax.axis_size(axis)
    first, last = (max(0, -steps), min(count, count - steps))
    return lax.ppermute(value, axis, [(source, source + steps) for source in range(first, last)])


def window(source, top, left, band_rows, band_cols):
    upper = lax.slice_in_dim(source, top, top + band_rows, axis=1)
    return lax.slice_in_dim(upper, left, left + band_cols, axis=2)


def on_device(features_in, depth_weights, point_weights, proj_weights, cotangent):
    samples, band_rows, band_cols, channels = features_in.shape
    weight_scale = 1.0 / math.sqrt(
        samples * lax.axis_size("dp") * band_rows * lax.axis_size("row") * band_cols
    )
    largest_reach = 3 * BASE_DILATION
    offsets = (2, 1, -1, -2)
    arrivals = []
    for offset in offsets:
        arrivals.append(shifted(features_in, "row", offset))
    tall_rows = jnp.concatenate(
        [arrivals[0], arrivals[1], features_in, arrivals[2], arrivals[3]], axis=1
    )
    padded = jnp.pad(tall_rows, ((0, 0), (0, 0), (largest_reach, largest_reach), (0, 0)))
    branch_maps = [features_in]
    for branch_level in range(3):
        tap_spacing = (branch_level + 1) * BASE_DILATION
        summed = jnp.zeros(features_in.shape, jnp.float32)
        for row_tap in range(3):
            for col_tap in range(3):
                input_kernel_tap = window(
                    padded,
                    largest_reach + (row_tap - 1) * tap_spacing,
                    largest_reach + (col_tap - 1) * tap_spacing,
                    band_rows,
                    band_cols,
                )
                summed = summed + input_kernel_tap.astype(jnp.float32) * depth_weights[
                    branch_level, row_tap, col_tap
                ].astype(jnp.float32)
        branch_maps.append(summed.astype(jnp.bfloat16))
    spread = jnp.stack(branch_maps)
    full_point = lax.all_gather(point_weights, "chan", axis=1, tiled=True)
    preact = jnp.einsum(
        "bsrwc,bcf->bsrwf",
        lax.all_to_all(spread, "chan", split_axis=3, concat_axis=4, tiled=True),
        full_point,
        preferred_element_type=jnp.float32,
    )
    activation = jax.nn.silu(preact).astype(jnp.bfloat16)
    output = jnp.einsum(
        "bsrwf,bfg->srwg", activation, proj_weights, preferred_element_type=jnp.float32
    ).astype(jnp.bfloat16)
    silu_gradient = jnp.einsum(
        "srwg,bfg->bsrwf", cotangent, proj_weights, preferred_element_type=jnp.float32
    )
    logistic = jax.nn.sigmoid(preact)
    pre_grad = (silu_gradient * logistic * (1.0 + preact * (1.0 - logistic))).astype(jnp.bfloat16)
    proj_term = jnp.einsum(
        "bsrwf,srwg->bfg", activation, cotangent, preferred_element_type=jnp.float32
    )
    grad_proj = lax.psum(proj_term, ("row", "chan", "dp")) * weight_scale
    incoming = lax.all_gather(pre_grad, "chan", axis=3, tiled=True)
    local_grad = jnp.einsum(
        "bsrwf,bcf->bsrwc", incoming, point_weights, preferred_element_type=jnp.float32
    ).astype(jnp.bfloat16)
    spread_grad = local_grad
    point_sum = jnp.einsum("bsrwc,bsrwf->bcf", spread, incoming, preferred_element_type=jnp.float32)
    spread_grad, point_term = (spread_grad, point_sum)
    depth_rows = []
    for branch_level in range(3):
        tap_spacing = (branch_level + 1) * BASE_DILATION
        branch_grad = spread_grad[branch_level + 1].astype(jnp.float32)
        gathered = []
        for row_tap in range(3):
            for col_tap in range(3):
                input_kernel_tap = window(
                    padded,
                    largest_reach + (row_tap - 1) * tap_spacing,
                    largest_reach + (col_tap - 1) * tap_spacing,
                    band_rows,
                    band_cols,
                )
                gathered.append(
                    jnp.sum(input_kernel_tap.astype(jnp.float32) * branch_grad, axis=(0, 1, 2))
                )
        depth_rows.append(jnp.stack(gathered).reshape(3, 3, channels))
    depth_term = jnp.stack(depth_rows)
    point_summed, depth_summed = lax.psum((point_term, depth_term), ("row", "dp"))
    grad_point = point_summed * weight_scale
    grad_depth = depth_summed * weight_scale
    neighbour_sets = []
    for branch_level in range(3):
        neighbour_sets.append(
            [shifted(spread_grad[branch_level + 1], "row", offset) for offset in offsets]
        )
    grad_in = spread_grad[0].astype(jnp.float32)
    for branch_level in range(3):
        tap_spacing = (branch_level + 1) * BASE_DILATION
        received = neighbour_sets[branch_level]
        grad_tall = jnp.concatenate(
            [received[0], received[1], spread_grad[branch_level + 1], received[2], received[3]],
            axis=1,
        )
        grad_padded = jnp.pad(grad_tall, ((0, 0), (0, 0), (largest_reach, largest_reach), (0, 0)))
        for row_tap in range(3):
            for col_tap in range(3):
                grad_tap = window(
                    grad_padded,
                    largest_reach - (row_tap - 1) * tap_spacing,
                    largest_reach - (col_tap - 1) * tap_spacing,
                    band_rows,
                    band_cols,
                )
                grad_in = grad_in + grad_tap.astype(jnp.float32) * depth_weights[
                    branch_level, row_tap, col_tap
                ].astype(jnp.float32)
    return (output, grad_in.astype(jnp.bfloat16), grad_depth, grad_point, grad_proj)


def folds(mesh, features_in):
    sizes = mesh.shape
    samples, rows, cols, channels = features_in.shape
    return (
        rows == 3 * BASE_DILATION
        and sizes["row"] == 2
        and sizes["chan"] == 4
        and sizes["dp"] == 4
        and samples == sizes["dp"]
        and cols % 64 == 0
        and channels % (128 * sizes["chan"]) == 0
    )


def solution(mesh):
    in_specs = (
        P("dp", "row", None, "chan"),
        P(None, None, None, "chan"),
        P(None, "chan", None),
        P(),
        P("dp", "row", "chan", None),
    )
    out_specs = (
        P("dp", "row", "chan", None),
        P("dp", "row", None, "chan"),
        P(None, None, None, "chan"),
        P(None, "chan", None),
        P(),
    )

    def run(*args):
        body = by_classes if folds(mesh, args[0]) else on_device
        return jax.shard_map(
            body, mesh=mesh, in_specs=in_specs, out_specs=out_specs, check_vma=False
        )(*args)

    return run
```

```python
import functools
import math

import jax
import jax.numpy as jnp
from jax import lax
from jax.experimental import pallas as pl
from jax.experimental.pallas import tpu as pltpu
from jax.sharding import PartitionSpec as P

BASE_DILATION = 12
F32 = jnp.float32
BF16 = jnp.bfloat16
VMEM_BYTES = 16 * 2**20


def swap(value, axis, flip):
    count = lax.axis_size(axis)
    return lax.ppermute(value, axis, [(i, i ^ flip) for i in range(count)])


def moved(value, steps):
    if steps == 0:
        return value
    count = value.shape[0]
    rolled = pltpu.roll(value, (-steps) % count, 0)
    place = lax.broadcasted_iota(jnp.int32, value.shape, 0)
    inside = place < count - steps if steps > 0 else place >= -steps
    return jnp.where(inside, rolled, 0.0)


def row_pairs(branch, classes):
    return [
        (q, i, q + (i - 1) * branch)
        for q in range(classes)
        for i in range(3)
        if 0 <= q + (i - 1) * branch < classes
    ]


def class_rows(upper, first, last, arrived):
    return (
        jnp.where(upper, first, arrived),
        jnp.where(upper, last, first),
        jnp.where(upper, arrived, last),
    )


def shape_of(shape, dtype):
    return jax.ShapeDtypeStruct(shape, dtype)


def in_hbm(value):
    return pltpu.with_memory_space_constraint(value, pltpu.HBM)


def result_of(shape, dtype):
    return jax.ShapeDtypeStruct(shape, dtype)


TOKEN = (8, 128)
STEPS = 2


def call(body, place, grid, after, ins, outs, name, scratch=()):
    def spec(block, split):
        dims = len(block)
        if isinstance(split, tuple):
            return pl.BlockSpec(block, lambda r, p: tuple(r if k is None else k for k in split))
        return pl.BlockSpec(block, lambda r, p: tuple(r if k == split else 0 for k in range(dims)))

    def kernel(place_ref, after_ref, *refs):
        last = len(ins) + len(outs) - 2
        body(place_ref, *refs[:last], *refs[last + 1 :])
        refs[last][...] = after_ref[...]

    ins = [(after, TOKEN, None)] + list(ins)
    outs = list(outs) + [(shape_of(TOKEN, F32), TOKEN, None)]
    return pl.pallas_call(
        kernel,
        grid_spec=pltpu.PrefetchScalarGridSpec(
            num_scalar_prefetch=1,
            grid=(grid,),
            in_specs=[spec(block, split) for _, block, split in ins],
            out_specs=[spec(block, split) for _, block, split in outs],
            scratch_shapes=list(scratch),
        ),
        out_shape=[s for s, _, _ in outs],
        compiler_params=pltpu.CompilerParams(vmem_limit_bytes=VMEM_BYTES),
        cost_estimate=pl.CostEstimate(flops=1, bytes_accessed=1, transcendentals=0),
        name=name,
    )(place, *[a for a, _, _ in ins])


def forward_kernel(branches, folded, place, x_ref, arrived_ref, taps_ref, *refs):
    classes, group, cols, channels = x_ref.shape
    count = len(branches)
    points, refs = refs[:count], refs[count:]
    keeps, sends, refs = refs[:count], refs[count : 2 * count], refs[2 * count :]
    spreads = dict(zip([b for b in branches if b], refs))
    if not folded:
        refs[-1][...] = x_ref[1]

    def residue(r, carry):
        rows = [x_ref[q, r].astype(F32) for q in range(classes)]
        if folded:
            rows = class_rows(place[1] == 0, rows[0], rows[2], arrived_ref[r].astype(F32))
        for branch, spread_ref in spreads.items():
            for q in range(classes):
                total = None
                for j in range(3):
                    part = None
                    for out, i, source in row_pairs(branch, classes):
                        if out == q:
                            tap = taps_ref[branch - 1, i, j].astype(F32)
                            term = rows[source] * tap[None, :]
                            part = term if part is None else part + term
                    part = moved(part, (j - 1) * branch * BASE_DILATION)
                    total = part if total is None else total + part
                spread_ref[q, r] = total.astype(BF16)
        return carry

    lax.fori_loop(0, group, residue, 0)
    for k, branch in enumerate(branches):
        cells = spreads[branch][...] if branch else x_ref[...]
        cells = cells.reshape(classes * group * cols, channels)
        partial = jnp.dot(cells, points[k][0], preferred_element_type=F32)
        split = partial.reshape(classes * group * 2, 2, cols // 4, partial.shape[-1])
        first = place[0] % 2 == 0
        keep = jnp.where(first, split[:, 0], split[:, 1])
        send = jnp.where(first, split[:, 1], split[:, 0])
        keeps[k][0] = keep.reshape(keeps[k].shape[1:])
        sends[k][0] = send.reshape(sends[k].shape[1:]).astype(BF16)


def forward(branches, folded, place, after, x, arrived, taps, point):
    classes, residues, cols, channels = x.shape
    filters = point.shape[2]
    group = residues // STEPS
    cell = (classes, group, cols, channels)
    part = (1, classes, group, 2, cols // 4, filters)
    part_shape = (1, classes, residues, 2, cols // 4, filters)
    outs = [(shape_of(part_shape, F32), part, 2) for _ in branches]
    outs += [(shape_of(part_shape, BF16), part, 2) for _ in branches]
    outs += [(pltpu.HBM(x.shape, BF16), cell, 1) for b in branches if b]
    if not folded:
        outs += [(shape_of(x.shape[1:], BF16), (group, cols, channels), 0)]
    return call(
        functools.partial(forward_kernel, branches, folded), place, STEPS, after,
        [
            (x, cell, 1),
            (arrived, (group, cols, channels) if folded else (1, 1, 8, 128), 0 if folded else None),
            (taps, taps.shape, None),
        ]
        + [(point, (1, channels, filters), (b, 0, 0)) for b in branches],
        outs, "forward_" + "_".join(map(str, branches)),
    )


def near_kernel(place, keep_ref, arrived_ref, *near_refs):
    for k, near_ref in enumerate(near_refs):
        near_ref[0] = (keep_ref[k] + arrived_ref[k].astype(F32)).astype(BF16)


def near_sum(name, place, after, keep, arrived):
    block = keep.shape[:2] + (keep.shape[2] // STEPS,) + keep.shape[3:]
    out = (1,) + block[1:]
    return call(
        near_kernel, place, STEPS, after, [(keep, block, 2), (arrived, block, 2)],
        [(shape_of((1,) + keep.shape[1:], BF16), out, 2)] * keep.shape[0], f"near_{name}",
    )


def first_near_kernel(place, keep_ref, arrived_ref, cot_ref, far_ref, near_ref, cots_ref, leaving_ref):
    near_ref[...] = (keep_ref[...] + arrived_ref[...].astype(F32)).astype(BF16)
    low_side = place[0] // 2 == 0
    cots_ref[:, 0] = jnp.where(low_side, cot_ref[...], far_ref[...])
    cots_ref[:, 1] = jnp.where(low_side, far_ref[...], cot_ref[...])
    n = leaving_ref.shape[0]
    leaving_ref[...] = cots_ref[n : 2 * n]


def first_near_sum(place, after, keep, arrived, cot, far):
    rows, width, filters = cot.shape
    cots = (rows, 2, width, filters)
    leaving = (rows // 3, 2, width, filters)
    return call(
        first_near_kernel, place, 1, after,
        [(a, a.shape, None) for a in (keep, arrived, cot, far)],
        [(shape_of(s, BF16), s, None) for s in (keep.shape, cots, leaving)], "near_first",
    )


def gate_kernel(branches, folded, place, *refs):
    count = len(branches)
    nears, fars, cot_ref, refs = refs[:count], refs[count : 2 * count], refs[2 * count], refs[2 * count + 1 :]
    _, classes, residues, sides, width, filters = nears[0].shape
    if folded:
        arrived_ref, refs = refs[0], refs[1:]
    projs, (mixed_ref, grad_ref, out_ref, proj_grad_ref, *leaving) = refs[:count], refs[count:]
    n = residues
    cots = cot_ref[...]
    if folded:
        cots = jnp.concatenate(
            class_rows(place[1] == 0, cots[:n], cots[2 * n : 3 * n], arrived_ref[...])
        )
    cells = cots.reshape(-1, filters)
    shape = (classes * residues, sides, width, filters)
    mixed = mixed_ref[...]
    for k in range(count):
        proj = projs[k][0]
        act_grad = lax.dot_general(cells, proj, (((1,), (1,)), ((), ())), preferred_element_type=F32)
        preact = (nears[k][0].astype(F32) + fars[k][0].astype(F32)).reshape(shape)
        logistic = 1.0 / (1.0 + jnp.exp(-preact))
        grad = act_grad.reshape(shape) * logistic * (1.0 + preact * (1.0 - logistic))
        grad_ref[k] = grad.astype(BF16).reshape(grad_ref.shape[1:])
        active = (preact * logistic).astype(BF16)
        mine = jnp.where(place[0] // 2 == 0, active[:, 0], active[:, 1]).reshape(-1, filters)
        mixed = mixed + jnp.dot(mine, proj, preferred_element_type=F32).reshape(mixed.shape)
        proj_grad_ref[k] = lax.dot_general(
            active.reshape(-1, filters), cells, (((0,), (0,)), ((), ())), preferred_element_type=F32
        )
    out_ref[...] = mixed
    if leaving:
        upper = place[1] == 0
        leaving[0][...] = jnp.where(upper, mixed[2 * n :], mixed[:n]).astype(BF16)


def gate(branches, folded, place, after, nears, fars, cots, arrived, proj, mixed, leaves=False):
    filters = proj.shape[-1]
    count = len(branches)
    arrays = [*nears, *fars, cots] + ([arrived] if folded else [])
    shapes = [
        ((count,) + nears[0].shape[1:], BF16), (mixed.shape, F32), ((count, filters, filters), F32)
    ]
    if leaves:
        shapes.append(((mixed.shape[0] // 3,) + mixed.shape[1:], BF16))
    return call(
        functools.partial(gate_kernel, branches, folded), place, 1, after,
        [(a, a.shape, None) for a in arrays]
        + [(proj, (1, filters, filters), (b, 0, 0)) for b in branches]
        + [(mixed, mixed.shape, None)],
        [(shape_of(shape, kind), shape, None) for shape, kind in shapes],
        "gate_" + "_".join(map(str, branches)),
    )


def whole_columns(place, own, other):
    thin = (-1,) + own.shape[-2:]
    own, other = own.reshape(thin), other.reshape(thin)
    first = place[0] % 2 == 0
    low = jnp.where(first, own, other)
    high = jnp.where(first, other, own)
    both = jnp.concatenate([low[:, None], high[:, None]], axis=1)
    return both.reshape(-1, own.shape[-1])


def backward_kernel(
    branch, folded, chained, place, own_ref, other_ref, x_ref, arrived_ref, spread_ref, taps_ref, point_ref,
    before_ref, *refs
):
    classes, group, cols, channels = x_ref.shape
    point_grad_ref, depth_ref, grads_ref = refs[-3:]
    upper = place[1] == 0
    pre = whole_columns(place, own_ref[0], other_ref[0])
    grads = lax.dot_general(pre, point_ref[0], (((1,), (1,)), ((), ())), preferred_element_type=F32)
    grads_ref[...] = grads.astype(BF16).reshape(grads_ref.shape)
    cells = spread_ref[...].reshape(classes * group * cols, channels)
    product = lax.dot_general(cells, pre, (((0,), (0,)), ((), ())), preferred_element_type=F32)

    @pl.when(pl.program_id(0) == 0)
    def _():
        point_grad_ref[...] = product
        depth_ref[...] = jnp.zeros_like(depth_ref)

    @pl.when(pl.program_id(0) > 0)
    def _():
        point_grad_ref[...] += product

    pairs = row_pairs(branch, classes)

    def residue(r, carry):
        rows = [x_ref[q, r].astype(F32) for q in range(classes)]
        if folded:
            rows = class_rows(upper, rows[0], rows[2], arrived_ref[r].astype(F32))
        grads = [grads_ref[q, r].astype(F32) for q in range(classes)]
        for j in range(3):
            near = [moved(row, (j - 1) * branch * BASE_DILATION) for row in rows]
            for i in range(3):
                part = None
                for q, tap, source in pairs:
                    if tap == i:
                        term = (near[source] * grads[q]).reshape(cols // 8, 8, channels).sum(axis=0)
                        part = term if part is None else part + term
                if part is not None:
                    depth_ref[i * 3 + j] += part
        totals = []
        for target in range(classes):
            total = before_ref[target, r] if chained else None
            for j in range(3):
                part = None
                for q, i, source in pairs:
                    if source == target:
                        term = grads[q] * taps_ref[branch - 1, i, j].astype(F32)[None, :]
                        part = term if part is None else part + term
                part = moved(part, -(j - 1) * branch * BASE_DILATION)
                total = part if total is None else total + part
            totals.append(total)
        if chained:
            leaving_ref, stay_ref = refs[:2]
            leaving_ref[r] = jnp.where(upper, totals[2], totals[0]).astype(BF16)
            stay_ref[0, r] = jnp.where(upper, totals[0], totals[1])
            stay_ref[1, r] = jnp.where(upper, totals[1], totals[2])
        else:
            for q in range(classes):
                refs[0][q, r] = totals[q]
        return carry

    lax.fori_loop(0, group, residue, 0)


def backward(branch, folded, place, after, own, other, index, x, arrived, spread, taps, point, before=None):
    classes, residues, cols, channels = x.shape
    filters = point.shape[2]
    group = residues // STEPS
    part = (1, classes, group, 2, cols // 4, filters)
    cell = (classes, group, cols, channels)
    thin = (group, cols, channels)
    chained = before is not None
    if chained:
        outs = [
            (shape_of(x.shape[1:], BF16), thin, 0),
            (pltpu.HBM((2,) + x.shape[1:], F32), (2,) + thin, 1),
        ]
    else:
        outs = [(pltpu.HBM(x.shape, F32), cell, 1)]
    outs += [
        (shape_of((channels, filters), F32), (channels, filters), None),
        (shape_of((9, 8, channels), F32), (9, 8, channels), None),
    ]
    small = (1, 1, 8, 128)
    return call(
        functools.partial(backward_kernel, branch, folded, chained), place, STEPS, after,
        [
            (own, part, (index, 0, None, 0, 0, 0)),
            (other, part, (index, 0, None, 0, 0, 0)),
            (x, cell, 1),
            (arrived, thin, 0) if folded else (x, small, None),
            (spread, cell, 1),
            (taps, taps.shape, None),
            (point, (1, channels, filters), (branch, 0, 0)),
            (before, cell, 1) if chained else (x, small, None),
        ],
        outs, f"backward_{branch}", scratch=[pltpu.VMEM(cell, BF16)],
    )


def join_kernel(place, own_ref, other_ref, x_ref, pre_ref, point_grad_ref):
    pre = whole_columns(place, own_ref[0], other_ref[0])
    pre_ref[...] = pre.reshape(pre_ref.shape)
    cells = x_ref[...].reshape(-1, x_ref.shape[-1])
    product = lax.dot_general(cells, pre, (((0,), (0,)), ((), ())), preferred_element_type=F32)

    @pl.when(pl.program_id(0) == 0)
    def _():
        point_grad_ref[...] = product

    @pl.when(pl.program_id(0) > 0)
    def _():
        point_grad_ref[...] += product


def join(place, after, own, other, index, x):
    classes, residues, cols, channels = x.shape
    filters = own.shape[-1]
    group = residues // STEPS
    part = (1, classes, group, 2, cols // 4, filters)
    return call(
        join_kernel, place, STEPS, after,
        [
            (own, part, (index, 0, None, 0, 0, 0)),
            (other, part, (index, 0, None, 0, 0, 0)),
            (x, (classes, group, cols, channels), 1),
        ],
        [
            (shape_of((classes, residues, cols, filters), BF16), (classes, group, cols, filters), 1),
            (shape_of((channels, filters), F32), (channels, filters), None),
        ],
        "join",
    )


def last_kernel(
    place, pre_ref, point_ref, band_ref, stay_ref, arrived_ref, mixed_ref, folded_ref, mixed_arrived_ref,
    input_ref, output_ref
):
    classes, group, cols, channels = band_ref.shape
    pre = pre_ref[...].reshape(classes * group * cols, -1)
    grads = lax.dot_general(pre, point_ref[0], (((1,), (1,)), ((), ())), preferred_element_type=F32)
    grads = grads.astype(BF16).astype(F32).reshape(band_ref.shape)
    others = (stay_ref[0], arrived_ref[...].astype(F32), stay_ref[1])
    for q in range(classes):
        input_ref[q] = (grads[q] + band_ref[q] + others[q]).astype(BF16)
    upper = place[1] == 0
    mixed = (
        jnp.where(upper, folded_ref[0], folded_ref[1]),
        mixed_arrived_ref[...].astype(F32),
        jnp.where(upper, folded_ref[1], folded_ref[2]),
    )
    for q in range(classes):
        output_ref[q] = (mixed_ref[q] + mixed[q]).astype(BF16)


def last(place, after, pre, point, band, stay, arrived, mixed, folded, mixed_arrived):
    classes, residues, cols, channels = band.shape
    filters = point.shape[2]
    group = residues // STEPS
    cell = (classes, group, cols, channels)
    thin = (classes, group) + mixed.shape[2:]
    return call(
        last_kernel, place, STEPS, after,
        [
            (pre, (classes, group, cols, filters), 1),
            (point, (1, channels, filters), (0, 0, 0)),
            (band, cell, 1),
            (stay, (2, group, cols, channels), 1),
            (arrived, (group, cols, channels), 0),
            (mixed, thin, 1),
            (folded, thin, 1),
            (mixed_arrived, thin[1:], 0),
        ],
        [(result_of(band.shape, BF16), cell, 1), (result_of(mixed.shape, BF16), thin, 1)], "last",
    )


def add_kernel(scale, place, *refs):
    *pairs, out_ref = refs
    at = 0
    for own_ref, other_ref in zip(pairs[::2], pairs[1::2]):
        rows = other_ref.shape[0]
        if len(own_ref.shape) == 3:
            own = jnp.where(place[2] == 0, own_ref[0], own_ref[1])
        else:
            own = own_ref[...]
        total = own.astype(F32) + other_ref[...].astype(F32)
        if scale != 1.0:
            total = total * scale
        out_ref[at : at + rows] = total.astype(out_ref.dtype)
        at += rows


def add(name, place, after, pairs, kind, scale=1.0):
    rows = sum(other.shape[0] for _, other in pairs)
    shape = (rows, pairs[0][1].shape[1])
    return call(
        functools.partial(add_kernel, scale), place, 1, after,
        [(a, a.shape, None) for pair in pairs for a in pair],
        [(shape_of(shape, kind), shape, None)], name,
    )


def finish_kernel(place, own30, far30, own1, far1, own2, far2, proj_ref, depth_ref, point_ref):
    core = place[2] == 0

    def halves(own, far, first, count):
        own, far = own[first : first + count], far[first : first + count]
        return jnp.where(core, own, far), jnp.where(core, far, own)

    channels = point_ref.shape[1]
    filters = proj_ref.shape[1]
    point_ref[3], point_ref[0] = halves(own30, far30, 0, channels)
    proj_ref[3], proj_ref[0] = halves(own30, far30, channels, filters)
    point_ref[1, : channels // 2], point_ref[1, channels // 2 :] = halves(own1, far1, 0, channels // 2)
    rows = own2.shape[0] - filters
    low, high = halves(own2, far2, 0, rows)
    point_ref[2, :rows] = low
    point_ref[2, rows:] = high[: channels - rows]
    depth_ref[...] = high[channels - rows :]
    proj_ref[1], proj_ref[2] = halves(own2, far2, rows, filters)


def finish(place, after, early, middle, late, channels, filters):
    arrays = [*early, *middle, *late]
    rows = 2 * (late[0].shape[0] - filters) - channels
    shapes = [(4, filters, filters), (rows, filters), (4, channels, filters)]
    return call(
        finish_kernel, place, 1, after, [(a, a.shape, None) for a in arrays],
        [(result_of(s, F32), s, None) for s in shapes], "finish",
    )


def cores(value):
    if len(value.shape) == 2:
        value = value.reshape((2, -1) + value.shape[1:])
    far = lax.dynamic_index_in_dim(value, 1 - lax.axis_index("dp") % 2, 0, keepdims=False)
    return value, swap(far, "dp", 1)


def by_classes(features_in, depth_weights, point_weights, proj_weights, cotangent):
    _, band_rows, cols, channels = features_in.shape
    filters = point_weights.shape[2]
    classes, n = 3, band_rows // 3
    scale = 1.0 / math.sqrt(lax.axis_size("dp") * band_rows * lax.axis_size("row") * cols)
    chan, row = lax.axis_index("chan"), lax.axis_index("row")
    core = lax.axis_index("dp") % 2
    place = jnp.stack([chan, row, core]).astype(jnp.int32)
    x = features_in[0].reshape(classes, n, cols, channels)

    weights = (depth_weights, point_weights)
    cot = cotangent[0]
    cot_far = swap(cot, "chan", 2)

    token = jnp.zeros(TOKEN, F32)
    keep3, keep0, send3, send0, spread3, x_leaving, token = forward(
        (3, 0), False, place, token, in_hbm(x), x, depth_weights, in_hbm(point_weights)
    )
    sent3, sent0 = swap(send3, "chan", 1), swap(send0, "chan", 1)
    arrived = swap(x_leaving, "row", 1)
    near3, cots, cots_leaving, token = first_near_sum(place, token, keep3, sent3, cot, cot_far)
    far3 = swap(near3, "chan", 2)
    near0, token = near_sum("0", place, token, keep0, sent0)
    far0 = swap(near0, "chan", 2)
    cots_arrived = swap(cots_leaving, "row", 1)
    keep1, keep2, send1, send2, spread1, spread2, token = forward(
        (1, 2), True, place, token, x, arrived, *weights
    )
    sent1, sent2 = swap(send1, "chan", 1), swap(send2, "chan", 1)
    near1, token = near_sum("1", place, token, keep1, sent1)
    far1 = swap(near1, "chan", 2)
    mixed = jnp.zeros(cot.shape, F32)
    grad30, band_mixed, proj30, token = gate(
        (3, 0), False, place, token, [near3, near0], [far3, far0], cots, None, proj_weights, mixed
    )
    other30 = swap(grad30, "chan", 1)
    proj30_own, proj30_near = cores(proj30)
    near2, token = near_sum("2", place, token, keep2, sent2)
    far2 = swap(near2, "chan", 2)
    grad1, class_mixed, proj1, token = gate(
        (1,), True, place, token, [near1], [far1], cots, cots_arrived, proj_weights, mixed
    )
    other1 = swap(grad1, "chan", 1)
    proj30_sum, token = add("proj_3_0", place, token, [(proj30_own, proj30_near)], BF16)
    proj30_pair = swap(proj30_sum, "chan", 1)
    band, point3, depth3, token = backward(
        3, False, place, token, grad30, other30, 0, x, x, spread3, *weights
    )
    grad2, class_mixed, proj2, mixed_leaving, token = gate(
        (2,), True, place, token, [near2], [far2], cots, cots_arrived, proj_weights, class_mixed, True
    )
    other2 = swap(grad2, "chan", 1)
    mixed_arrived = swap(mixed_leaving, "row", 1)
    proj12_own, proj12_near = cores(jnp.concatenate([proj1, proj2]))
    pre0, point0, token = join(place, token, grad30, other30, 1, x)
    point30_own, point30_near = cores(jnp.stack([point3, point0]))
    total1, point1, depth1, token = backward(
        1, True, place, token, grad1, other1, 0, x, arrived, spread1, *weights
    )
    point1_own, point1_near = cores(point1)
    early, token = add(
        "early_y", place, token, [(point30_own, point30_near), (proj30_sum, proj30_pair)], BF16
    )
    early_y = swap(early, "row", 1)
    proj12_sum, token = add("proj_1_2", place, token, [(proj12_own, proj12_near)], BF16)
    proj12_pair = swap(proj12_sum, "chan", 1)
    middle, token = add("middle_y", place, token, [(point1_own, point1_near)], BF16)
    middle_y = swap(middle, "row", 1)
    leaving, stay, point2, depth2, token = backward(
        2, True, place, token, grad2, other2, 0, x, arrived, spread2, *weights, before=total1
    )
    input_arrived = swap(leaving, "row", 1)
    early, token = add("early_x", place, token, [(early, early_y)], BF16)
    early_x = swap(early, "dp", 2)
    depth_rows = 27 * channels // filters
    padded = -(-depth_rows // 32) * 32
    depth = jnp.concatenate([depth1, depth2, depth3]).sum(axis=1).reshape(depth_rows, filters)
    depth = jnp.pad(depth, ((0, padded - depth_rows), (0, 0)))
    late_own, late_near = cores(jnp.concatenate([point2, depth]))
    late, token = add(
        "late_x", place, token, [(late_own, late_near), (proj12_sum, proj12_pair)], BF16
    )
    late_x = swap(late, "dp", 2)
    middle, token = add("middle_x", place, token, [(middle, middle_y)], BF16)
    middle_x = swap(middle, "dp", 2)
    bands = band_mixed.reshape((classes, n) + band_mixed.shape[1:])
    folds = class_mixed.reshape(bands.shape)
    grad_input, output, token = last(
        place, token, pre0, point_weights, in_hbm(band), in_hbm(stay), input_arrived, bands, folds,
        mixed_arrived,
    )
    late, token = add("late_y", place, token, [(late, late_x)], BF16)
    late_y = swap(late, "row", 1)
    early, token = add("early", place, token, [(early, early_x)], F32, scale)
    early_far = swap(early, "dp", 1)
    middle, token = add("middle", place, token, [(middle, middle_x)], F32, scale)
    middle_far = swap(middle, "dp", 1)
    late, token = add("late", place, token, [(late, late_y)], F32, scale)
    late_far = swap(late, "dp", 1)
    grad_proj, depth, grad_point, token = finish(
        place, token, (early, early_far), (middle, middle_far), (late, late_far), channels, filters
    )
    grad_depth = depth[:depth_rows].reshape(3, 3, 3, channels)
    return (
        output.reshape(cotangent.shape), grad_input.reshape(features_in.shape), grad_depth, grad_point,
        grad_proj,
    )


def shifted(value, axis, steps):
    count = lax.axis_size(axis)
    first, last = (max(0, -steps), min(count, count - steps))
    return lax.ppermute(value, axis, [(source, source + steps) for source in range(first, last)])


def window(source, top, left, band_rows, band_cols):
    upper = lax.slice_in_dim(source, top, top + band_rows, axis=1)
    return lax.slice_in_dim(upper, left, left + band_cols, axis=2)


def on_device(features_in, depth_weights, point_weights, proj_weights, cotangent):
    samples, band_rows, band_cols, channels = features_in.shape
    weight_scale = 1.0 / math.sqrt(
        samples * lax.axis_size("dp") * band_rows * lax.axis_size("row") * band_cols
    )
    largest_reach = 3 * BASE_DILATION
    offsets = (2, 1, -1, -2)
    arrivals = []
    for offset in offsets:
        arrivals.append(shifted(features_in, "row", offset))
    tall_rows = jnp.concatenate(
        [arrivals[0], arrivals[1], features_in, arrivals[2], arrivals[3]], axis=1
    )
    padded = jnp.pad(tall_rows, ((0, 0), (0, 0), (largest_reach, largest_reach), (0, 0)))
    branch_maps = [features_in]
    for branch_level in range(3):
        tap_spacing = (branch_level + 1) * BASE_DILATION
        summed = jnp.zeros(features_in.shape, jnp.float32)
        for row_tap in range(3):
            for col_tap in range(3):
                input_kernel_tap = window(
                    padded,
                    largest_reach + (row_tap - 1) * tap_spacing,
                    largest_reach + (col_tap - 1) * tap_spacing,
                    band_rows,
                    band_cols,
                )
                summed = summed + input_kernel_tap.astype(jnp.float32) * depth_weights[
                    branch_level, row_tap, col_tap
                ].astype(jnp.float32)
        branch_maps.append(summed.astype(jnp.bfloat16))
    spread = jnp.stack(branch_maps)
    full_point = lax.all_gather(point_weights, "chan", axis=1, tiled=True)
    preact = jnp.einsum(
        "bsrwc,bcf->bsrwf",
        lax.all_to_all(spread, "chan", split_axis=3, concat_axis=4, tiled=True),
        full_point,
        preferred_element_type=jnp.float32,
    )
    activation = jax.nn.silu(preact).astype(jnp.bfloat16)
    output = jnp.einsum(
        "bsrwf,bfg->srwg", activation, proj_weights, preferred_element_type=jnp.float32
    ).astype(jnp.bfloat16)
    silu_gradient = jnp.einsum(
        "srwg,bfg->bsrwf", cotangent, proj_weights, preferred_element_type=jnp.float32
    )
    logistic = jax.nn.sigmoid(preact)
    pre_grad = (silu_gradient * logistic * (1.0 + preact * (1.0 - logistic))).astype(jnp.bfloat16)
    proj_term = jnp.einsum(
        "bsrwf,srwg->bfg", activation, cotangent, preferred_element_type=jnp.float32
    )
    grad_proj = lax.psum(proj_term, ("row", "chan", "dp")) * weight_scale
    incoming = lax.all_gather(pre_grad, "chan", axis=3, tiled=True)
    local_grad = jnp.einsum(
        "bsrwf,bcf->bsrwc", incoming, point_weights, preferred_element_type=jnp.float32
    ).astype(jnp.bfloat16)
    spread_grad = local_grad
    point_sum = jnp.einsum("bsrwc,bsrwf->bcf", spread, incoming, preferred_element_type=jnp.float32)
    spread_grad, point_term = (spread_grad, point_sum)
    depth_rows = []
    for branch_level in range(3):
        tap_spacing = (branch_level + 1) * BASE_DILATION
        branch_grad = spread_grad[branch_level + 1].astype(jnp.float32)
        gathered = []
        for row_tap in range(3):
            for col_tap in range(3):
                input_kernel_tap = window(
                    padded,
                    largest_reach + (row_tap - 1) * tap_spacing,
                    largest_reach + (col_tap - 1) * tap_spacing,
                    band_rows,
                    band_cols,
                )
                gathered.append(
                    jnp.sum(input_kernel_tap.astype(jnp.float32) * branch_grad, axis=(0, 1, 2))
                )
        depth_rows.append(jnp.stack(gathered).reshape(3, 3, channels))
    depth_term = jnp.stack(depth_rows)
    point_summed, depth_summed = lax.psum((point_term, depth_term), ("row", "dp"))
    grad_point = point_summed * weight_scale
    grad_depth = depth_summed * weight_scale
    neighbour_sets = []
    for branch_level in range(3):
        neighbour_sets.append(
            [shifted(spread_grad[branch_level + 1], "row", offset) for offset in offsets]
        )
    grad_in = spread_grad[0].astype(jnp.float32)
    for branch_level in range(3):
        tap_spacing = (branch_level + 1) * BASE_DILATION
        received = neighbour_sets[branch_level]
        grad_tall = jnp.concatenate(
            [received[0], received[1], spread_grad[branch_level + 1], received[2], received[3]],
            axis=1,
        )
        grad_padded = jnp.pad(grad_tall, ((0, 0), (0, 0), (largest_reach, largest_reach), (0, 0)))
        for row_tap in range(3):
            for col_tap in range(3):
                grad_tap = window(
                    grad_padded,
                    largest_reach - (row_tap - 1) * tap_spacing,
                    largest_reach - (col_tap - 1) * tap_spacing,
                    band_rows,
                    band_cols,
                )
                grad_in = grad_in + grad_tap.astype(jnp.float32) * depth_weights[
                    branch_level, row_tap, col_tap
                ].astype(jnp.float32)
    return (output, grad_in.astype(jnp.bfloat16), grad_depth, grad_point, grad_proj)


def folds(mesh, features_in):
    sizes = mesh.shape
    samples, rows, cols, channels = features_in.shape
    return (
        rows == 3 * BASE_DILATION
        and sizes["row"] == 2
        and sizes["chan"] == 4
        and sizes["dp"] == 4
        and samples == sizes["dp"]
        and cols % 64 == 0
        and channels % (128 * sizes["chan"]) == 0
    )


def solution(mesh):
    in_specs = (
        P("dp", "row", None, "chan"),
        P(None, None, None, "chan"),
        P(None, "chan", None),
        P(),
        P("dp", "row", "chan", None),
    )
    out_specs = (
        P("dp", "row", "chan", None),
        P("dp", "row", None, "chan"),
        P(None, None, None, "chan"),
        P(None, "chan", None),
        P(),
    )

    def run(*args):
        body = by_classes if folds(mesh, args[0]) else on_device
        return jax.shard_map(
            body, mesh=mesh, in_specs=in_specs, out_specs=out_specs, check_vma=False
        )(*args)

    return run
```

```python
import functools
import math

import jax
import jax.numpy as jnp
from jax import lax
from jax.experimental import pallas as pl
from jax.experimental.pallas import tpu as pltpu
from jax.sharding import PartitionSpec as P

BASE_DILATION = 12
F32 = jnp.float32
BF16 = jnp.bfloat16
VMEM_BYTES = 16 * 2**20


def swap(value, axis, flip):
    count = lax.axis_size(axis)
    return lax.ppermute(value, axis, [(i, i ^ flip) for i in range(count)])


def moved(value, steps):
    if steps == 0:
        return value
    count = value.shape[0]
    rolled = pltpu.roll(value, (-steps) % count, 0)
    place = lax.broadcasted_iota(jnp.int32, value.shape, 0)
    inside = place < count - steps if steps > 0 else place >= -steps
    return jnp.where(inside, rolled, 0.0)


def row_pairs(branch, classes):
    return [
        (q, i, q + (i - 1) * branch)
        for q in range(classes)
        for i in range(3)
        if 0 <= q + (i - 1) * branch < classes
    ]


def class_rows(upper, first, last, arrived):
    return (
        jnp.where(upper, first, arrived),
        jnp.where(upper, last, first),
        jnp.where(upper, arrived, last),
    )


def shape_of(shape, dtype):
    return jax.ShapeDtypeStruct(shape, dtype)


def in_hbm(value):
    return pltpu.with_memory_space_constraint(value, pltpu.HBM)


def result_of(shape, dtype):
    return jax.ShapeDtypeStruct(shape, dtype)


TOKEN = (8, 128)
STEPS = 2


def call(body, place, grid, after, ins, outs, name, scratch=()):
    def spec(block, split):
        dims = len(block)
        if isinstance(split, tuple):
            return pl.BlockSpec(block, lambda r, p: tuple(r if k is None else k for k in split))
        return pl.BlockSpec(block, lambda r, p: tuple(r if k == split else 0 for k in range(dims)))

    def kernel(place_ref, after_ref, *refs):
        last = len(ins) + len(outs) - 2
        body(place_ref, *refs[:last], *refs[last + 1 :])
        refs[last][...] = after_ref[...]

    ins = [(after, TOKEN, None)] + list(ins)
    outs = list(outs) + [(shape_of(TOKEN, F32), TOKEN, None)]
    return pl.pallas_call(
        kernel,
        grid_spec=pltpu.PrefetchScalarGridSpec(
            num_scalar_prefetch=1,
            grid=(grid,),
            in_specs=[spec(block, split) for _, block, split in ins],
            out_specs=[spec(block, split) for _, block, split in outs],
            scratch_shapes=list(scratch),
        ),
        out_shape=[s for s, _, _ in outs],
        compiler_params=pltpu.CompilerParams(vmem_limit_bytes=VMEM_BYTES),
        cost_estimate=pl.CostEstimate(flops=1, bytes_accessed=1, transcendentals=0),
        name=name,
    )(place, *[a for a, _, _ in ins])


def forward_kernel(branches, folded, place, x_ref, arrived_ref, taps_ref, *refs):
    classes, group, cols, channels = x_ref.shape
    count = len(branches)
    points, refs = refs[:count], refs[count:]
    keeps, sends, refs = refs[:count], refs[count : 2 * count], refs[2 * count :]
    spreads = dict(zip([b for b in branches if b], refs))
    if not folded:
        refs[-1][...] = x_ref[1]

    def residue(r, carry):
        rows = [x_ref[q, r].astype(F32) for q in range(classes)]
        if folded:
            rows = class_rows(place[1] == 0, rows[0], rows[2], arrived_ref[r].astype(F32))
        for branch, spread_ref in spreads.items():
            for q in range(classes):
                total = None
                for j in range(3):
                    part = None
                    for out, i, source in row_pairs(branch, classes):
                        if out == q:
                            tap = taps_ref[branch - 1, i, j].astype(F32)
                            term = rows[source] * tap[None, :]
                            part = term if part is None else part + term
                    part = moved(part, (j - 1) * branch * BASE_DILATION)
                    total = part if total is None else total + part
                spread_ref[q, r] = total.astype(BF16)
        return carry

    lax.fori_loop(0, group, residue, 0)
    for k, branch in enumerate(branches):
        cells = spreads[branch][...] if branch else x_ref[...]
        cells = cells.reshape(classes * group * cols, channels)
        partial = jnp.dot(cells, points[k][0], preferred_element_type=F32)
        split = partial.reshape(classes * group * 2, 2, cols // 4, partial.shape[-1])
        first = place[0] % 2 == 0
        keep = jnp.where(first, split[:, 0], split[:, 1])
        send = jnp.where(first, split[:, 1], split[:, 0])
        keeps[k][0] = keep.reshape(keeps[k].shape[1:])
        sends[k][0] = send.reshape(sends[k].shape[1:]).astype(BF16)


def forward(branches, folded, place, after, x, arrived, taps, point):
    classes, residues, cols, channels = x.shape
    filters = point.shape[2]
    group = residues // STEPS
    cell = (classes, group, cols, channels)
    part = (1, classes, group, 2, cols // 4, filters)
    part_shape = (1, classes, residues, 2, cols // 4, filters)
    outs = [(shape_of(part_shape, F32), part, 2) for _ in branches]
    outs += [(shape_of(part_shape, BF16), part, 2) for _ in branches]
    outs += [(pltpu.HBM(x.shape, BF16), cell, 1) for b in branches if b]
    if not folded:
        outs += [(shape_of(x.shape[1:], BF16), (group, cols, channels), 0)]
    return call(
        functools.partial(forward_kernel, branches, folded), place, STEPS, after,
        [
            (x, cell, 1),
            (arrived, (group, cols, channels) if folded else (1, 1, 8, 128), 0 if folded else None),
            (taps, taps.shape, None),
        ]
        + [(point, (1, channels, filters), (b, 0, 0)) for b in branches],
        outs, "forward_" + "_".join(map(str, branches)),
    )


def near_kernel(place, keep_ref, arrived_ref, near_ref):
    near_ref[...] = (keep_ref[...] + arrived_ref[...].astype(F32)).astype(BF16)


def near_sum(name, place, after, keep, arrived):
    return call(
        near_kernel, place, 1, after, [(keep, keep.shape, None), (arrived, keep.shape, None)],
        [(shape_of(keep.shape, BF16), keep.shape, None)], f"near_{name}",
    )


def near_cots_kernel(place, keep_ref, arrived_ref, cot_ref, far_ref, near_ref, cots_ref, leaving_ref):
    near_kernel(place, keep_ref, arrived_ref, near_ref)
    low_side = place[0] // 2 == 0
    cots_ref[:, 0] = jnp.where(low_side, cot_ref[...], far_ref[...])
    cots_ref[:, 1] = jnp.where(low_side, far_ref[...], cot_ref[...])
    n = leaving_ref.shape[0]
    leaving_ref[...] = cots_ref[n : 2 * n]


def near_sum_cots(name, place, after, keep, arrived, cot, far):
    rows, width, filters = cot.shape
    cots = (rows, 2, width, filters)
    leaving = (rows // 3, 2, width, filters)
    return call(
        near_cots_kernel, place, 1, after,
        [(a, a.shape, None) for a in (keep, arrived, cot, far)],
        [(shape_of(s, BF16), s, None) for s in (keep.shape, cots, leaving)], f"near_{name}",
    )


def gate_kernel(branch, folded, stacked, place, near_ref, far_ref, cot_ref, *refs):
    _, classes, residues, sides, width, filters = near_ref.shape
    if folded:
        arrived_ref, refs = refs[0], refs[1:]
    paired = len(refs) > 5
    if paired:
        proj_ref, mixed_ref, earlier_ref, *refs = refs
        above = []
        if stacked:
            above, refs = refs[:2], refs[2:]
        grad_ref, out_ref, keep_ref, send_ref, *leaving = refs
    else:
        proj_ref, mixed_ref, grad_ref, out_ref, proj_grad_ref = refs
    n = residues
    cots = cot_ref[...]
    if folded:
        cots = jnp.concatenate(
            class_rows(place[1] == 0, cots[:n], cots[2 * n : 3 * n], arrived_ref[...])
        )
    cells = cots.reshape(-1, filters)
    shape = (classes * residues, sides, width, filters)
    proj = proj_ref[0]
    act_grad = lax.dot_general(cells, proj, (((1,), (1,)), ((), ())), preferred_element_type=F32)
    preact = (near_ref[0].astype(F32) + far_ref[0].astype(F32)).reshape(shape)
    logistic = 1.0 / (1.0 + jnp.exp(-preact))
    grad = act_grad.reshape(shape) * logistic * (1.0 + preact * (1.0 - logistic))
    grad_ref[0] = grad.astype(BF16).reshape(grad_ref.shape[1:])
    active = (preact * logistic).astype(BF16)
    mine = jnp.where(place[0] // 2 == 0, active[:, 0], active[:, 1]).reshape(-1, filters)
    mixed = mixed_ref[...] + jnp.dot(mine, proj, preferred_element_type=F32).reshape(out_ref.shape)
    out_ref[...] = mixed
    proj_grad = lax.dot_general(
        active.reshape(-1, filters), cells, (((0,), (0,)), ((), ())), preferred_element_type=F32
    )
    if not paired:
        proj_grad_ref[...] = proj_grad
        return
    first = place[2] == 0
    at = keep_ref.shape[0] - filters
    keep_ref[at:] = jnp.where(first, earlier_ref[...], proj_grad)
    send_ref[at:] = jnp.where(first, proj_grad, earlier_ref[...]).astype(BF16)
    if above:
        keep_ref[:at] = above[0][...]
        send_ref[:at] = above[1][...]
    if leaving:
        leaving[0][...] = jnp.where(place[1] == 0, mixed[2 * n :], mixed[:n]).astype(BF16)


def gate(branch, folded, place, after, near, far, cots, arrived, proj, mixed, earlier=None, above=()):
    filters = proj.shape[-1]
    arrays = [near, far, cots] + ([arrived] if folded else [])
    ins = [(a, a.shape, None) for a in arrays] + [(proj, (1, filters, filters), (branch, 0, 0))]
    ins += [(a, a.shape, None) for a in ([mixed] if earlier is None else [mixed, earlier, *above])]
    part = (2 * filters if above else filters, filters)
    shapes = [(near.shape, BF16), (mixed.shape, F32), (part, F32)]
    if earlier is not None:
        shapes.append((part, BF16))
    if above:
        shapes.append(((mixed.shape[0] // 3,) + mixed.shape[1:], BF16))
    return call(
        functools.partial(gate_kernel, branch, folded, bool(above)), place, 1, after, ins,
        [(shape_of(shape, kind), shape, None) for shape, kind in shapes], f"gate_{branch}",
    )


def whole_columns(place, own, other):
    thin = (-1,) + own.shape[-2:]
    own, other = own.reshape(thin), other.reshape(thin)
    first = place[0] % 2 == 0
    low = jnp.where(first, own, other)
    high = jnp.where(first, other, own)
    both = jnp.concatenate([low[:, None], high[:, None]], axis=1)
    return both.reshape(-1, own.shape[-1])


def split_by_core(place, low, high, keep_ref, send_ref):
    first = place[2] == 0
    rows = low.shape[0]
    keep_ref[:rows] = jnp.where(first, low, high)
    send_ref[:rows] = jnp.where(first, high, low).astype(send_ref.dtype)


def backward_kernel(
    branch, folded, final, chained, place, own_ref, other_ref, x_ref, arrived_ref, spread_ref, taps_ref,
    point_ref, before_ref, *refs
):
    classes, group, cols, channels = x_ref.shape
    point_grad_ref, depth_ref, grads_ref = refs[-3:]
    refs = refs[:-3]
    upper = place[1] == 0
    pre = whole_columns(place, own_ref[0], other_ref[0])
    grads = lax.dot_general(pre, point_ref[0], (((1,), (1,)), ((), ())), preferred_element_type=F32)
    grads_ref[...] = grads.astype(BF16).reshape(grads_ref.shape)
    cells = spread_ref[...].reshape(classes * group * cols, channels)
    product = lax.dot_general(cells, pre, (((0,), (0,)), ((), ())), preferred_element_type=F32)

    @pl.when(pl.program_id(0) == 0)
    def _():
        point_grad_ref[...] = product
        depth_ref[...] = jnp.zeros_like(depth_ref)

    @pl.when(pl.program_id(0) > 0)
    def _():
        point_grad_ref[...] += product

    outs = refs[2:] if chained else refs
    pairs = row_pairs(branch, classes)

    def residue(r, carry):
        rows = [x_ref[q, r].astype(F32) for q in range(classes)]
        if folded:
            rows = class_rows(upper, rows[0], rows[2], arrived_ref[r].astype(F32))
        grads = [grads_ref[q, r].astype(F32) for q in range(classes)]
        for j in range(3):
            near = [moved(row, (j - 1) * branch * BASE_DILATION) for row in rows]
            for i in range(3):
                part = None
                for q, tap, source in pairs:
                    if tap == i:
                        term = (near[source] * grads[q]).reshape(cols // 8, 8, channels).sum(axis=0)
                        part = term if part is None else part + term
                if part is not None:
                    depth_ref[i * 3 + j] += part
        totals = []
        for target in range(classes):
            total = before_ref[target, r] if chained else None
            for j in range(3):
                part = None
                for q, i, source in pairs:
                    if source == target:
                        term = grads[q] * taps_ref[branch - 1, i, j].astype(F32)[None, :]
                        part = term if part is None else part + term
                part = moved(part, -(j - 1) * branch * BASE_DILATION)
                total = part if total is None else total + part
            totals.append(total)
        if chained:
            leaving_ref, stay_ref = outs[:2]
            leaving_ref[r] = jnp.where(upper, totals[2], totals[0]).astype(BF16)
            stay_ref[0, r] = jnp.where(upper, totals[0], totals[1])
            stay_ref[1, r] = jnp.where(upper, totals[1], totals[2])
        else:
            for q in range(classes):
                outs[0][q, r] = totals[q]
        return carry

    lax.fori_loop(0, group, residue, 0)

    @pl.when(pl.program_id(0) == STEPS - 1)
    def _():
        depth = depth_ref[...].sum(axis=1)
        if final:
            keep_ref, send_ref = outs[-2:]
            half, filters = channels // 2, point_grad_ref.shape[1]
            split_by_core(place, point_grad_ref[:half], point_grad_ref[half:], keep_ref, send_ref)
            if chained:
                depths = jnp.concatenate([refs[0][...], depth, refs[1][...]])
                low, high = depths[:, :filters], depths[:, filters:]
                first = place[2] == 0
                keep_ref[half : half + 27] = jnp.where(first, low, high)
                send_ref[half : half + 27] = jnp.where(first, high, low).astype(BF16)
                blank = jnp.zeros((keep_ref.shape[0] - half - 27, filters), F32)
                keep_ref[half + 27 :] = blank
                send_ref[half + 27 :] = blank.astype(BF16)
            else:
                outs[-3][...] = depth
        else:
            outs[-2][...] = point_grad_ref[...]
            outs[-1][...] = depth


def backward(
    branch, folded, final, place, after, own, other, x, arrived, spread, taps, point, before=None, depths=()
):
    classes, residues, cols, channels = x.shape
    filters = point.shape[2]
    group = residues // STEPS
    part = (1, classes, group, 2, cols // 4, filters)
    cell = (classes, group, cols, channels)
    thin = (group, cols, channels)
    chained = before is not None
    if chained:
        outs = [
            (shape_of(x.shape[1:], BF16), thin, 0),
            (pltpu.HBM((2,) + x.shape[1:], F32), (2,) + thin, 1),
        ]
    else:
        outs = [(pltpu.HBM(x.shape, F32), cell, 1)]
    halves = (channels // 2 + (32 if chained else 0), filters)
    shapes = [(channels, filters), (9, channels)]
    if final:
        shapes = [halves, halves] if chained else [(9, channels), halves, halves]
    outs += [(shape_of(shape, F32), shape, None) for shape in shapes]
    if final:
        outs[-1] = (shape_of(halves, BF16), halves, None)
    small = (1, 1, 8, 128)
    return call(
        functools.partial(backward_kernel, branch, folded, final, chained), place, STEPS, after,
        [
            (own, part, 2),
            (other, part, 2),
            (x, cell, 1),
            (arrived, thin, 0) if folded else (x, small, None),
            (spread, cell, 1),
            (taps, taps.shape, None),
            (point, (1, channels, filters), (branch, 0, 0)),
            (before, cell, 1) if chained else (x, small, None),
        ]
        + [(d, d.shape, None) for d in depths],
        outs, f"backward_{branch}",
        scratch=[
            pltpu.VMEM((channels, filters), F32),
            pltpu.VMEM((9, 8, channels), F32),
            pltpu.VMEM(cell, BF16),
        ],
    )


def join_kernel(place, own_ref, other_ref, x_ref, earlier_ref, pre_ref, keep_ref, send_ref, total_ref):
    pre = whole_columns(place, own_ref[0], other_ref[0])
    pre_ref[...] = pre.reshape(pre_ref.shape)
    cells = x_ref[...].reshape(-1, x_ref.shape[-1])
    product = lax.dot_general(cells, pre, (((0,), (0,)), ((), ())), preferred_element_type=F32)

    @pl.when(pl.program_id(0) == 0)
    def _():
        total_ref[...] = product

    @pl.when(pl.program_id(0) > 0)
    def _():
        total_ref[...] += product

    @pl.when(pl.program_id(0) == STEPS - 1)
    def _():
        split_by_core(place, earlier_ref[...], total_ref[...], keep_ref, send_ref)


def join(place, after, own, other, x, earlier):
    classes, residues, cols, channels = x.shape
    filters = own.shape[-1]
    group = residues // STEPS
    part = (1, classes, group, 2, cols // 4, filters)
    return call(
        join_kernel, place, STEPS, after,
        [
            (own, part, 2),
            (other, part, 2),
            (x, (classes, group, cols, channels), 1),
            (earlier, earlier.shape, None),
        ],
        [
            (shape_of((classes, residues, cols, filters), BF16), (classes, group, cols, filters), 1),
            (shape_of(earlier.shape, F32), earlier.shape, None),
            (shape_of(earlier.shape, BF16), earlier.shape, None),
        ],
        "join", scratch=[pltpu.VMEM(earlier.shape, F32)],
    )


def last_kernel(
    place, pre_ref, point_ref, band_ref, stay_ref, arrived_ref, mixed_ref, folded_ref, mixed_arrived_ref,
    input_ref, output_ref
):
    classes, group, cols, channels = band_ref.shape
    pre = pre_ref[...].reshape(classes * group * cols, -1)
    grads = lax.dot_general(pre, point_ref[0], (((1,), (1,)), ((), ())), preferred_element_type=F32)
    grads = grads.astype(BF16).astype(F32).reshape(band_ref.shape)
    others = (stay_ref[0], arrived_ref[...].astype(F32), stay_ref[1])
    for q in range(classes):
        input_ref[q] = (grads[q] + band_ref[q] + others[q]).astype(BF16)
    upper = place[1] == 0
    mixed = (
        jnp.where(upper, folded_ref[0], folded_ref[1]),
        mixed_arrived_ref[...].astype(F32),
        jnp.where(upper, folded_ref[1], folded_ref[2]),
    )
    for q in range(classes):
        output_ref[q] = (mixed_ref[q] + mixed[q]).astype(BF16)


def last(place, after, pre, point, band, stay, arrived, mixed, folded, mixed_arrived):
    classes, residues, cols, channels = band.shape
    filters = point.shape[2]
    group = residues // STEPS
    cell = (classes, group, cols, channels)
    thin = (classes, group) + mixed.shape[2:]
    return call(
        last_kernel, place, STEPS, after,
        [
            (pre, (classes, group, cols, filters), 1),
            (point, (1, channels, filters), (0, 0, 0)),
            (band, cell, 1),
            (stay, (2, group, cols, channels), 1),
            (arrived, (group, cols, channels), 0),
            (mixed, thin, 1),
            (folded, thin, 1),
            (mixed_arrived, thin[1:], 0),
        ],
        [(result_of(band.shape, BF16), cell, 1), (result_of(mixed.shape, BF16), thin, 1)], "last",
    )


def add_kernel(scale, counts, place, *refs):
    *terms, out_ref = refs
    at = 0
    for count in counts:
        group, terms = terms[:count], terms[count:]
        values = [ref[...].astype(F32) for ref in group]
        total = values[0] + values[1]
        if scale != 1.0:
            total = total * scale
        rows = group[0].shape[0]
        out_ref[at : at + rows] = total.astype(out_ref.dtype)
        at += rows


def add(name, place, after, groups, kind, scale=1.0):
    shape = (sum(group[0].shape[0] for group in groups), groups[0][0].shape[1])
    counts = [len(group) for group in groups]
    return call(
        functools.partial(add_kernel, scale, counts), place, 1, after,
        [(a, a.shape, None) for group in groups for a in group],
        [(shape_of(shape, kind), shape, None)], name,
    )


def finish_kernel(place, own30, far30, own1, far1, own2, far2, proj_ref, depth_ref, point_ref):
    core = place[2] == 0

    def halves(own, far, first, count):
        own, far = own[first : first + count], far[first : first + count]
        return jnp.where(core, own, far), jnp.where(core, far, own)

    channels = point_ref.shape[1]
    filters = proj_ref.shape[1]
    half = channels // 2
    point_ref[3], point_ref[0] = halves(own30, far30, 0, channels)
    point_ref[1, :half], point_ref[1, half:] = halves(own1, far1, 0, half)
    proj_ref[3], proj_ref[0] = halves(own1, far1, half, filters)
    proj_ref[1], proj_ref[2] = halves(own1, far1, half + filters, filters)
    point_ref[2, :half], point_ref[2, half:] = halves(own2, far2, 0, half)
    low, high = halves(own2, far2, half, 27)
    for k in range(9):
        rows = slice(3 * k, 3 * k + 3)
        depth_ref[k // 3, k % 3, :, :filters] = low[rows]
        depth_ref[k // 3, k % 3, :, filters:] = high[rows]


def finish(place, after, early, middle, late, channels, filters):
    arrays = [*early, *middle, *late]
    shapes = [(4, filters, filters), (3, 3, 3, channels), (4, channels, filters)]
    return call(
        finish_kernel, place, 1, after, [(a, a.shape, None) for a in arrays],
        [(result_of(s, F32), s, None) for s in shapes], "finish",
    )


def by_classes(features_in, depth_weights, point_weights, proj_weights, cotangent):
    _, band_rows, cols, channels = features_in.shape
    filters = point_weights.shape[2]
    classes, n = 3, band_rows // 3
    scale = 1.0 / math.sqrt(lax.axis_size("dp") * band_rows * lax.axis_size("row") * cols)
    chan, row = lax.axis_index("chan"), lax.axis_index("row")
    core = lax.axis_index("dp") % 2
    place = jnp.stack([chan, row, core]).astype(jnp.int32)
    x = features_in[0].reshape(classes, n, cols, channels)

    weights = (depth_weights, point_weights)
    cot = cotangent[0]
    cot_far = swap(cot, "chan", 2)

    token, blank = jnp.zeros(TOKEN, F32), jnp.zeros(cot.shape, F32)
    keep3, keep0, send3, send0, spread3, x_leaving, token = forward(
        (3, 0), False, place, token, in_hbm(x), x, in_hbm(depth_weights), in_hbm(point_weights)
    )
    sent3, sent0 = swap(send3, "chan", 1), swap(send0, "chan", 1)
    arrived = swap(x_leaving, "row", 1)
    near3, token = near_sum("3", place, token, keep3, sent3)
    far3 = swap(near3, "chan", 2)
    keep1, keep2, send1, send2, spread1, spread2, token = forward(
        (1, 2), True, place, token, x, arrived, *weights
    )
    sent1, sent2 = swap(send1, "chan", 1), swap(send2, "chan", 1)
    near0, cots, cots_leaving, token = near_sum_cots("0", place, token, keep0, sent0, cot, cot_far)
    far0 = swap(near0, "chan", 2)
    cots_arrived = swap(cots_leaving, "row", 1)
    grad3, band_mixed, proj3, token = gate(
        3, False, place, token, near3, far3, cots, None, proj_weights, blank
    )
    other3 = swap(grad3, "chan", 1)
    near1, token = near_sum("1", place, token, keep1, sent1)
    far1 = swap(near1, "chan", 2)
    grad0, band_mixed, proj_keep, proj_send, token = gate(
        0, False, place, token, near0, far0, cots, None, proj_weights, band_mixed, proj3
    )
    other0 = swap(grad0, "chan", 1)
    near2, token = near_sum("2", place, token, keep2, sent2)
    far2 = swap(near2, "chan", 2)
    grad1, class_mixed, proj1, token = gate(
        1, True, place, token, near1, far1, cots, cots_arrived, proj_weights, blank
    )
    other1 = swap(grad1, "chan", 1)
    band, point3, depth3, token = backward(
        3, False, False, place, token, grad3, other3, x, x, spread3, *weights
    )
    pre0, point_keep, point_send, token = join(place, token, grad0, other0, x, point3)
    point30 = (point_keep, swap(point_send, "dp", 1))
    grad2, class_mixed, proj_keep, proj_send, mixed_leaving, token = gate(
        2, True, place, token, near2, far2, cots, cots_arrived, proj_weights, class_mixed, proj1,
        (proj_keep, proj_send),
    )
    other2 = swap(grad2, "chan", 1)
    mixed_arrived = swap(mixed_leaving, "row", 1)
    proj = (proj_keep, swap(proj_send, "dp", 1))
    total1, depth1, point_keep, point_send, token = backward(
        1, True, True, place, token, grad1, other1, x, arrived, spread1, *weights
    )
    point1 = (point_keep, swap(point_send, "dp", 1))
    early, token = add("early_y", place, token, [point30], BF16)
    early = (early, swap(early, "row", 1))
    leaving, stay, late_keep, late_send, token = backward(
        2, True, True, place, token, grad2, other2, x, arrived, spread2, *weights, before=total1,
        depths=(depth1, depth3),
    )
    input_arrived = swap(leaving, "row", 1)
    late = (late_keep, swap(late_send, "dp", 1))
    proj, token = add("proj", place, token, [proj], BF16)
    proj = (proj, swap(proj, "chan", 1))
    early, token = add("early_x", place, token, [early], BF16)
    early = (early, swap(early, "dp", 2))
    late, token = add("late_x", place, token, [late], BF16)
    late = (late, swap(late, "dp", 2))
    middle, token = add("middle_y", place, token, [point1, proj], BF16)
    middle = (middle, swap(middle, "row", 1))
    late, token = add("late_y", place, token, [late], BF16)
    late = (late, swap(late, "row", 1))
    early, token = add("early", place, token, [early], F32, scale)
    early = (early, swap(early, "dp", 1))
    middle, token = add("middle_x", place, token, [middle], BF16)
    middle = (middle, swap(middle, "dp", 2))
    late, token = add("late", place, token, [late], F32, scale)
    late = (late, swap(late, "dp", 1))
    bands = band_mixed.reshape((classes, n) + band_mixed.shape[1:])
    folds = class_mixed.reshape(bands.shape)
    grad_input, output, token = last(
        place, token, pre0, point_weights, in_hbm(band), in_hbm(stay), input_arrived, bands, folds,
        mixed_arrived,
    )
    middle, token = add("middle", place, token, [middle], F32, scale)
    middle = (middle, swap(middle, "dp", 1))
    grad_proj, grad_depth, grad_point, token = finish(
        place, token, early, middle, late, channels, filters
    )
    return (
        output.reshape(cotangent.shape), grad_input.reshape(features_in.shape), grad_depth, grad_point,
        grad_proj,
    )


def shifted(value, axis, steps):
    count = lax.axis_size(axis)
    first, last = (max(0, -steps), min(count, count - steps))
    return lax.ppermute(value, axis, [(source, source + steps) for source in range(first, last)])


def window(source, top, left, band_rows, band_cols):
    upper = lax.slice_in_dim(source, top, top + band_rows, axis=1)
    return lax.slice_in_dim(upper, left, left + band_cols, axis=2)


def on_device(features_in, depth_weights, point_weights, proj_weights, cotangent):
    samples, band_rows, band_cols, channels = features_in.shape
    weight_scale = 1.0 / math.sqrt(
        samples * lax.axis_size("dp") * band_rows * lax.axis_size("row") * band_cols
    )
    largest_reach = 3 * BASE_DILATION
    offsets = (2, 1, -1, -2)
    arrivals = []
    for offset in offsets:
        arrivals.append(shifted(features_in, "row", offset))
    tall_rows = jnp.concatenate(
        [arrivals[0], arrivals[1], features_in, arrivals[2], arrivals[3]], axis=1
    )
    padded = jnp.pad(tall_rows, ((0, 0), (0, 0), (largest_reach, largest_reach), (0, 0)))
    branch_maps = [features_in]
    for branch_level in range(3):
        tap_spacing = (branch_level + 1) * BASE_DILATION
        summed = jnp.zeros(features_in.shape, jnp.float32)
        for row_tap in range(3):
            for col_tap in range(3):
                input_kernel_tap = window(
                    padded,
                    largest_reach + (row_tap - 1) * tap_spacing,
                    largest_reach + (col_tap - 1) * tap_spacing,
                    band_rows,
                    band_cols,
                )
                summed = summed + input_kernel_tap.astype(jnp.float32) * depth_weights[
                    branch_level, row_tap, col_tap
                ].astype(jnp.float32)
        branch_maps.append(summed.astype(jnp.bfloat16))
    spread = jnp.stack(branch_maps)
    full_point = lax.all_gather(point_weights, "chan", axis=1, tiled=True)
    preact = jnp.einsum(
        "bsrwc,bcf->bsrwf",
        lax.all_to_all(spread, "chan", split_axis=3, concat_axis=4, tiled=True),
        full_point,
        preferred_element_type=jnp.float32,
    )
    activation = jax.nn.silu(preact).astype(jnp.bfloat16)
    output = jnp.einsum(
        "bsrwf,bfg->srwg", activation, proj_weights, preferred_element_type=jnp.float32
    ).astype(jnp.bfloat16)
    silu_gradient = jnp.einsum(
        "srwg,bfg->bsrwf", cotangent, proj_weights, preferred_element_type=jnp.float32
    )
    logistic = jax.nn.sigmoid(preact)
    pre_grad = (silu_gradient * logistic * (1.0 + preact * (1.0 - logistic))).astype(jnp.bfloat16)
    proj_term = jnp.einsum(
        "bsrwf,srwg->bfg", activation, cotangent, preferred_element_type=jnp.float32
    )
    grad_proj = lax.psum(proj_term, ("row", "chan", "dp")) * weight_scale
    incoming = lax.all_gather(pre_grad, "chan", axis=3, tiled=True)
    local_grad = jnp.einsum(
        "bsrwf,bcf->bsrwc", incoming, point_weights, preferred_element_type=jnp.float32
    ).astype(jnp.bfloat16)
    spread_grad = local_grad
    point_sum = jnp.einsum("bsrwc,bsrwf->bcf", spread, incoming, preferred_element_type=jnp.float32)
    spread_grad, point_term = (spread_grad, point_sum)
    depth_rows = []
    for branch_level in range(3):
        tap_spacing = (branch_level + 1) * BASE_DILATION
        branch_grad = spread_grad[branch_level + 1].astype(jnp.float32)
        gathered = []
        for row_tap in range(3):
            for col_tap in range(3):
                input_kernel_tap = window(
                    padded,
                    largest_reach + (row_tap - 1) * tap_spacing,
                    largest_reach + (col_tap - 1) * tap_spacing,
                    band_rows,
                    band_cols,
                )
                gathered.append(
                    jnp.sum(input_kernel_tap.astype(jnp.float32) * branch_grad, axis=(0, 1, 2))
                )
        depth_rows.append(jnp.stack(gathered).reshape(3, 3, channels))
    depth_term = jnp.stack(depth_rows)
    point_summed, depth_summed = lax.psum((point_term, depth_term), ("row", "dp"))
    grad_point = point_summed * weight_scale
    grad_depth = depth_summed * weight_scale
    neighbour_sets = []
    for branch_level in range(3):
        neighbour_sets.append(
            [shifted(spread_grad[branch_level + 1], "row", offset) for offset in offsets]
        )
    grad_in = spread_grad[0].astype(jnp.float32)
    for branch_level in range(3):
        tap_spacing = (branch_level + 1) * BASE_DILATION
        received = neighbour_sets[branch_level]
        grad_tall = jnp.concatenate(
            [received[0], received[1], spread_grad[branch_level + 1], received[2], received[3]],
            axis=1,
        )
        grad_padded = jnp.pad(grad_tall, ((0, 0), (0, 0), (largest_reach, largest_reach), (0, 0)))
        for row_tap in range(3):
            for col_tap in range(3):
                grad_tap = window(
                    grad_padded,
                    largest_reach - (row_tap - 1) * tap_spacing,
                    largest_reach - (col_tap - 1) * tap_spacing,
                    band_rows,
                    band_cols,
                )
                grad_in = grad_in + grad_tap.astype(jnp.float32) * depth_weights[
                    branch_level, row_tap, col_tap
                ].astype(jnp.float32)
    return (output, grad_in.astype(jnp.bfloat16), grad_depth, grad_point, grad_proj)


def folds(mesh, features_in):
    sizes = mesh.shape
    samples, rows, cols, channels = features_in.shape
    return (
        rows == 3 * BASE_DILATION
        and sizes["row"] == 2
        and sizes["chan"] == 4
        and sizes["dp"] == 4
        and samples == sizes["dp"]
        and cols % 64 == 0
        and channels % (128 * sizes["chan"]) == 0
    )


def solution(mesh):
    in_specs = (
        P("dp", "row", None, "chan"),
        P(None, None, None, "chan"),
        P(None, "chan", None),
        P(),
        P("dp", "row", "chan", None),
    )
    out_specs = (
        P("dp", "row", "chan", None),
        P("dp", "row", None, "chan"),
        P(None, None, None, "chan"),
        P(None, "chan", None),
        P(),
    )

    def run(*args):
        body = by_classes if folds(mesh, args[0]) else on_device
        return jax.shard_map(
            body, mesh=mesh, in_specs=in_specs, out_specs=out_specs, check_vma=False
        )(*args)

    return run
```

```python
import functools
import math

import jax
import jax.numpy as jnp
from jax import lax
from jax.experimental import pallas as pl
from jax.experimental.pallas import tpu as pltpu
from jax.sharding import PartitionSpec as P

BASE_DILATION = 12
F32 = jnp.float32
BF16 = jnp.bfloat16
VMEM_BYTES = 16 * 2**20


def swap(value, axis, flip):
    count = lax.axis_size(axis)
    return lax.ppermute(value, axis, [(i, i ^ flip) for i in range(count)])


def moved(value, steps):
    if steps == 0:
        return value
    count = value.shape[0]
    rolled = pltpu.roll(value, (-steps) % count, 0)
    place = lax.broadcasted_iota(jnp.int32, value.shape, 0)
    inside = place < count - steps if steps > 0 else place >= -steps
    return jnp.where(inside, rolled, 0.0)


def row_pairs(branch, classes):
    return [
        (q, i, q + (i - 1) * branch)
        for q in range(classes)
        for i in range(3)
        if 0 <= q + (i - 1) * branch < classes
    ]


def class_rows(upper, first, last, arrived):
    return (
        jnp.where(upper, first, arrived),
        jnp.where(upper, last, first),
        jnp.where(upper, arrived, last),
    )


def shape_of(shape, dtype):
    return jax.ShapeDtypeStruct(shape, dtype)


def in_hbm(value):
    return pltpu.with_memory_space_constraint(value, pltpu.HBM)


def result_of(shape, dtype):
    return jax.ShapeDtypeStruct(shape, dtype)


TOKEN = (8, 128)
STEPS = 2


def call(body, place, grid, after, ins, outs, name, scratch=()):
    def spec(block, split):
        dims = len(block)
        if isinstance(split, tuple):
            return pl.BlockSpec(block, lambda r, p: tuple(r if k is None else k for k in split))
        return pl.BlockSpec(block, lambda r, p: tuple(r if k == split else 0 for k in range(dims)))

    def kernel(place_ref, after_ref, *refs):
        last = len(ins) + len(outs) - 2
        body(place_ref, *refs[:last], *refs[last + 1 :])
        refs[last][...] = after_ref[...]

    ins = [(after, TOKEN, None)] + list(ins)
    outs = list(outs) + [(shape_of(TOKEN, F32), TOKEN, None)]
    return pl.pallas_call(
        kernel,
        grid_spec=pltpu.PrefetchScalarGridSpec(
            num_scalar_prefetch=1,
            grid=(grid,),
            in_specs=[spec(block, split) for _, block, split in ins],
            out_specs=[spec(block, split) for _, block, split in outs],
            scratch_shapes=list(scratch),
        ),
        out_shape=[s for s, _, _ in outs],
        compiler_params=pltpu.CompilerParams(vmem_limit_bytes=VMEM_BYTES),
        cost_estimate=pl.CostEstimate(flops=1, bytes_accessed=1, transcendentals=0),
        name=name,
    )(place, *[a for a, _, _ in ins])


def forward_kernel(branches, folded, place, x_ref, arrived_ref, taps_ref, *refs):
    classes, group, cols, channels = x_ref.shape
    count = len(branches)
    points, refs = refs[:count], refs[count:]
    keeps, sends, refs = refs[:count], refs[count : 2 * count], refs[2 * count :]
    spreads = dict(zip([b for b in branches if b], refs))
    if not branches[0]:
        refs[-1][...] = x_ref[1]

    def residue(r, carry):
        rows = [x_ref[q, r].astype(F32) for q in range(classes)]
        if folded:
            rows = class_rows(place[1] == 0, rows[0], rows[2], arrived_ref[r].astype(F32))
        for branch, spread_ref in spreads.items():
            for q in range(classes):
                total = None
                for j in range(3):
                    part = None
                    for out, i, source in row_pairs(branch, classes):
                        if out == q:
                            tap = taps_ref[branch - 1, i, j].astype(F32)
                            term = rows[source] * tap[None, :]
                            part = term if part is None else part + term
                    part = moved(part, (j - 1) * branch * BASE_DILATION)
                    total = part if total is None else total + part
                spread_ref[q, r] = total.astype(BF16)
        return carry

    lax.fori_loop(0, group, residue, 0)
    for k, branch in enumerate(branches):
        cells = spreads[branch][...] if branch else x_ref[...]
        cells = cells.reshape(classes * group * cols, channels)
        partial = jnp.dot(cells, points[k][0], preferred_element_type=F32)
        split = partial.reshape(classes * group * 2, 2, cols // 4, partial.shape[-1])
        first = place[0] % 2 == 0
        keep = jnp.where(first, split[:, 0], split[:, 1])
        send = jnp.where(first, split[:, 1], split[:, 0])
        keeps[k][0] = keep.reshape(keeps[k].shape[1:])
        sends[k][0] = send.reshape(sends[k].shape[1:]).astype(BF16)


def forward(branches, folded, place, after, x, arrived, taps, point):
    classes, residues, cols, channels = x.shape
    filters = point.shape[2]
    group = residues // STEPS
    cell = (classes, group, cols, channels)
    part = (1, classes, group, 2, cols // 4, filters)
    part_shape = (1, classes, residues, 2, cols // 4, filters)
    outs = [(shape_of(part_shape, F32), part, 2) for _ in branches]
    outs += [(shape_of(part_shape, BF16), part, 2) for _ in branches]
    outs += [(pltpu.HBM(x.shape, BF16), cell, 1) for b in branches if b]
    if not branches[0]:
        outs += [(shape_of(x.shape[1:], BF16), (group, cols, channels), 0)]
    return call(
        functools.partial(forward_kernel, branches, folded), place, STEPS, after,
        [
            (x, cell, 1),
            (arrived, (group, cols, channels) if folded else (1, 1, 8, 128), 0 if folded else None),
            (taps, taps.shape, None),
        ]
        + [(point, (1, channels, filters), (b, 0, 0)) for b in branches],
        outs, "forward_" + "_".join(map(str, branches)),
    )


def near_kernel(place, keep_ref, arrived_ref, near_ref):
    near_ref[...] = (keep_ref[...] + arrived_ref[...].astype(F32)).astype(BF16)


def near_sum(name, place, after, keep, arrived):
    return call(
        near_kernel, place, 1, after, [(keep, keep.shape, None), (arrived, keep.shape, None)],
        [(shape_of(keep.shape, BF16), keep.shape, None)], f"near_{name}",
    )


def near_cot_kernel(place, keep_ref, arrived_ref, cot_ref, near_ref):
    near_ref[:, :, :, :2] = (keep_ref[...] + arrived_ref[...].astype(F32)).astype(BF16)
    near_ref[0, :, :, 2] = cot_ref[...].reshape(near_ref.shape[1:3] + near_ref.shape[4:])


def near_sum_cot(name, place, after, keep, arrived, cot):
    shape = keep.shape[:3] + (3,) + keep.shape[4:]
    return call(
        near_cot_kernel, place, 1, after,
        [(keep, keep.shape, None), (arrived, keep.shape, None), (cot, cot.shape, None)],
        [(shape_of(shape, BF16), shape, None)], f"near_{name}",
    )


def gate_kernel(branch, folded, first_gate, place, near_ref, far_ref, *refs):
    cot_ref = None
    if not first_gate:
        cot_ref, refs = refs[0], refs[1:]
    _, classes, residues, sides, width, filters = near_ref.shape
    if folded:
        arrived_ref, refs = refs[0], refs[1:]
    n, sides = residues, 2
    low_side = place[0] // 2 == 0
    if cot_ref is None:
        cots_ref, cots_leaving_ref, *refs = refs[-2:] + refs[:-2]
        own = near_ref[0, :, :, 2].reshape(classes * n, width, filters)
        far = far_ref[0, :, :, 2].reshape(classes * n, width, filters)
        cots_ref[:, 0] = jnp.where(low_side, own, far)
        cots_ref[:, 1] = jnp.where(low_side, far, own)
        cots_leaving_ref[...] = cots_ref[n : 2 * n]
        cot_ref = cots_ref
    paired = len(refs) > 5
    if paired:
        proj_ref, mixed_ref, earlier_ref, grad_ref, out_ref, keep_ref, send_ref, *leaving = refs
    else:
        proj_ref, mixed_ref, grad_ref, out_ref, proj_grad_ref = refs
    cots = cot_ref[...]
    if folded:
        cots = jnp.concatenate(
            class_rows(place[1] == 0, cots[:n], cots[2 * n : 3 * n], arrived_ref[...])
        )
    cells = cots.reshape(-1, filters)
    shape = (classes * residues, sides, width, filters)
    proj = proj_ref[0]
    act_grad = lax.dot_general(cells, proj, (((1,), (1,)), ((), ())), preferred_element_type=F32)
    preact = (near_ref[0, :, :, :2].astype(F32) + far_ref[0, :, :, :2].astype(F32)).reshape(shape)
    logistic = 1.0 / (1.0 + jnp.exp(-preact))
    grad = act_grad.reshape(shape) * logistic * (1.0 + preact * (1.0 - logistic))
    grad_ref[0] = grad.astype(BF16).reshape(grad_ref.shape[1:])
    active = (preact * logistic).astype(BF16)
    mine = jnp.where(low_side, active[:, 0], active[:, 1]).reshape(-1, filters)
    mixed = mixed_ref[...] + jnp.dot(mine, proj, preferred_element_type=F32).reshape(out_ref.shape)
    out_ref[...] = mixed
    proj_grad = lax.dot_general(
        active.reshape(-1, filters), cells, (((0,), (0,)), ((), ())), preferred_element_type=F32
    )
    if not paired:
        proj_grad_ref[...] = proj_grad
        return
    first = place[2] == 0
    keep_ref[...] = jnp.where(first, earlier_ref[...], proj_grad)
    send_ref[...] = jnp.where(first, proj_grad, earlier_ref[...]).astype(BF16)
    if leaving:
        leaving[0][...] = jnp.where(place[1] == 0, mixed[2 * n :], mixed[:n]).astype(BF16)


def gate(branch, folded, place, after, near, far, cots, arrived, proj, mixed, earlier=None, leaves=False):
    filters = proj.shape[-1]
    first_gate = cots is None
    arrays = [near, far] + ([] if first_gate else [cots]) + ([arrived] if folded else [])
    ins = [(a, a.shape, None) for a in arrays] + [(proj, (1, filters, filters), (branch, 0, 0))]
    ins += [(a, a.shape, None) for a in ([mixed] if earlier is None else [mixed, earlier])]
    part = (filters, filters)
    shapes = [(near.shape[:3] + (2,) + near.shape[4:], BF16), (mixed.shape, F32), (part, F32)]
    if earlier is not None:
        shapes.append((part, BF16))
    if first_gate:
        shapes.append(((mixed.shape[0], 2) + mixed.shape[1:], BF16))
        shapes.append(((mixed.shape[0] // 3, 2) + mixed.shape[1:], BF16))
    if leaves:
        shapes.append(((mixed.shape[0] // 3,) + mixed.shape[1:], BF16))
    return call(
        functools.partial(gate_kernel, branch, folded, first_gate), place, 1, after, ins,
        [(shape_of(shape, kind), shape, None) for shape, kind in shapes], f"gate_{branch}",
    )


def whole_columns(place, own, other):
    thin = (-1,) + own.shape[-2:]
    own, other = own.reshape(thin), other.reshape(thin)
    first = place[0] % 2 == 0
    low = jnp.where(first, own, other)
    high = jnp.where(first, other, own)
    both = jnp.concatenate([low[:, None], high[:, None]], axis=1)
    return both.reshape(-1, own.shape[-1])


def split_by_core(place, low, high, keep_ref, send_ref):
    first = place[2] == 0
    rows = low.shape[0]
    keep_ref[:rows] = jnp.where(first, low, high)
    send_ref[:rows] = jnp.where(first, high, low).astype(send_ref.dtype)


def backward_kernel(
    branch, folded, final, chained, place, own_ref, other_ref, x_ref, arrived_ref, spread_ref, taps_ref,
    point_ref, before_ref, *refs
):
    classes, group, cols, channels = x_ref.shape
    point_grad_ref, depth_ref, grads_ref = refs[-3:]
    refs = refs[:-3]
    if chained:
        mixed_ref, refs = refs[0], refs[1:]
    upper = place[1] == 0
    pre = whole_columns(place, own_ref[0], other_ref[0])
    grads = lax.dot_general(pre, point_ref[0], (((1,), (1,)), ((), ())), preferred_element_type=F32)
    grads_ref[...] = grads.astype(BF16).reshape(grads_ref.shape)
    cells = spread_ref[...].reshape(classes * group * cols, channels)
    product = lax.dot_general(cells, pre, (((0,), (0,)), ((), ())), preferred_element_type=F32)

    @pl.when(pl.program_id(0) == 0)
    def _():
        point_grad_ref[...] = product
        depth_ref[...] = jnp.zeros_like(depth_ref)

    @pl.when(pl.program_id(0) > 0)
    def _():
        point_grad_ref[...] += product

    outs = refs[2:] if chained else refs
    pairs = row_pairs(branch, classes)

    def residue(r, carry):
        rows = [x_ref[q, r].astype(F32) for q in range(classes)]
        if folded:
            rows = class_rows(upper, rows[0], rows[2], arrived_ref[r].astype(F32))
        grads = [grads_ref[q, r].astype(F32) for q in range(classes)]
        for j in range(3):
            near = [moved(row, (j - 1) * branch * BASE_DILATION) for row in rows]
            for i in range(3):
                part = None
                for q, tap, source in pairs:
                    if tap == i:
                        term = (near[source] * grads[q]).reshape(cols // 8, 8, channels).sum(axis=0)
                        part = term if part is None else part + term
                if part is not None:
                    depth_ref[i * 3 + j] += part
        totals = []
        for target in range(classes):
            total = before_ref[target, r] if chained else None
            for j in range(3):
                part = None
                for q, i, source in pairs:
                    if source == target:
                        term = grads[q] * taps_ref[branch - 1, i, j].astype(F32)[None, :]
                        part = term if part is None else part + term
                part = moved(part, -(j - 1) * branch * BASE_DILATION)
                total = part if total is None else total + part
            totals.append(total)
        if chained:
            leaving_ref, stay_ref = outs[:2]
            leaving_ref[r, :cols] = jnp.where(upper, totals[2], totals[0]).astype(BF16)
            leaving_ref[r, cols:, : mixed_ref.shape[2]] = mixed_ref[r]
            stay_ref[0, r] = jnp.where(upper, totals[0], totals[1])
            stay_ref[1, r] = jnp.where(upper, totals[1], totals[2])
        else:
            for q in range(classes):
                outs[0][q, r] = totals[q]
        return carry

    lax.fori_loop(0, group, residue, 0)

    @pl.when(pl.program_id(0) == STEPS - 1)
    def _():
        depth = depth_ref[...].sum(axis=1)
        if final:
            keep_ref, send_ref = outs[-2:]
            half, filters = channels // 2, point_grad_ref.shape[1]
            split_by_core(place, point_grad_ref[:half], point_grad_ref[half:], keep_ref, send_ref)
            if chained:
                depths = jnp.concatenate([refs[0][...], depth, refs[1][...]])
                low, high = depths[:, :filters], depths[:, filters:]
                first = place[2] == 0
                keep_ref[half : half + 27] = jnp.where(first, low, high)
                send_ref[half : half + 27] = jnp.where(first, high, low).astype(BF16)
                blank = jnp.zeros((keep_ref.shape[0] - half - 27, filters), F32)
                keep_ref[half + 27 :] = blank
                send_ref[half + 27 :] = blank.astype(BF16)
            else:
                outs[-3][...] = depth
        else:
            outs[-2][...] = point_grad_ref[...]
            outs[-1][...] = depth


def backward(
    branch, folded, final, place, after, own, other, x, arrived, spread, taps, point, before=None, depths=(),
    mixed=None
):
    classes, residues, cols, channels = x.shape
    filters = point.shape[2]
    group = residues // STEPS
    part = (1, classes, group, 2, cols // 4, filters)
    cell = (classes, group, cols, channels)
    thin = (group, cols, channels)
    chained = before is not None
    if chained:
        outs = [
            (shape_of((residues, cols + cols // 4, channels), BF16), (group, cols + cols // 4, channels), 0),
            (pltpu.HBM((2,) + x.shape[1:], F32), (2,) + thin, 1),
        ]
    else:
        outs = [(pltpu.HBM(x.shape, F32), cell, 1)]
    halves = (channels // 2 + (32 if chained else 0), filters)
    shapes = [(channels, filters), (9, channels)]
    if final:
        shapes = [halves, halves] if chained else [(9, channels), halves, halves]
    outs += [(shape_of(shape, F32), shape, None) for shape in shapes]
    if final:
        outs[-1] = (shape_of(halves, BF16), halves, None)
    small = (1, 1, 8, 128)
    return call(
        functools.partial(backward_kernel, branch, folded, final, chained), place, STEPS, after,
        [
            (own, part, 2),
            (other, part, 2),
            (x, cell, 1),
            (arrived, thin, 0) if folded else (x, small, None),
            (spread, cell, 1),
            (taps, taps.shape, None),
            (point, (1, channels, filters), (branch, 0, 0)),
            (before, cell, 1) if chained else (x, small, None),
        ]
        + ([(mixed, (group,) + mixed.shape[1:], 0)] if chained else [])
        + [(d, d.shape, None) for d in depths],
        outs, f"backward_{branch}",
        scratch=[
            pltpu.VMEM((channels, filters), F32),
            pltpu.VMEM((9, 8, channels), F32),
            pltpu.VMEM(cell, BF16),
        ],
    )


def join_kernel(place, own_ref, other_ref, x_ref, earlier_ref, pre_ref, keep_ref, send_ref, total_ref):
    pre = whole_columns(place, own_ref[0], other_ref[0])
    pre_ref[...] = pre.reshape(pre_ref.shape)
    cells = x_ref[...].reshape(-1, x_ref.shape[-1])
    product = lax.dot_general(cells, pre, (((0,), (0,)), ((), ())), preferred_element_type=F32)

    @pl.when(pl.program_id(0) == 0)
    def _():
        total_ref[...] = product

    @pl.when(pl.program_id(0) > 0)
    def _():
        total_ref[...] += product

    @pl.when(pl.program_id(0) == STEPS - 1)
    def _():
        split_by_core(place, earlier_ref[...], total_ref[...], keep_ref, send_ref)


def join(place, after, own, other, x, earlier):
    classes, residues, cols, channels = x.shape
    filters = own.shape[-1]
    group = residues // STEPS
    part = (1, classes, group, 2, cols // 4, filters)
    return call(
        join_kernel, place, STEPS, after,
        [
            (own, part, 2),
            (other, part, 2),
            (x, (classes, group, cols, channels), 1),
            (earlier, earlier.shape, None),
        ],
        [
            (shape_of((classes, residues, cols, filters), BF16), (classes, group, cols, filters), 1),
            (shape_of(earlier.shape, F32), earlier.shape, None),
            (shape_of(earlier.shape, BF16), earlier.shape, None),
        ],
        "join", scratch=[pltpu.VMEM(earlier.shape, F32)],
    )


def last_kernel(
    place, pre_ref, point_ref, band_ref, stay_ref, arrived_ref, mixed_ref, folded_ref, input_ref, output_ref
):
    classes, group, cols, channels = band_ref.shape
    pre = pre_ref[...].reshape(classes * group * cols, -1)
    grads = lax.dot_general(pre, point_ref[0], (((1,), (1,)), ((), ())), preferred_element_type=F32)
    grads = grads.astype(BF16).astype(F32).reshape(band_ref.shape)
    others = (stay_ref[0], arrived_ref[:, :cols].astype(F32), stay_ref[1])
    for q in range(classes):
        input_ref[q] = (grads[q] + band_ref[q] + others[q]).astype(BF16)
    upper = place[1] == 0
    mixed = (
        jnp.where(upper, folded_ref[0], folded_ref[1]),
        arrived_ref[:, cols:, : mixed_ref.shape[-1]].astype(F32),
        jnp.where(upper, folded_ref[1], folded_ref[2]),
    )
    for q in range(classes):
        output_ref[q] = (mixed_ref[q] + mixed[q]).astype(BF16)


def last(place, after, pre, point, band, stay, arrived, mixed, folded):
    classes, residues, cols, channels = band.shape
    filters = point.shape[2]
    group = residues // STEPS
    cell = (classes, group, cols, channels)
    thin = (classes, group) + mixed.shape[2:]
    return call(
        last_kernel, place, STEPS, after,
        [
            (pre, (classes, group, cols, filters), 1),
            (point, (1, channels, filters), (0, 0, 0)),
            (band, cell, 1),
            (stay, (2, group, cols, channels), 1),
            (arrived, (group,) + arrived.shape[1:], 0),
            (mixed, thin, 1),
            (folded, thin, 1),
        ],
        [(result_of(band.shape, BF16), cell, 1), (result_of(mixed.shape, BF16), thin, 1)], "last",
    )


def add_kernel(scale, counts, place, *refs):
    terms, out_ref = refs[: sum(counts)], refs[-1]
    at = 0
    for count in counts:
        group, terms = terms[:count], terms[count:]
        values = [ref[...].astype(F32) for ref in group]
        total = sum(values[1:], values[0])
        if scale != 1.0:
            total = total * scale
        rows = group[0].shape[0]
        out_ref[at : at + rows] = total.astype(out_ref.dtype)
        at += rows


def add(name, place, after, groups, kind, scale=1.0, arrived=()):
    shape = (sum(group[0].shape[0] for group in groups), groups[0][0].shape[1])
    counts = [len(group) for group in groups]
    return call(
        functools.partial(add_kernel, scale, counts), place, 1, after,
        [(a, a.shape, None) for group in groups for a in group]
        + [(a, (1,) * (len(a.shape) - 2) + a.shape[-2:], None) for a in arrived],
        [(shape_of(shape, kind), shape, None)], name,
    )


def finish_kernel(place, own30, far30, own_proj, far_proj, own21, far21, proj_ref, depth_ref, point_ref):
    core = place[2] == 0

    def halves(own, far, first, count):
        own, far = own[first : first + count], far[first : first + count]
        return jnp.where(core, own, far), jnp.where(core, far, own)

    channels = point_ref.shape[1]
    filters = proj_ref.shape[1]
    half = channels // 2
    point_ref[3], point_ref[0] = halves(own30, far30, 0, channels)
    proj_ref[3], proj_ref[0] = halves(own_proj, far_proj, 0, filters)
    proj_ref[1], proj_ref[2] = halves(own_proj, far_proj, filters, filters)
    point_ref[2, :half], point_ref[2, half:] = halves(own21, far21, 0, half)
    low, high = halves(own21, far21, half, 27)
    for k in range(9):
        rows = slice(3 * k, 3 * k + 3)
        depth_ref[k // 3, k % 3, :, :filters] = low[rows]
        depth_ref[k // 3, k % 3, :, filters:] = high[rows]
    first = own21.shape[0] - half
    point_ref[1, :half], point_ref[1, half:] = halves(own21, far21, first, half)


def finish(place, after, early, proj, late, channels, filters):
    arrays = [*early, *proj, *late]
    shapes = [(4, filters, filters), (3, 3, 3, channels), (4, channels, filters)]
    return call(
        finish_kernel, place, 1, after, [(a, a.shape, None) for a in arrays],
        [(result_of(s, F32), s, None) for s in shapes], "finish",
    )


def by_classes(features_in, depth_weights, point_weights, proj_weights, cotangent):
    _, band_rows, cols, channels = features_in.shape
    filters = point_weights.shape[2]
    classes, n = 3, band_rows // 3
    scale = 1.0 / math.sqrt(lax.axis_size("dp") * band_rows * lax.axis_size("row") * cols)
    chan, row = lax.axis_index("chan"), lax.axis_index("row")
    core = lax.axis_index("dp") % 2
    place = jnp.stack([chan, row, core]).astype(jnp.int32)
    x = features_in[0].reshape(classes, n, cols, channels)

    weights = (depth_weights, point_weights)
    cot = cotangent[0]

    token, blank = jnp.zeros(TOKEN, F32), jnp.zeros(cot.shape, F32)
    keep3, send3, spread3, token = forward(
        (3,), False, place, token, in_hbm(x), x, in_hbm(depth_weights), in_hbm(point_weights)
    )
    sent3 = swap(send3, "chan", 1)
    keep0, send0, x_leaving, token = forward(
        (0,), False, place, token, x, x, in_hbm(depth_weights), in_hbm(point_weights)
    )
    sent0 = swap(send0, "chan", 1)
    arrived = swap(x_leaving, "row", 1)
    near3, token = near_sum_cot("3", place, token, keep3, sent3, cot)
    far3 = swap(near3, "chan", 2)
    keep1, keep2, send1, send2, spread1, spread2, token = forward(
        (1, 2), True, place, token, x, arrived, *weights
    )
    sent1, sent2 = swap(send1, "chan", 1), swap(send2, "chan", 1)
    near0, token = near_sum("0", place, token, keep0, sent0)
    far0 = swap(near0, "chan", 2)
    grad3, band_mixed, proj3, cots, cots_leaving, token = gate(
        3, False, place, token, near3, far3, None, None, proj_weights, blank
    )
    other3 = swap(grad3, "chan", 1)
    cots_arrived = swap(cots_leaving, "row", 1)
    near1, token = near_sum("1", place, token, keep1, sent1)
    far1 = swap(near1, "chan", 2)
    grad0, band_mixed, proj_keep, proj_send, token = gate(
        0, False, place, token, near0, far0, cots, None, proj_weights, band_mixed, proj3
    )
    other0 = swap(grad0, "chan", 1)
    proj30 = (proj_keep, swap(proj_send, "dp", 1))
    near2, token = near_sum("2", place, token, keep2, sent2)
    far2 = swap(near2, "chan", 2)
    grad1, class_mixed, proj1, token = gate(
        1, True, place, token, near1, far1, cots, cots_arrived, proj_weights, blank
    )
    other1 = swap(grad1, "chan", 1)
    band, point3, depth3, token = backward(
        3, False, False, place, token, grad3, other3, x, x, spread3, *weights
    )
    pre0, point_keep, point_send, token = join(place, token, grad0, other0, x, point3)
    point30 = (point_keep, swap(point_send, "dp", 1))
    grad2, class_mixed, proj_keep, proj_send, mixed_leaving, token = gate(
        2, True, place, token, near2, far2, cots, cots_arrived, proj_weights, class_mixed, proj1,
        leaves=True,
    )
    other2 = swap(grad2, "chan", 1)
    proj12 = (proj_keep, swap(proj_send, "dp", 1))
    total1, depth1, point_keep, point_send, token = backward(
        1, True, True, place, token, grad1, other1, x, arrived, spread1, *weights
    )
    point1 = (point_keep, swap(point_send, "dp", 1))
    proj, token = add("proj", place, token, [proj30, proj12], BF16)
    proj = (proj, swap(proj, "chan", 1))
    early, token = add("early_1", place, token, [point30], BF16)
    early = (early, swap(early, "row", 1))
    leaving, stay, late_keep, late_send, token = backward(
        2, True, True, place, token, grad2, other2, x, arrived, spread2, *weights, before=in_hbm(total1),
        depths=(depth1, depth3), mixed=mixed_leaving,
    )
    input_arrived = swap(leaving, "row", 1)
    late = (late_keep, swap(late_send, "dp", 1))
    proj, token = add("proj_1", place, token, [proj], BF16)
    proj = (proj, swap(proj, "row", 1))
    early, token = add("early_2", place, token, [early], BF16)
    early = (early, swap(early, "dp", 2))
    late, token = add("late_1", place, token, [late, point1], BF16)
    late = (late, swap(late, "dp", 2))
    early, token = add("early", place, token, [early], F32, scale)
    early = (early, swap(early, "dp", 1))
    late, token = add("late_2", place, token, [late], BF16)
    late = (late, swap(late, "row", 1))
    proj, token = add("proj_2", place, token, [proj], BF16)
    proj = (proj, swap(proj, "dp", 2))
    bands = band_mixed.reshape((classes, n) + band_mixed.shape[1:])
    folds = class_mixed.reshape(bands.shape)
    grad_input, output, token = last(
        place, token, pre0, point_weights, in_hbm(band), in_hbm(stay), input_arrived, bands, folds
    )
    proj, token = add("proj_sum", place, token, [proj], F32, scale)
    proj = (proj, swap(proj, "dp", 1))
    late, token = add("late", place, token, [late], F32, scale)
    late = (late, swap(late, "dp", 1))
    grad_proj, grad_depth, grad_point, token = finish(
        place, token, early, proj, late, channels, filters
    )
    return (
        output.reshape(cotangent.shape), grad_input.reshape(features_in.shape), grad_depth, grad_point,
        grad_proj,
    )


def shifted(value, axis, steps):
    count = lax.axis_size(axis)
    first, last = (max(0, -steps), min(count, count - steps))
    return lax.ppermute(value, axis, [(source, source + steps) for source in range(first, last)])


def window(source, top, left, band_rows, band_cols):
    upper = lax.slice_in_dim(source, top, top + band_rows, axis=1)
    return lax.slice_in_dim(upper, left, left + band_cols, axis=2)


def on_device(features_in, depth_weights, point_weights, proj_weights, cotangent):
    samples, band_rows, band_cols, channels = features_in.shape
    weight_scale = 1.0 / math.sqrt(
        samples * lax.axis_size("dp") * band_rows * lax.axis_size("row") * band_cols
    )
    largest_reach = 3 * BASE_DILATION
    offsets = (2, 1, -1, -2)
    arrivals = []
    for offset in offsets:
        arrivals.append(shifted(features_in, "row", offset))
    tall_rows = jnp.concatenate(
        [arrivals[0], arrivals[1], features_in, arrivals[2], arrivals[3]], axis=1
    )
    padded = jnp.pad(tall_rows, ((0, 0), (0, 0), (largest_reach, largest_reach), (0, 0)))
    branch_maps = [features_in]
    for branch_level in range(3):
        tap_spacing = (branch_level + 1) * BASE_DILATION
        summed = jnp.zeros(features_in.shape, jnp.float32)
        for row_tap in range(3):
            for col_tap in range(3):
                input_kernel_tap = window(
                    padded,
                    largest_reach + (row_tap - 1) * tap_spacing,
                    largest_reach + (col_tap - 1) * tap_spacing,
                    band_rows,
                    band_cols,
                )
                summed = summed + input_kernel_tap.astype(jnp.float32) * depth_weights[
                    branch_level, row_tap, col_tap
                ].astype(jnp.float32)
        branch_maps.append(summed.astype(jnp.bfloat16))
    spread = jnp.stack(branch_maps)
    full_point = lax.all_gather(point_weights, "chan", axis=1, tiled=True)
    preact = jnp.einsum(
        "bsrwc,bcf->bsrwf",
        lax.all_to_all(spread, "chan", split_axis=3, concat_axis=4, tiled=True),
        full_point,
        preferred_element_type=jnp.float32,
    )
    activation = jax.nn.silu(preact).astype(jnp.bfloat16)
    output = jnp.einsum(
        "bsrwf,bfg->srwg", activation, proj_weights, preferred_element_type=jnp.float32
    ).astype(jnp.bfloat16)
    silu_gradient = jnp.einsum(
        "srwg,bfg->bsrwf", cotangent, proj_weights, preferred_element_type=jnp.float32
    )
    logistic = jax.nn.sigmoid(preact)
    pre_grad = (silu_gradient * logistic * (1.0 + preact * (1.0 - logistic))).astype(jnp.bfloat16)
    proj_term = jnp.einsum(
        "bsrwf,srwg->bfg", activation, cotangent, preferred_element_type=jnp.float32
    )
    grad_proj = lax.psum(proj_term, ("row", "chan", "dp")) * weight_scale
    incoming = lax.all_gather(pre_grad, "chan", axis=3, tiled=True)
    local_grad = jnp.einsum(
        "bsrwf,bcf->bsrwc", incoming, point_weights, preferred_element_type=jnp.float32
    ).astype(jnp.bfloat16)
    spread_grad = local_grad
    point_sum = jnp.einsum("bsrwc,bsrwf->bcf", spread, incoming, preferred_element_type=jnp.float32)
    spread_grad, point_term = (spread_grad, point_sum)
    depth_rows = []
    for branch_level in range(3):
        tap_spacing = (branch_level + 1) * BASE_DILATION
        branch_grad = spread_grad[branch_level + 1].astype(jnp.float32)
        gathered = []
        for row_tap in range(3):
            for col_tap in range(3):
                input_kernel_tap = window(
                    padded,
                    largest_reach + (row_tap - 1) * tap_spacing,
                    largest_reach + (col_tap - 1) * tap_spacing,
                    band_rows,
                    band_cols,
                )
                gathered.append(
                    jnp.sum(input_kernel_tap.astype(jnp.float32) * branch_grad, axis=(0, 1, 2))
                )
        depth_rows.append(jnp.stack(gathered).reshape(3, 3, channels))
    depth_term = jnp.stack(depth_rows)
    point_summed, depth_summed = lax.psum((point_term, depth_term), ("row", "dp"))
    grad_point = point_summed * weight_scale
    grad_depth = depth_summed * weight_scale
    neighbour_sets = []
    for branch_level in range(3):
        neighbour_sets.append(
            [shifted(spread_grad[branch_level + 1], "row", offset) for offset in offsets]
        )
    grad_in = spread_grad[0].astype(jnp.float32)
    for branch_level in range(3):
        tap_spacing = (branch_level + 1) * BASE_DILATION
        received = neighbour_sets[branch_level]
        grad_tall = jnp.concatenate(
            [received[0], received[1], spread_grad[branch_level + 1], received[2], received[3]],
            axis=1,
        )
        grad_padded = jnp.pad(grad_tall, ((0, 0), (0, 0), (largest_reach, largest_reach), (0, 0)))
        for row_tap in range(3):
            for col_tap in range(3):
                grad_tap = window(
                    grad_padded,
                    largest_reach - (row_tap - 1) * tap_spacing,
                    largest_reach - (col_tap - 1) * tap_spacing,
                    band_rows,
                    band_cols,
                )
                grad_in = grad_in + grad_tap.astype(jnp.float32) * depth_weights[
                    branch_level, row_tap, col_tap
                ].astype(jnp.float32)
    return (output, grad_in.astype(jnp.bfloat16), grad_depth, grad_point, grad_proj)


def folds(mesh, features_in):
    sizes = mesh.shape
    samples, rows, cols, channels = features_in.shape
    return (
        rows == 3 * BASE_DILATION
        and sizes["row"] == 2
        and sizes["chan"] == 4
        and sizes["dp"] == 4
        and samples == sizes["dp"]
        and cols % 64 == 0
        and channels % (128 * sizes["chan"]) == 0
    )


def solution(mesh):
    in_specs = (
        P("dp", "row", None, "chan"),
        P(None, None, None, "chan"),
        P(None, "chan", None),
        P(),
        P("dp", "row", "chan", None),
    )
    out_specs = (
        P("dp", "row", "chan", None),
        P("dp", "row", None, "chan"),
        P(None, None, None, "chan"),
        P(None, "chan", None),
        P(),
    )

    def run(*args):
        body = by_classes if folds(mesh, args[0]) else on_device
        return jax.shard_map(
            body, mesh=mesh, in_specs=in_specs, out_specs=out_specs, check_vma=False
        )(*args)

    return run
```

```python
import functools
import math

import jax
import jax.numpy as jnp
from jax import lax
from jax.experimental import pallas as pl
from jax.experimental.pallas import tpu as pltpu
from jax.sharding import PartitionSpec as P

BASE_DILATION = 12
F32 = jnp.float32
BF16 = jnp.bfloat16
VMEM_BYTES = 28 * 2**20


def swap(value, axis, flip):
    count = lax.axis_size(axis)
    return lax.ppermute(value, axis, [(i, i ^ flip) for i in range(count)])


def moved(value, steps):
    count, width = value.shape
    if steps == 0:
        return 0, value
    far = abs(steps)
    whole, rest = far // 8 * 8, far % 8
    size = count - whole
    if rest == 0:
        return (0, value[whole:]) if steps > 0 else (whole, value[:size])
    blank = jnp.zeros((8, width), value.dtype)
    if steps > 0:
        longer = jnp.concatenate([value[whole:], blank])
        return 0, pltpu.roll(longer, size + 8 - rest, 0)[:size]
    longer = jnp.concatenate([blank, value[:size]])
    return whole, pltpu.roll(longer, rest, 0)[8:]


def add_moved(total, value, steps):
    if steps == 0:
        return value if total is None else total + value
    first, part = moved(value, steps)
    after = first + part.shape[0]
    pieces = [total[first:after] + part]
    if first > 0:
        pieces = [total[:first]] + pieces
    if after < total.shape[0]:
        pieces = pieces + [total[after:]]
    return jnp.concatenate(pieces)


def row_pairs(branch, classes):
    return [
        (q, i, q + (i - 1) * branch)
        for q in range(classes)
        for i in range(3)
        if 0 <= q + (i - 1) * branch < classes
    ]


def class_rows(upper, first, last, arrived):
    return (
        jnp.where(upper, first, arrived),
        jnp.where(upper, last, first),
        jnp.where(upper, arrived, last),
    )


def shape_of(shape, dtype):
    return jax.ShapeDtypeStruct(shape, dtype)


def in_hbm(value):
    return pltpu.with_memory_space_constraint(value, pltpu.HBM)


def result_of(shape, dtype):
    return jax.ShapeDtypeStruct(shape, dtype)


TOKEN = (8, 128)
STEPS = 1


def call(body, place, grid, after, ins, outs, name, scratch=()):
    def spec(block, split):
        dims = len(block)
        if isinstance(split, tuple):
            return pl.BlockSpec(block, lambda r, p: tuple(r if k is None else k for k in split))
        return pl.BlockSpec(block, lambda r, p: tuple(r if k == split else 0 for k in range(dims)))

    def kernel(place_ref, after_ref, *refs):
        last = len(ins) + len(outs) - 2
        body(place_ref, *refs[:last], *refs[last + 1 :])
        refs[last][...] = after_ref[...]

    ins = [(after, TOKEN, None)] + list(ins)
    outs = list(outs) + [(shape_of(TOKEN, F32), TOKEN, None)]
    return pl.pallas_call(
        kernel,
        grid_spec=pltpu.PrefetchScalarGridSpec(
            num_scalar_prefetch=1,
            grid=(grid,),
            in_specs=[spec(block, split) for _, block, split in ins],
            out_specs=[spec(block, split) for _, block, split in outs],
            scratch_shapes=list(scratch),
        ),
        out_shape=[s for s, _, _ in outs],
        compiler_params=pltpu.CompilerParams(vmem_limit_bytes=VMEM_BYTES),
        cost_estimate=pl.CostEstimate(flops=1, bytes_accessed=1, transcendentals=0),
        name=name,
    )(place, *[a for a, _, _ in ins])


def forward_kernel(branches, folded, place, x_ref, arrived_ref, taps_ref, *refs):
    classes, group, cols, channels = x_ref.shape
    count = len(branches)
    points, refs = refs[:count], refs[count:]
    keeps, sends, refs = refs[:count], refs[count : 2 * count], refs[2 * count :]
    spreads = dict(zip([b for b in branches if b], refs))
    if not branches[0]:
        refs[-1][...] = x_ref[1]

    def residue(r, carry):
        rows = [x_ref[q, r].astype(F32) for q in range(classes)]
        if folded:
            rows = class_rows(place[1] == 0, rows[0], rows[2], arrived_ref[r].astype(F32))
        for branch, spread_ref in spreads.items():
            for q in range(classes):
                total = None
                for j in (1, 0, 2):
                    part = None
                    for out, i, source in row_pairs(branch, classes):
                        if out == q:
                            tap = taps_ref[branch - 1, i, j].astype(F32)
                            term = rows[source] * tap[None, :]
                            part = term if part is None else part + term
                    total = add_moved(total, part, (j - 1) * branch * BASE_DILATION)
                spread_ref[q, r] = total.astype(BF16)
        return carry

    lax.fori_loop(0, group, residue, 0)
    for k, branch in enumerate(branches):
        cells = spreads[branch][...] if branch else x_ref[...]
        cells = cells.reshape(classes * group * cols, channels)
        partial = jnp.dot(cells, points[k][0], preferred_element_type=F32)
        split = partial.reshape(classes * group * 2, 2, cols // 4, partial.shape[-1])
        first = place[0] % 2 == 0
        keep = jnp.where(first, split[:, 0], split[:, 1])
        send = jnp.where(first, split[:, 1], split[:, 0])
        keeps[k][0] = keep.reshape(keeps[k].shape[1:])
        sends[k][0] = send.reshape(sends[k].shape[1:]).astype(BF16)


def forward(branches, folded, place, after, x, arrived, taps, point):
    classes, residues, cols, channels = x.shape
    filters = point.shape[2]
    group = residues // STEPS
    cell = (classes, group, cols, channels)
    part = (1, classes, group, 2, cols // 4, filters)
    part_shape = (1, classes, residues, 2, cols // 4, filters)
    outs = [(shape_of(part_shape, F32), part, 2) for _ in branches]
    outs += [(shape_of(part_shape, BF16), part, 2) for _ in branches]
    outs += [(shape_of(x.shape, BF16), cell, 1) for b in branches if b]
    if not branches[0]:
        outs += [(shape_of(x.shape[1:], BF16), (group, cols, channels), 0)]
    return call(
        functools.partial(forward_kernel, branches, folded), place, STEPS, after,
        [
            (x, cell, 1),
            (arrived, (group, cols, channels) if folded else (1, 1, 8, 128), 0 if folded else None),
            (taps, taps.shape, None),
        ]
        + [(point, (1, channels, filters), (b, 0, 0)) for b in branches],
        outs, "forward_" + "_".join(map(str, branches)),
    )


def near_kernel(place, keep_ref, arrived_ref, near_ref):
    near_ref[...] = (keep_ref[...] + arrived_ref[...].astype(F32)).astype(BF16)


def near_sum(name, place, after, keep, arrived):
    return call(
        near_kernel, place, 1, after, [(keep, keep.shape, None), (arrived, keep.shape, None)],
        [(shape_of(keep.shape, BF16), keep.shape, None)], f"near_{name}",
    )


def near_cot_kernel(place, keep_ref, arrived_ref, cot_ref, near_ref):
    near_ref[:, :, :, :2] = (keep_ref[...] + arrived_ref[...].astype(F32)).astype(BF16)
    near_ref[0, :, :, 2] = cot_ref[...].reshape(near_ref.shape[1:3] + near_ref.shape[4:])


def near_sum_cot(name, place, after, keep, arrived, cot):
    shape = keep.shape[:3] + (3,) + keep.shape[4:]
    return call(
        near_cot_kernel, place, 1, after,
        [(keep, keep.shape, None), (arrived, keep.shape, None), (cot, cot.shape, None)],
        [(shape_of(shape, BF16), shape, None)], f"near_{name}",
    )


def gate_kernel(branch, folded, first_gate, place, near_ref, far_ref, *refs):
    cot_ref = None
    if not first_gate:
        cot_ref, refs = refs[0], refs[1:]
    _, classes, residues, sides, width, filters = near_ref.shape
    if folded:
        arrived_ref, refs = refs[0], refs[1:]
    n, sides = residues, 2
    low_side = place[0] // 2 == 0
    if cot_ref is None:
        cots_ref, cots_leaving_ref, *refs = refs[-2:] + refs[:-2]
        own = near_ref[0, :, :, 2].reshape(classes * n, width, filters)
        far = far_ref[0, :, :, 2].reshape(classes * n, width, filters)
        cots_ref[:, 0] = jnp.where(low_side, own, far)
        cots_ref[:, 1] = jnp.where(low_side, far, own)
        cots_leaving_ref[...] = cots_ref[n : 2 * n]
        cot_ref = cots_ref
    paired = len(refs) > 5
    if paired:
        proj_ref, mixed_ref, earlier_ref, grad_ref, out_ref, keep_ref, send_ref, *leaving = refs
    else:
        proj_ref, mixed_ref, grad_ref, out_ref, proj_grad_ref = refs
    cots = cot_ref[...]
    if folded:
        cots = jnp.concatenate(
            class_rows(place[1] == 0, cots[:n], cots[2 * n : 3 * n], arrived_ref[...])
        )
    cells = cots.reshape(-1, filters)
    shape = (classes * residues, sides, width, filters)
    proj = proj_ref[0]
    act_grad = lax.dot_general(cells, proj, (((1,), (1,)), ((), ())), preferred_element_type=F32)
    preact = (near_ref[0, :, :, :2].astype(F32) + far_ref[0, :, :, :2].astype(F32)).reshape(shape)
    logistic = 1.0 / (1.0 + jnp.exp(-preact))
    grad = act_grad.reshape(shape) * logistic * (1.0 + preact * (1.0 - logistic))
    grad_ref[0] = grad.astype(BF16).reshape(grad_ref.shape[1:])
    active = (preact * logistic).astype(BF16)
    mine = jnp.where(low_side, active[:, 0], active[:, 1]).reshape(-1, filters)
    mixed = mixed_ref[...] + jnp.dot(mine, proj, preferred_element_type=F32).reshape(out_ref.shape)
    out_ref[...] = mixed
    proj_grad = lax.dot_general(
        active.reshape(-1, filters), cells, (((0,), (0,)), ((), ())), preferred_element_type=F32
    )
    if not paired:
        proj_grad_ref[...] = proj_grad
        return
    first = place[2] == 0
    keep_ref[...] = jnp.where(first, earlier_ref[...], proj_grad)
    send_ref[...] = jnp.where(first, proj_grad, earlier_ref[...]).astype(BF16)
    if leaving:
        leaving[0][...] = jnp.where(place[1] == 0, mixed[2 * n :], mixed[:n]).astype(BF16)


def gate(branch, folded, place, after, near, far, cots, arrived, proj, mixed, earlier=None, leaves=False):
    filters = proj.shape[-1]
    first_gate = cots is None
    arrays = [near, far] + ([] if first_gate else [cots]) + ([arrived] if folded else [])
    ins = [(a, a.shape, None) for a in arrays] + [(proj, (1, filters, filters), (branch, 0, 0))]
    ins += [(a, a.shape, None) for a in ([mixed] if earlier is None else [mixed, earlier])]
    part = (filters, filters)
    shapes = [(near.shape[:3] + (2,) + near.shape[4:], BF16), (mixed.shape, F32), (part, F32)]
    if earlier is not None:
        shapes.append((part, BF16))
    if first_gate:
        shapes.append(((mixed.shape[0], 2) + mixed.shape[1:], BF16))
        shapes.append(((mixed.shape[0] // 3, 2) + mixed.shape[1:], BF16))
    if leaves:
        shapes.append(((mixed.shape[0] // 3,) + mixed.shape[1:], BF16))
    return call(
        functools.partial(gate_kernel, branch, folded, first_gate), place, 1, after, ins,
        [(shape_of(shape, kind), shape, None) for shape, kind in shapes], f"gate_{branch}",
    )


def whole_columns(place, own, other):
    thin = (-1,) + own.shape[-2:]
    own, other = own.reshape(thin), other.reshape(thin)
    first = place[0] % 2 == 0
    low = jnp.where(first, own, other)
    high = jnp.where(first, other, own)
    both = jnp.concatenate([low[:, None], high[:, None]], axis=1)
    return both.reshape(-1, own.shape[-1])


def split_by_core(place, low, high, keep_ref, send_ref):
    first = place[2] == 0
    rows = low.shape[0]
    keep_ref[:rows] = jnp.where(first, low, high)
    send_ref[:rows] = jnp.where(first, high, low).astype(send_ref.dtype)


def backward_kernel(
    branch, folded, final, chained, place, own_ref, other_ref, x_ref, arrived_ref, spread_ref, taps_ref,
    point_ref, before_ref, *refs
):
    classes, group, cols, channels = x_ref.shape
    point_grad_ref, depth_ref, grads_ref = refs[-3:]
    refs = refs[:-3]
    if chained:
        mixed_ref, refs = refs[0], refs[1:]
    upper = place[1] == 0
    pre = whole_columns(place, own_ref[0], other_ref[0])
    grads = lax.dot_general(pre, point_ref[0], (((1,), (1,)), ((), ())), preferred_element_type=F32)
    grads_ref[...] = grads.astype(BF16).reshape(grads_ref.shape)
    cells = spread_ref[...].reshape(classes * group * cols, channels)
    product = lax.dot_general(cells, pre, (((0,), (0,)), ((), ())), preferred_element_type=F32)

    @pl.when(pl.program_id(0) == 0)
    def _():
        point_grad_ref[...] = product
        depth_ref[...] = jnp.zeros_like(depth_ref)

    @pl.when(pl.program_id(0) > 0)
    def _():
        point_grad_ref[...] += product

    outs = refs[2:] if chained else refs
    pairs = row_pairs(branch, classes)

    def residue(r, carry):
        rows = [x_ref[q, r].astype(F32) for q in range(classes)]
        if folded:
            rows = class_rows(upper, rows[0], rows[2], arrived_ref[r].astype(F32))
        grads = [grads_ref[q, r].astype(F32) for q in range(classes)]
        for j in range(3):
            shifts = [moved(row, (j - 1) * branch * BASE_DILATION) for row in rows]
            first, near = shifts[0][0], [part for _, part in shifts]
            size = near[0].shape[0]
            for i in range(3):
                part = None
                for q, tap, source in pairs:
                    if tap == i:
                        term = near[source] * grads[q][first : first + size]
                        term = term.reshape(size // 8, 8, channels).sum(axis=0)
                        part = term if part is None else part + term
                if part is not None:
                    depth_ref[i * 3 + j] += part
        totals = []
        for target in range(classes):
            total = before_ref[target, r] if chained else None
            for j in (1, 0, 2):
                part = None
                for q, i, source in pairs:
                    if source == target:
                        term = grads[q] * taps_ref[branch - 1, i, j].astype(F32)[None, :]
                        part = term if part is None else part + term
                total = add_moved(total, part, -(j - 1) * branch * BASE_DILATION)
            totals.append(total)
        if chained:
            leaving_ref, stay_ref = outs[:2]
            leaving_ref[r, :cols] = jnp.where(upper, totals[2], totals[0]).astype(BF16)
            leaving_ref[r, cols:, : mixed_ref.shape[2]] = mixed_ref[r]
            stay_ref[0, r] = jnp.where(upper, totals[0], totals[1])
            stay_ref[1, r] = jnp.where(upper, totals[1], totals[2])
        else:
            for q in range(classes):
                outs[0][q, r] = totals[q]
        return carry

    lax.fori_loop(0, group, residue, 0)

    @pl.when(pl.program_id(0) == STEPS - 1)
    def _():
        depth = depth_ref[...].sum(axis=1)
        if final:
            keep_ref, send_ref = outs[-2:]
            half, filters = channels // 2, point_grad_ref.shape[1]
            split_by_core(place, point_grad_ref[:half], point_grad_ref[half:], keep_ref, send_ref)
            if chained:
                depths = jnp.concatenate([refs[0][...], depth, refs[1][...]])
                low, high = depths[:, :filters], depths[:, filters:]
                first = place[2] == 0
                keep_ref[half : half + 27] = jnp.where(first, low, high)
                send_ref[half : half + 27] = jnp.where(first, high, low).astype(BF16)
                blank = jnp.zeros((keep_ref.shape[0] - half - 27, filters), F32)
                keep_ref[half + 27 :] = blank
                send_ref[half + 27 :] = blank.astype(BF16)
            else:
                outs[-3][...] = depth
        else:
            outs[-2][...] = point_grad_ref[...]
            outs[-1][...] = depth


def backward(
    branch, folded, final, place, after, own, other, x, arrived, spread, taps, point, before=None, depths=(),
    mixed=None
):
    classes, residues, cols, channels = x.shape
    filters = point.shape[2]
    group = residues // STEPS
    part = (1, classes, group, 2, cols // 4, filters)
    cell = (classes, group, cols, channels)
    thin = (group, cols, channels)
    chained = before is not None
    if chained:
        outs = [
            (shape_of((residues, cols + cols // 4, channels), BF16), (group, cols + cols // 4, channels), 0),
            (shape_of((2,) + x.shape[1:], F32), (2,) + thin, 1),
        ]
    else:
        outs = [(shape_of(x.shape, F32), cell, 1)]
    halves = (channels // 2 + (32 if chained else 0), filters)
    shapes = [(channels, filters), (9, channels)]
    if final:
        shapes = [halves, halves] if chained else [(9, channels), halves, halves]
    outs += [(shape_of(shape, F32), shape, None) for shape in shapes]
    if final:
        outs[-1] = (shape_of(halves, BF16), halves, None)
    small = (1, 1, 8, 128)
    return call(
        functools.partial(backward_kernel, branch, folded, final, chained), place, STEPS, after,
        [
            (own, part, 2),
            (other, part, 2),
            (x, cell, 1),
            (arrived, thin, 0) if folded else (x, small, None),
            (spread, cell, 1),
            (taps, taps.shape, None),
            (point, (1, channels, filters), (branch, 0, 0)),
            (before, cell, 1) if chained else (x, small, None),
        ]
        + ([(mixed, (group,) + mixed.shape[1:], 0)] if chained else [])
        + [(d, d.shape, None) for d in depths],
        outs, f"backward_{branch}",
        scratch=[
            pltpu.VMEM((channels, filters), F32),
            pltpu.VMEM((9, 8, channels), F32),
            pltpu.VMEM(cell, BF16),
        ],
    )


def join_kernel(place, own_ref, other_ref, x_ref, earlier_ref, pre_ref, keep_ref, send_ref, total_ref):
    pre = whole_columns(place, own_ref[0], other_ref[0])
    pre_ref[...] = pre.reshape(pre_ref.shape)
    cells = x_ref[...].reshape(-1, x_ref.shape[-1])
    product = lax.dot_general(cells, pre, (((0,), (0,)), ((), ())), preferred_element_type=F32)

    @pl.when(pl.program_id(0) == 0)
    def _():
        total_ref[...] = product

    @pl.when(pl.program_id(0) > 0)
    def _():
        total_ref[...] += product

    @pl.when(pl.program_id(0) == STEPS - 1)
    def _():
        split_by_core(place, earlier_ref[...], total_ref[...], keep_ref, send_ref)


def join(place, after, own, other, x, earlier):
    classes, residues, cols, channels = x.shape
    filters = own.shape[-1]
    group = residues // STEPS
    part = (1, classes, group, 2, cols // 4, filters)
    return call(
        join_kernel, place, STEPS, after,
        [
            (own, part, 2),
            (other, part, 2),
            (x, (classes, group, cols, channels), 1),
            (earlier, earlier.shape, None),
        ],
        [
            (shape_of((classes, residues, cols, filters), BF16), (classes, group, cols, filters), 1),
            (shape_of(earlier.shape, F32), earlier.shape, None),
            (shape_of(earlier.shape, BF16), earlier.shape, None),
        ],
        "join", scratch=[pltpu.VMEM(earlier.shape, F32)],
    )


def last_kernel(
    place, pre_ref, point_ref, band_ref, stay_ref, arrived_ref, mixed_ref, folded_ref, input_ref, output_ref
):
    classes, group, cols, channels = band_ref.shape
    pre = pre_ref[...].reshape(classes * group * cols, -1)
    grads = lax.dot_general(pre, point_ref[0], (((1,), (1,)), ((), ())), preferred_element_type=F32)
    grads = grads.astype(BF16).astype(F32).reshape(band_ref.shape)
    others = (stay_ref[0], arrived_ref[:, :cols].astype(F32), stay_ref[1])
    for q in range(classes):
        input_ref[q] = (grads[q] + band_ref[q] + others[q]).astype(BF16)
    upper = place[1] == 0
    mixed = (
        jnp.where(upper, folded_ref[0], folded_ref[1]),
        arrived_ref[:, cols:, : mixed_ref.shape[-1]].astype(F32),
        jnp.where(upper, folded_ref[1], folded_ref[2]),
    )
    for q in range(classes):
        output_ref[q] = (mixed_ref[q] + mixed[q]).astype(BF16)


def last(place, after, pre, point, band, stay, arrived, mixed, folded):
    classes, residues, cols, channels = band.shape
    filters = point.shape[2]
    group = residues // STEPS
    cell = (classes, group, cols, channels)
    thin = (classes, group) + mixed.shape[2:]
    return call(
        last_kernel, place, STEPS, after,
        [
            (pre, (classes, group, cols, filters), 1),
            (point, (1, channels, filters), (0, 0, 0)),
            (band, cell, 1),
            (stay, (2, group, cols, channels), 1),
            (arrived, (group,) + arrived.shape[1:], 0),
            (mixed, thin, 1),
            (folded, thin, 1),
        ],
        [(result_of(band.shape, BF16), cell, 1), (result_of(mixed.shape, BF16), thin, 1)], "last",
    )


def add_kernel(scale, counts, place, *refs):
    terms, out_ref = refs[: sum(counts)], refs[-1]
    at = 0
    for count in counts:
        group, terms = terms[:count], terms[count:]
        values = [ref[...].astype(F32) for ref in group]
        total = sum(values[1:], values[0])
        if scale != 1.0:
            total = total * scale
        rows = group[0].shape[0]
        out_ref[at : at + rows] = total.astype(out_ref.dtype)
        at += rows


def add(name, place, after, groups, kind, scale=1.0, arrived=()):
    shape = (sum(group[0].shape[0] for group in groups), groups[0][0].shape[1])
    counts = [len(group) for group in groups]
    return call(
        functools.partial(add_kernel, scale, counts), place, 1, after,
        [(a, a.shape, None) for group in groups for a in group]
        + [(a, (1,) * (len(a.shape) - 2) + a.shape[-2:], None) for a in arrived],
        [(shape_of(shape, kind), shape, None)], name,
    )


def finish_kernel(place, own30, far30, own_proj, far_proj, own21, far21, proj_ref, depth_ref, point_ref):
    core = place[2] == 0

    def halves(own, far, first, count):
        own, far = own[first : first + count], far[first : first + count]
        return jnp.where(core, own, far), jnp.where(core, far, own)

    channels = point_ref.shape[1]
    filters = proj_ref.shape[1]
    half = channels // 2
    point_ref[3], point_ref[0] = halves(own30, far30, 0, channels)
    proj_ref[3], proj_ref[0] = halves(own_proj, far_proj, 0, filters)
    proj_ref[1], proj_ref[2] = halves(own_proj, far_proj, filters, filters)
    point_ref[2, :half], point_ref[2, half:] = halves(own21, far21, 0, half)
    low, high = halves(own21, far21, half, 27)
    for k in range(9):
        rows = slice(3 * k, 3 * k + 3)
        depth_ref[k // 3, k % 3, :, :filters] = low[rows]
        depth_ref[k // 3, k % 3, :, filters:] = high[rows]
    first = own21.shape[0] - half
    point_ref[1, :half], point_ref[1, half:] = halves(own21, far21, first, half)


def finish(place, after, early, proj, late, channels, filters):
    arrays = [*early, *proj, *late]
    shapes = [(4, filters, filters), (3, 3, 3, channels), (4, channels, filters)]
    return call(
        finish_kernel, place, 1, after, [(a, a.shape, None) for a in arrays],
        [(result_of(s, F32), s, None) for s in shapes], "finish",
    )


def by_classes(features_in, depth_weights, point_weights, proj_weights, cotangent):
    _, band_rows, cols, channels = features_in.shape
    filters = point_weights.shape[2]
    classes, n = 3, band_rows // 3
    scale = 1.0 / math.sqrt(lax.axis_size("dp") * band_rows * lax.axis_size("row") * cols)
    chan, row = lax.axis_index("chan"), lax.axis_index("row")
    core = lax.axis_index("dp") % 2
    place = jnp.stack([chan, row, core]).astype(jnp.int32)
    x = features_in[0].reshape(classes, n, cols, channels)

    weights = (depth_weights, point_weights)
    cot = cotangent[0]

    token, blank = jnp.zeros(TOKEN, F32), jnp.zeros(cot.shape, F32)
    keep3, send3, spread3, token = forward(
        (3,), False, place, token, in_hbm(x), x, in_hbm(depth_weights), in_hbm(point_weights)
    )
    sent3 = swap(send3, "chan", 1)
    keep0, send0, x_leaving, token = forward(
        (0,), False, place, token, x, x, in_hbm(depth_weights), in_hbm(point_weights)
    )
    sent0 = swap(send0, "chan", 1)
    arrived = swap(x_leaving, "row", 1)
    near3, token = near_sum_cot("3", place, token, keep3, sent3, cot)
    far3 = swap(near3, "chan", 2)
    keep1, keep2, send1, send2, spread1, spread2, token = forward(
        (1, 2), True, place, token, x, arrived, *weights
    )
    sent1, sent2 = swap(send1, "chan", 1), swap(send2, "chan", 1)
    near0, token = near_sum("0", place, token, keep0, sent0)
    far0 = swap(near0, "chan", 2)
    grad3, band_mixed, proj3, cots, cots_leaving, token = gate(
        3, False, place, token, near3, far3, None, None, proj_weights, blank
    )
    other3 = swap(grad3, "chan", 1)
    cots_arrived = swap(cots_leaving, "row", 1)
    near1, token = near_sum("1", place, token, keep1, sent1)
    far1 = swap(near1, "chan", 2)
    grad0, band_mixed, proj_keep, proj_send, token = gate(
        0, False, place, token, near0, far0, cots, None, proj_weights, band_mixed, proj3
    )
    other0 = swap(grad0, "chan", 1)
    proj30 = (proj_keep, swap(proj_send, "dp", 1))
    near2, token = near_sum("2", place, token, keep2, sent2)
    far2 = swap(near2, "chan", 2)
    grad1, class_mixed, proj1, token = gate(
        1, True, place, token, near1, far1, cots, cots_arrived, proj_weights, blank
    )
    other1 = swap(grad1, "chan", 1)
    band, point3, depth3, token = backward(
        3, False, False, place, token, grad3, other3, x, x, spread3, *weights
    )
    grad2, class_mixed, proj_keep, proj_send, mixed_leaving, token = gate(
        2, True, place, token, near2, far2, cots, cots_arrived, proj_weights, class_mixed, proj1,
        leaves=True,
    )
    other2 = swap(grad2, "chan", 1)
    proj12 = (proj_keep, swap(proj_send, "dp", 1))
    pre0, point_keep, point_send, token = join(place, token, grad0, other0, x, point3)
    point30 = (point_keep, swap(point_send, "dp", 1))
    total1, depth1, point_keep, point_send, token = backward(
        1, True, True, place, token, grad1, other1, x, arrived, spread1, *weights
    )
    point1 = (point_keep, swap(point_send, "dp", 1))
    proj, token = add("proj", place, token, [proj30, proj12], BF16)
    proj = (proj, swap(proj, "chan", 1))
    early, token = add("early_1", place, token, [point30], BF16)
    early = (early, swap(early, "row", 1))
    leaving, stay, late_keep, late_send, token = backward(
        2, True, True, place, token, grad2, other2, x, arrived, spread2, *weights, before=total1,
        depths=(depth1, depth3), mixed=mixed_leaving,
    )
    input_arrived = swap(leaving, "row", 1)
    late = (late_keep, swap(late_send, "dp", 1))
    proj, token = add("proj_1", place, token, [proj], BF16, arrived=[early[1]])
    proj = (proj, swap(proj, "row", 1))
    late, token = add("late_1", place, token, [late, point1], BF16)
    late = (late, swap(late, "dp", 2))
    late, token = add("late_2", place, token, [late], BF16)
    late = (late, swap(late, "row", 1))
    early, token = add("early_2", place, token, [early], BF16)
    early = (early, swap(early, "dp", 2))
    proj, token = add("proj_2", place, token, [proj], BF16)
    proj = (proj, swap(proj, "dp", 2))
    early, token = add("early", place, token, [early], F32, scale)
    early = (early, swap(early, "dp", 1))
    proj, token = add("proj_sum", place, token, [proj], F32, scale)
    proj = (proj, swap(proj, "dp", 1))
    late, token = add("late", place, token, [late], F32, scale, arrived=[input_arrived])
    late = (late, swap(late, "dp", 1))
    bands = band_mixed.reshape((classes, n) + band_mixed.shape[1:])
    folds = class_mixed.reshape(bands.shape)
    grad_input, output, token = last(
        place, token, pre0, point_weights, band, stay, input_arrived, bands, folds
    )
    grad_proj, grad_depth, grad_point, token = finish(
        place, token, early, proj, late, channels, filters
    )
    return (
        output.reshape(cotangent.shape), grad_input.reshape(features_in.shape), grad_depth, grad_point,
        grad_proj,
    )


def shifted(value, axis, steps):
    count = lax.axis_size(axis)
    first, last = (max(0, -steps), min(count, count - steps))
    return lax.ppermute(value, axis, [(source, source + steps) for source in range(first, last)])


def window(source, top, left, band_rows, band_cols):
    upper = lax.slice_in_dim(source, top, top + band_rows, axis=1)
    return lax.slice_in_dim(upper, left, left + band_cols, axis=2)


def on_device(features_in, depth_weights, point_weights, proj_weights, cotangent):
    samples, band_rows, band_cols, channels = features_in.shape
    weight_scale = 1.0 / math.sqrt(
        samples * lax.axis_size("dp") * band_rows * lax.axis_size("row") * band_cols
    )
    largest_reach = 3 * BASE_DILATION
    offsets = (2, 1, -1, -2)
    arrivals = []
    for offset in offsets:
        arrivals.append(shifted(features_in, "row", offset))
    tall_rows = jnp.concatenate(
        [arrivals[0], arrivals[1], features_in, arrivals[2], arrivals[3]], axis=1
    )
    padded = jnp.pad(tall_rows, ((0, 0), (0, 0), (largest_reach, largest_reach), (0, 0)))
    branch_maps = [features_in]
    for branch_level in range(3):
        tap_spacing = (branch_level + 1) * BASE_DILATION
        summed = jnp.zeros(features_in.shape, jnp.float32)
        for row_tap in range(3):
            for col_tap in range(3):
                input_kernel_tap = window(
                    padded,
                    largest_reach + (row_tap - 1) * tap_spacing,
                    largest_reach + (col_tap - 1) * tap_spacing,
                    band_rows,
                    band_cols,
                )
                summed = summed + input_kernel_tap.astype(jnp.float32) * depth_weights[
                    branch_level, row_tap, col_tap
                ].astype(jnp.float32)
        branch_maps.append(summed.astype(jnp.bfloat16))
    spread = jnp.stack(branch_maps)
    full_point = lax.all_gather(point_weights, "chan", axis=1, tiled=True)
    preact = jnp.einsum(
        "bsrwc,bcf->bsrwf",
        lax.all_to_all(spread, "chan", split_axis=3, concat_axis=4, tiled=True),
        full_point,
        preferred_element_type=jnp.float32,
    )
    activation = jax.nn.silu(preact).astype(jnp.bfloat16)
    output = jnp.einsum(
        "bsrwf,bfg->srwg", activation, proj_weights, preferred_element_type=jnp.float32
    ).astype(jnp.bfloat16)
    silu_gradient = jnp.einsum(
        "srwg,bfg->bsrwf", cotangent, proj_weights, preferred_element_type=jnp.float32
    )
    logistic = jax.nn.sigmoid(preact)
    pre_grad = (silu_gradient * logistic * (1.0 + preact * (1.0 - logistic))).astype(jnp.bfloat16)
    proj_term = jnp.einsum(
        "bsrwf,srwg->bfg", activation, cotangent, preferred_element_type=jnp.float32
    )
    grad_proj = lax.psum(proj_term, ("row", "chan", "dp")) * weight_scale
    incoming = lax.all_gather(pre_grad, "chan", axis=3, tiled=True)
    local_grad = jnp.einsum(
        "bsrwf,bcf->bsrwc", incoming, point_weights, preferred_element_type=jnp.float32
    ).astype(jnp.bfloat16)
    spread_grad = local_grad
    point_sum = jnp.einsum("bsrwc,bsrwf->bcf", spread, incoming, preferred_element_type=jnp.float32)
    spread_grad, point_term = (spread_grad, point_sum)
    depth_rows = []
    for branch_level in range(3):
        tap_spacing = (branch_level + 1) * BASE_DILATION
        branch_grad = spread_grad[branch_level + 1].astype(jnp.float32)
        gathered = []
        for row_tap in range(3):
            for col_tap in range(3):
                input_kernel_tap = window(
                    padded,
                    largest_reach + (row_tap - 1) * tap_spacing,
                    largest_reach + (col_tap - 1) * tap_spacing,
                    band_rows,
                    band_cols,
                )
                gathered.append(
                    jnp.sum(input_kernel_tap.astype(jnp.float32) * branch_grad, axis=(0, 1, 2))
                )
        depth_rows.append(jnp.stack(gathered).reshape(3, 3, channels))
    depth_term = jnp.stack(depth_rows)
    point_summed, depth_summed = lax.psum((point_term, depth_term), ("row", "dp"))
    grad_point = point_summed * weight_scale
    grad_depth = depth_summed * weight_scale
    neighbour_sets = []
    for branch_level in range(3):
        neighbour_sets.append(
            [shifted(spread_grad[branch_level + 1], "row", offset) for offset in offsets]
        )
    grad_in = spread_grad[0].astype(jnp.float32)
    for branch_level in range(3):
        tap_spacing = (branch_level + 1) * BASE_DILATION
        received = neighbour_sets[branch_level]
        grad_tall = jnp.concatenate(
            [received[0], received[1], spread_grad[branch_level + 1], received[2], received[3]],
            axis=1,
        )
        grad_padded = jnp.pad(grad_tall, ((0, 0), (0, 0), (largest_reach, largest_reach), (0, 0)))
        for row_tap in range(3):
            for col_tap in range(3):
                grad_tap = window(
                    grad_padded,
                    largest_reach - (row_tap - 1) * tap_spacing,
                    largest_reach - (col_tap - 1) * tap_spacing,
                    band_rows,
                    band_cols,
                )
                grad_in = grad_in + grad_tap.astype(jnp.float32) * depth_weights[
                    branch_level, row_tap, col_tap
                ].astype(jnp.float32)
    return (output, grad_in.astype(jnp.bfloat16), grad_depth, grad_point, grad_proj)


def folds(mesh, features_in):
    sizes = mesh.shape
    samples, rows, cols, channels = features_in.shape
    return (
        rows == 3 * BASE_DILATION
        and sizes["row"] == 2
        and sizes["chan"] == 4
        and sizes["dp"] == 4
        and samples == sizes["dp"]
        and cols % 64 == 0
        and channels % (128 * sizes["chan"]) == 0
    )


def solution(mesh):
    in_specs = (
        P("dp", "row", None, "chan"),
        P(None, None, None, "chan"),
        P(None, "chan", None),
        P(),
        P("dp", "row", "chan", None),
    )
    out_specs = (
        P("dp", "row", "chan", None),
        P("dp", "row", None, "chan"),
        P(None, None, None, "chan"),
        P(None, "chan", None),
        P(),
    )

    def run(*args):
        body = by_classes if folds(mesh, args[0]) else on_device
        return jax.shard_map(
            body, mesh=mesh, in_specs=in_specs, out_specs=out_specs, check_vma=False
        )(*args)

    return run
```

```python
import functools
import math

import jax
import jax.numpy as jnp
from jax import lax
from jax.experimental import pallas as pl
from jax.experimental.pallas import tpu as pltpu
from jax.sharding import PartitionSpec as P

BASE_DILATION = 12
F32 = jnp.float32
BF16 = jnp.bfloat16
VMEM_BYTES = 28 * 2**20


def swap(value, axis, flip):
    count = lax.axis_size(axis)
    return lax.ppermute(value, axis, [(i, i ^ flip) for i in range(count)])


def moved(value, steps):
    count, width = value.shape
    if steps == 0:
        return 0, value
    far = abs(steps)
    whole, rest = far // 8 * 8, far % 8
    size = count - whole
    if rest == 0:
        return (0, value[whole:]) if steps > 0 else (whole, value[:size])
    blank = jnp.zeros((8, width), value.dtype)
    if steps > 0:
        longer = jnp.concatenate([value[whole:], blank])
        return 0, pltpu.roll(longer, size + 8 - rest, 0)[:size]
    longer = jnp.concatenate([blank, value[:size]])
    return whole, pltpu.roll(longer, rest, 0)[8:]


def add_moved(total, value, steps):
    if steps == 0:
        return value if total is None else total + value
    first, part = moved(value, steps)
    after = first + part.shape[0]
    pieces = [total[first:after] + part]
    if first > 0:
        pieces = [total[:first]] + pieces
    if after < total.shape[0]:
        pieces = pieces + [total[after:]]
    return jnp.concatenate(pieces)


def row_pairs(branch, classes):
    return [
        (q, i, q + (i - 1) * branch)
        for q in range(classes)
        for i in range(3)
        if 0 <= q + (i - 1) * branch < classes
    ]


def class_rows(upper, first, last, arrived):
    return (
        jnp.where(upper, first, arrived),
        jnp.where(upper, last, first),
        jnp.where(upper, arrived, last),
    )


def shape_of(shape, dtype):
    return jax.ShapeDtypeStruct(shape, dtype)


def in_hbm(value):
    return pltpu.with_memory_space_constraint(value, pltpu.HBM)


def result_of(shape, dtype):
    return jax.ShapeDtypeStruct(shape, dtype)


TOKEN = (8, 128)
STEPS = 1


def call(body, place, grid, after, ins, outs, name, scratch=()):
    def spec(block, split):
        dims = len(block)
        if isinstance(split, tuple):
            return pl.BlockSpec(block, lambda r, p: tuple(r if k is None else k for k in split))
        return pl.BlockSpec(block, lambda r, p: tuple(r if k == split else 0 for k in range(dims)))

    def kernel(place_ref, after_ref, *refs):
        last = len(ins) + len(outs) - 2
        body(place_ref, *refs[:last], *refs[last + 1 :])
        refs[last][...] = after_ref[...]

    ins = [(after, TOKEN, None)] + list(ins)
    outs = list(outs) + [(shape_of(TOKEN, F32), TOKEN, None)]
    return pl.pallas_call(
        kernel,
        grid_spec=pltpu.PrefetchScalarGridSpec(
            num_scalar_prefetch=1,
            grid=(grid,),
            in_specs=[spec(block, split) for _, block, split in ins],
            out_specs=[spec(block, split) for _, block, split in outs],
            scratch_shapes=list(scratch),
        ),
        out_shape=[s for s, _, _ in outs],
        compiler_params=pltpu.CompilerParams(vmem_limit_bytes=VMEM_BYTES),
        cost_estimate=pl.CostEstimate(flops=1, bytes_accessed=1, transcendentals=0),
        name=name,
    )(place, *[a for a, _, _ in ins])


def forward_kernel(branches, folded, place, x_ref, arrived_ref, taps_ref, *refs):
    classes, group, cols, channels = x_ref.shape
    count = len(branches)
    points, refs = refs[:count], refs[count:]
    keeps, sends, refs = refs[:count], refs[count : 2 * count], refs[2 * count :]
    spreads = dict(zip([b for b in branches if b], refs))
    if not branches[0]:
        refs[-1][...] = x_ref[1]

    def residue(r, carry):
        rows = [x_ref[q, r].astype(F32) for q in range(classes)]
        if folded:
            rows = class_rows(place[1] == 0, rows[0], rows[2], arrived_ref[r].astype(F32))
        for branch, spread_ref in spreads.items():
            for q in range(classes):
                total = None
                for j in (1, 0, 2):
                    part = None
                    for out, i, source in row_pairs(branch, classes):
                        if out == q:
                            tap = taps_ref[branch - 1, i, j].astype(F32)
                            term = rows[source] * tap[None, :]
                            part = term if part is None else part + term
                    total = add_moved(total, part, (j - 1) * branch * BASE_DILATION)
                spread_ref[q, r] = total.astype(BF16)
        return carry

    lax.fori_loop(0, group, residue, 0)
    for k, branch in enumerate(branches):
        cells = spreads[branch][...] if branch else x_ref[...]
        cells = cells.reshape(classes * group * cols, channels)
        partial = jnp.dot(cells, points[k][0], preferred_element_type=F32)
        split = partial.reshape(classes * group * 2, 2, cols // 4, partial.shape[-1])
        first = place[0] % 2 == 0
        keep = jnp.where(first, split[:, 0], split[:, 1])
        send = jnp.where(first, split[:, 1], split[:, 0])
        keeps[k][0] = keep.reshape(keeps[k].shape[1:])
        sends[k][0] = send.reshape(sends[k].shape[1:]).astype(BF16)


def forward(branches, folded, place, after, x, arrived, taps, point):
    classes, residues, cols, channels = x.shape
    filters = point.shape[2]
    group = residues // STEPS
    cell = (classes, group, cols, channels)
    part = (1, classes, group, 2, cols // 4, filters)
    part_shape = (1, classes, residues, 2, cols // 4, filters)
    outs = [(shape_of(part_shape, F32), part, 2) for _ in branches]
    outs += [(shape_of(part_shape, BF16), part, 2) for _ in branches]
    outs += [(shape_of(x.shape, BF16), cell, 1) for b in branches if b]
    if not branches[0]:
        outs += [(shape_of(x.shape[1:], BF16), (group, cols, channels), 0)]
    return call(
        functools.partial(forward_kernel, branches, folded), place, STEPS, after,
        [
            (x, cell, 1),
            (arrived, (group, cols, channels) if folded else (1, 1, 8, 128), 0 if folded else None),
            (taps, taps.shape, None),
        ]
        + [(point, (1, channels, filters), (b, 0, 0)) for b in branches],
        outs, "forward_" + "_".join(map(str, branches)),
    )


def near_kernel(place, keep_ref, arrived_ref, near_ref):
    near_ref[...] = (keep_ref[...] + arrived_ref[...].astype(F32)).astype(BF16)


def near_sum(name, place, after, keep, arrived):
    return call(
        near_kernel, place, 1, after, [(keep, keep.shape, None), (arrived, keep.shape, None)],
        [(shape_of(keep.shape, BF16), keep.shape, None)], f"near_{name}",
    )


def near_cot_kernel(place, keep_ref, arrived_ref, cot_ref, near_ref):
    near_ref[:, :, :, :2] = (keep_ref[...] + arrived_ref[...].astype(F32)).astype(BF16)
    near_ref[0, :, :, 2] = cot_ref[...].reshape(near_ref.shape[1:3] + near_ref.shape[4:])


def near_sum_cot(name, place, after, keep, arrived, cot):
    shape = keep.shape[:3] + (3,) + keep.shape[4:]
    return call(
        near_cot_kernel, place, 1, after,
        [(keep, keep.shape, None), (arrived, keep.shape, None), (cot, cot.shape, None)],
        [(shape_of(shape, BF16), shape, None)], f"near_{name}",
    )


def gate_kernel(branch, folded, first_gate, place, near_ref, far_ref, *refs):
    cot_ref = None
    if not first_gate:
        cot_ref, refs = refs[0], refs[1:]
    _, classes, residues, sides, width, filters = near_ref.shape
    if folded:
        arrived_ref, refs = refs[0], refs[1:]
    n, sides = residues, 2
    low_side = place[0] // 2 == 0
    if cot_ref is None:
        cots_ref, cots_leaving_ref, *refs = refs[-2:] + refs[:-2]
        own = near_ref[0, :, :, 2].reshape(classes * n, width, filters)
        far = far_ref[0, :, :, 2].reshape(classes * n, width, filters)
        cots_ref[:, 0] = jnp.where(low_side, own, far)
        cots_ref[:, 1] = jnp.where(low_side, far, own)
        cots_leaving_ref[...] = cots_ref[n : 2 * n]
        cot_ref = cots_ref
    paired = len(refs) > 5
    if paired:
        proj_ref, mixed_ref, earlier_ref, grad_ref, out_ref, keep_ref, send_ref, *leaving = refs
    else:
        proj_ref, mixed_ref, grad_ref, out_ref, proj_grad_ref = refs
    cots = cot_ref[...]
    if folded:
        cots = jnp.concatenate(
            class_rows(place[1] == 0, cots[:n], cots[2 * n : 3 * n], arrived_ref[...])
        )
    cells = cots.reshape(-1, filters)
    shape = (classes * residues, sides, width, filters)
    proj = proj_ref[0]
    act_grad = lax.dot_general(cells, proj, (((1,), (1,)), ((), ())), preferred_element_type=F32)
    preact = (near_ref[0, :, :, :2].astype(F32) + far_ref[0, :, :, :2].astype(F32)).reshape(shape)
    logistic = 1.0 / (1.0 + jnp.exp(-preact))
    grad = act_grad.reshape(shape) * logistic * (1.0 + preact * (1.0 - logistic))
    grad_ref[0] = grad.astype(BF16).reshape(grad_ref.shape[1:])
    active = (preact * logistic).astype(BF16)
    mine = jnp.where(low_side, active[:, 0], active[:, 1]).reshape(-1, filters)
    mixed = mixed_ref[...] + jnp.dot(mine, proj, preferred_element_type=F32).reshape(out_ref.shape)
    out_ref[...] = mixed
    proj_grad = lax.dot_general(
        active.reshape(-1, filters), cells, (((0,), (0,)), ((), ())), preferred_element_type=F32
    )
    if not paired:
        proj_grad_ref[...] = proj_grad
        return
    first = place[2] == 0
    keep_ref[...] = jnp.where(first, earlier_ref[...], proj_grad)
    send_ref[...] = jnp.where(first, proj_grad, earlier_ref[...]).astype(BF16)
    if leaving:
        leaving[0][...] = jnp.where(place[1] == 0, mixed[2 * n :], mixed[:n]).astype(BF16)


def gate(branch, folded, place, after, near, far, cots, arrived, proj, mixed, earlier=None, leaves=False):
    filters = proj.shape[-1]
    first_gate = cots is None
    arrays = [near, far] + ([] if first_gate else [cots]) + ([arrived] if folded else [])
    ins = [(a, a.shape, None) for a in arrays] + [(proj, (1, filters, filters), (branch, 0, 0))]
    ins += [(a, a.shape, None) for a in ([mixed] if earlier is None else [mixed, earlier])]
    part = (filters, filters)
    shapes = [(near.shape[:3] + (2,) + near.shape[4:], BF16), (mixed.shape, F32), (part, F32)]
    if earlier is not None:
        shapes.append((part, BF16))
    if first_gate:
        shapes.append(((mixed.shape[0], 2) + mixed.shape[1:], BF16))
        shapes.append(((mixed.shape[0] // 3, 2) + mixed.shape[1:], BF16))
    if leaves:
        shapes.append(((mixed.shape[0] // 3,) + mixed.shape[1:], BF16))
    return call(
        functools.partial(gate_kernel, branch, folded, first_gate), place, 1, after, ins,
        [(shape_of(shape, kind), shape, None) for shape, kind in shapes], f"gate_{branch}",
    )


def whole_columns(place, own, other):
    thin = (-1,) + own.shape[-2:]
    own, other = own.reshape(thin), other.reshape(thin)
    first = place[0] % 2 == 0
    low = jnp.where(first, own, other)
    high = jnp.where(first, other, own)
    both = jnp.concatenate([low[:, None], high[:, None]], axis=1)
    return both.reshape(-1, own.shape[-1])


def split_by_core(place, low, high, keep_ref, send_ref):
    first = place[2] == 0
    rows = low.shape[0]
    keep_ref[:rows] = jnp.where(first, low, high)
    send_ref[:rows] = jnp.where(first, high, low).astype(send_ref.dtype)


def backward_kernel(
    branch, folded, final, chained, place, own_ref, other_ref, x_ref, arrived_ref, spread_ref, taps_ref,
    point_ref, before_ref, *refs
):
    classes, group, cols, channels = x_ref.shape
    point_grad_ref, depth_ref, grads_ref = refs[-3:]
    refs = refs[:-3]
    if chained:
        mixed_ref, refs = refs[0], refs[1:]
    upper = place[1] == 0
    pre = whole_columns(place, own_ref[0], other_ref[0])
    grads = lax.dot_general(pre, point_ref[0], (((1,), (1,)), ((), ())), preferred_element_type=F32)
    grads_ref[...] = grads.astype(BF16).reshape(grads_ref.shape)
    cells = spread_ref[...].reshape(classes * group * cols, channels)
    product = lax.dot_general(cells, pre, (((0,), (0,)), ((), ())), preferred_element_type=F32)

    @pl.when(pl.program_id(0) == 0)
    def _():
        point_grad_ref[...] = product
        depth_ref[...] = jnp.zeros_like(depth_ref)

    @pl.when(pl.program_id(0) > 0)
    def _():
        point_grad_ref[...] += product

    outs = refs[2:] if chained else refs
    pairs = row_pairs(branch, classes)

    def residue(r, carry):
        rows = [x_ref[q, r].astype(F32) for q in range(classes)]
        if folded:
            rows = class_rows(upper, rows[0], rows[2], arrived_ref[r].astype(F32))
        grads = [grads_ref[q, r].astype(F32) for q in range(classes)]
        for j in range(3):
            shifts = [moved(row, (j - 1) * branch * BASE_DILATION) for row in rows]
            first, near = shifts[0][0], [part for _, part in shifts]
            size = near[0].shape[0]
            for i in range(3):
                part = None
                for q, tap, source in pairs:
                    if tap == i:
                        term = near[source] * grads[q][first : first + size]
                        term = term.reshape(size // 8, 8, channels).sum(axis=0)
                        part = term if part is None else part + term
                if part is not None:
                    depth_ref[i * 3 + j] += part
        totals = []
        for target in range(classes):
            total = before_ref[target, r] if chained else None
            for j in (1, 0, 2):
                part = None
                for q, i, source in pairs:
                    if source == target:
                        term = grads[q] * taps_ref[branch - 1, i, j].astype(F32)[None, :]
                        part = term if part is None else part + term
                total = add_moved(total, part, -(j - 1) * branch * BASE_DILATION)
            totals.append(total)
        if chained:
            leaving_ref, stay_ref = outs[:2]
            at = pl.multiple_of(r * cols, cols)
            leaving_ref[pl.ds(at, cols)] = jnp.where(upper, totals[2], totals[0]).astype(BF16)
            stay_ref[0, r] = jnp.where(upper, totals[0], totals[1])
            stay_ref[1, r] = jnp.where(upper, totals[1], totals[2])
        else:
            for q in range(classes):
                outs[0][q, r] = totals[q]
        return carry

    lax.fori_loop(0, group, residue, 0)
    if chained:
        width, filters = mixed_ref.shape[1:]
        for r in range(group // 2):
            at = group * cols + r * width
            outs[0][at : at + width, :filters] = mixed_ref[r]
            outs[0][at : at + width, filters:] = mixed_ref[r + group // 2]

    @pl.when(pl.program_id(0) == STEPS - 1)
    def _():
        depth = depth_ref[...].sum(axis=1)
        if final:
            keep_ref, send_ref = outs[-2:]
            half, filters = channels // 2, point_grad_ref.shape[1]
            split_by_core(place, point_grad_ref[:half], point_grad_ref[half:], keep_ref, send_ref)
            if chained:
                depths = jnp.concatenate([refs[0][...], depth, refs[1][...]])
                low, high = depths[:, :filters], depths[:, filters:]
                first = place[2] == 0
                keep_ref[half : half + 27] = jnp.where(first, low, high)
                send_ref[half : half + 27] = jnp.where(first, high, low).astype(BF16)
                blank = jnp.zeros((keep_ref.shape[0] - half - 27, filters), F32)
                keep_ref[half + 27 :] = blank
                send_ref[half + 27 :] = blank.astype(BF16)
            else:
                outs[-3][...] = depth
        else:
            outs[-2][...] = point_grad_ref[...]
            outs[-1][...] = depth


def backward(
    branch, folded, final, place, after, own, other, x, arrived, spread, taps, point, before=None, depths=(),
    mixed=None
):
    classes, residues, cols, channels = x.shape
    filters = point.shape[2]
    group = residues // STEPS
    part = (1, classes, group, 2, cols // 4, filters)
    cell = (classes, group, cols, channels)
    thin = (group, cols, channels)
    chained = before is not None
    flat = (residues * cols + residues // 2 * (cols // 4), channels)
    if chained:
        outs = [
            (shape_of(flat, BF16), flat, None),
            (shape_of((2,) + x.shape[1:], F32), (2,) + thin, 1),
        ]
    else:
        outs = [(shape_of(x.shape, F32), cell, 1)]
    halves = (channels // 2 + (32 if chained else 0), filters)
    shapes = [(channels, filters), (9, channels)]
    if final:
        shapes = [halves, halves] if chained else [(9, channels), halves, halves]
    outs += [(shape_of(shape, F32), shape, None) for shape in shapes]
    if final:
        outs[-1] = (shape_of(halves, BF16), halves, None)
    small = (1, 1, 8, 128)
    return call(
        functools.partial(backward_kernel, branch, folded, final, chained), place, STEPS, after,
        [
            (own, part, 2),
            (other, part, 2),
            (x, cell, 1),
            (arrived, thin, 0) if folded else (x, small, None),
            (spread, cell, 1),
            (taps, taps.shape, None),
            (point, (1, channels, filters), (branch, 0, 0)),
            (before, cell, 1) if chained else (x, small, None),
        ]
        + ([(mixed, (group,) + mixed.shape[1:], 0)] if chained else [])
        + [(d, d.shape, None) for d in depths],
        outs, f"backward_{branch}",
        scratch=[
            pltpu.VMEM((channels, filters), F32),
            pltpu.VMEM((9, 8, channels), F32),
            pltpu.VMEM(cell, BF16),
        ],
    )


def join_kernel(place, own_ref, other_ref, x_ref, earlier_ref, pre_ref, keep_ref, send_ref, total_ref):
    pre = whole_columns(place, own_ref[0], other_ref[0])
    pre_ref[...] = pre.reshape(pre_ref.shape)
    cells = x_ref[...].reshape(-1, x_ref.shape[-1])
    product = lax.dot_general(cells, pre, (((0,), (0,)), ((), ())), preferred_element_type=F32)

    @pl.when(pl.program_id(0) == 0)
    def _():
        total_ref[...] = product

    @pl.when(pl.program_id(0) > 0)
    def _():
        total_ref[...] += product

    @pl.when(pl.program_id(0) == STEPS - 1)
    def _():
        split_by_core(place, earlier_ref[...], total_ref[...], keep_ref, send_ref)


def join(place, after, own, other, x, earlier):
    classes, residues, cols, channels = x.shape
    filters = own.shape[-1]
    group = residues // STEPS
    part = (1, classes, group, 2, cols // 4, filters)
    return call(
        join_kernel, place, STEPS, after,
        [
            (own, part, 2),
            (other, part, 2),
            (x, (classes, group, cols, channels), 1),
            (earlier, earlier.shape, None),
        ],
        [
            (shape_of((classes, residues, cols, filters), BF16), (classes, group, cols, filters), 1),
            (shape_of(earlier.shape, F32), earlier.shape, None),
            (shape_of(earlier.shape, BF16), earlier.shape, None),
        ],
        "join", scratch=[pltpu.VMEM(earlier.shape, F32)],
    )


def last_kernel(
    place, pre_ref, point_ref, band_ref, stay_ref, arrived_ref, mixed_ref, folded_ref, input_ref, output_ref
):
    classes, group, cols, channels = band_ref.shape
    pre = pre_ref[...].reshape(classes * group * cols, -1)
    grads = lax.dot_general(pre, point_ref[0], (((1,), (1,)), ((), ())), preferred_element_type=F32)
    grads = grads.astype(BF16).astype(F32).reshape(band_ref.shape)
    cells = group * cols
    arrived = arrived_ref[:cells].reshape(group, cols, channels).astype(F32)
    others = (stay_ref[0], arrived, stay_ref[1])
    for q in range(classes):
        input_ref[q] = (grads[q] + band_ref[q] + others[q]).astype(BF16)
    upper = place[1] == 0
    width, filters = mixed_ref.shape[2:]
    rest = arrived_ref[cells:].reshape(group // 2, width, channels)
    mixed = (
        jnp.where(upper, folded_ref[0], folded_ref[1]),
        jnp.concatenate([rest[..., :filters], rest[..., filters:]]).astype(F32),
        jnp.where(upper, folded_ref[1], folded_ref[2]),
    )
    for q in range(classes):
        output_ref[q] = (mixed_ref[q] + mixed[q]).astype(BF16)


def last(place, after, pre, point, band, stay, arrived, mixed, folded):
    classes, residues, cols, channels = band.shape
    filters = point.shape[2]
    group = residues // STEPS
    cell = (classes, group, cols, channels)
    thin = (classes, group) + mixed.shape[2:]
    return call(
        last_kernel, place, STEPS, after,
        [
            (pre, (classes, group, cols, filters), 1),
            (point, (1, channels, filters), (0, 0, 0)),
            (band, cell, 1),
            (stay, (2, group, cols, channels), 1),
            (arrived, arrived.shape, None),
            (mixed, thin, 1),
            (folded, thin, 1),
        ],
        [(result_of(band.shape, BF16), cell, 1), (result_of(mixed.shape, BF16), thin, 1)], "last",
    )


def add_kernel(scale, counts, place, *refs):
    terms, out_ref = refs[: sum(counts)], refs[-1]
    at = 0
    for count in counts:
        group, terms = terms[:count], terms[count:]
        values = [ref[...].astype(F32) for ref in group]
        total = sum(values[1:], values[0])
        if scale != 1.0:
            total = total * scale
        rows = group[0].shape[0]
        out_ref[at : at + rows] = total.astype(out_ref.dtype)
        at += rows


def add(name, place, after, groups, kind, scale=1.0, arrived=()):
    shape = (sum(group[0].shape[0] for group in groups), groups[0][0].shape[1])
    counts = [len(group) for group in groups]
    return call(
        functools.partial(add_kernel, scale, counts), place, 1, after,
        [(a, a.shape, None) for group in groups for a in group]
        + [(a, (1,) * (len(a.shape) - 2) + a.shape[-2:], None) for a in arrived],
        [(shape_of(shape, kind), shape, None)], name,
    )


def finish_kernel(place, own30, far30, own_proj, far_proj, own21, far21, proj_ref, depth_ref, point_ref):
    core = place[2] == 0

    def halves(own, far, first, count):
        own, far = own[first : first + count], far[first : first + count]
        return jnp.where(core, own, far), jnp.where(core, far, own)

    channels = point_ref.shape[1]
    filters = proj_ref.shape[1]
    half = channels // 2
    point_ref[3], point_ref[0] = halves(own30, far30, 0, channels)
    proj_ref[3], proj_ref[0] = halves(own_proj, far_proj, 0, filters)
    proj_ref[1], proj_ref[2] = halves(own_proj, far_proj, filters, filters)
    point_ref[2, :half], point_ref[2, half:] = halves(own21, far21, 0, half)
    low, high = halves(own21, far21, half, 27)
    for k in range(9):
        rows = slice(3 * k, 3 * k + 3)
        depth_ref[k // 3, k % 3, :, :filters] = low[rows]
        depth_ref[k // 3, k % 3, :, filters:] = high[rows]
    first = own21.shape[0] - half
    point_ref[1, :half], point_ref[1, half:] = halves(own21, far21, first, half)


def finish(place, after, early, proj, late, channels, filters):
    arrays = [*early, *proj, *late]
    shapes = [(4, filters, filters), (3, 3, 3, channels), (4, channels, filters)]
    return call(
        finish_kernel, place, 1, after, [(a, a.shape, None) for a in arrays],
        [(result_of(s, F32), s, None) for s in shapes], "finish",
    )


def by_classes(features_in, depth_weights, point_weights, proj_weights, cotangent):
    _, band_rows, cols, channels = features_in.shape
    filters = point_weights.shape[2]
    classes, n = 3, band_rows // 3
    scale = 1.0 / math.sqrt(lax.axis_size("dp") * band_rows * lax.axis_size("row") * cols)
    chan, row = lax.axis_index("chan"), lax.axis_index("row")
    core = lax.axis_index("dp") % 2
    place = jnp.stack([chan, row, core]).astype(jnp.int32)
    x = features_in[0].reshape(classes, n, cols, channels)

    weights = (depth_weights, point_weights)
    cot = cotangent[0]

    token, blank = jnp.zeros(TOKEN, F32), jnp.zeros(cot.shape, F32)
    keep3, send3, spread3, token = forward(
        (3,), False, place, token, in_hbm(x), x, in_hbm(depth_weights), in_hbm(point_weights)
    )
    sent3 = swap(send3, "chan", 1)
    keep0, send0, x_leaving, token = forward(
        (0,), False, place, token, x, x, in_hbm(depth_weights), in_hbm(point_weights)
    )
    sent0 = swap(send0, "chan", 1)
    arrived = swap(x_leaving, "row", 1)
    near3, token = near_sum_cot("3", place, token, keep3, sent3, cot)
    far3 = swap(near3, "chan", 2)
    keep1, keep2, send1, send2, spread1, spread2, token = forward(
        (1, 2), True, place, token, x, arrived, *weights
    )
    sent1, sent2 = swap(send1, "chan", 1), swap(send2, "chan", 1)
    near0, token = near_sum("0", place, token, keep0, sent0)
    far0 = swap(near0, "chan", 2)
    grad3, band_mixed, proj3, cots, cots_leaving, token = gate(
        3, False, place, token, near3, far3, None, None, proj_weights, blank
    )
    other3 = swap(grad3, "chan", 1)
    cots_arrived = swap(cots_leaving, "row", 1)
    near1, token = near_sum("1", place, token, keep1, sent1)
    far1 = swap(near1, "chan", 2)
    grad0, band_mixed, proj_keep, proj_send, token = gate(
        0, False, place, token, near0, far0, cots, None, proj_weights, band_mixed, proj3
    )
    other0 = swap(grad0, "chan", 1)
    proj30 = (proj_keep, swap(proj_send, "dp", 1))
    near2, token = near_sum("2", place, token, keep2, sent2)
    far2 = swap(near2, "chan", 2)
    grad1, class_mixed, proj1, token = gate(
        1, True, place, token, near1, far1, cots, cots_arrived, proj_weights, blank
    )
    other1 = swap(grad1, "chan", 1)
    band, point3, depth3, token = backward(
        3, False, False, place, token, grad3, other3, x, x, spread3, *weights
    )
    grad2, class_mixed, proj_keep, proj_send, mixed_leaving, token = gate(
        2, True, place, token, near2, far2, cots, cots_arrived, proj_weights, class_mixed, proj1,
        leaves=True,
    )
    other2 = swap(grad2, "chan", 1)
    proj12 = (proj_keep, swap(proj_send, "dp", 1))
    pre0, point_keep, point_send, token = join(place, token, grad0, other0, x, point3)
    point30 = (point_keep, swap(point_send, "dp", 1))
    total1, depth1, point_keep, point_send, token = backward(
        1, True, True, place, token, grad1, other1, x, arrived, spread1, *weights
    )
    point1 = (point_keep, swap(point_send, "dp", 1))
    proj, token = add("proj", place, token, [proj30, proj12], BF16)
    proj = (proj, swap(proj, "chan", 1))
    early, token = add("early_1", place, token, [point30], BF16)
    early = (early, swap(early, "row", 1))
    leaving, stay, late_keep, late_send, token = backward(
        2, True, True, place, token, grad2, other2, x, arrived, spread2, *weights, before=total1,
        depths=(depth1, depth3), mixed=mixed_leaving,
    )
    input_arrived = swap(leaving, "row", 1)
    late = (late_keep, swap(late_send, "dp", 1))
    proj, token = add("proj_1", place, token, [proj], BF16, arrived=[early[1]])
    proj = (proj, swap(proj, "row", 1))
    late, token = add("late_1", place, token, [late, point1], BF16)
    late = (late, swap(late, "dp", 2))
    late, token = add("late_2", place, token, [late], BF16)
    late = (late, swap(late, "row", 1))
    early, token = add("early_2", place, token, [early], BF16)
    early = (early, swap(early, "dp", 2))
    proj, token = add("proj_2", place, token, [proj], BF16)
    proj = (proj, swap(proj, "dp", 2))
    early, token = add("early", place, token, [early], F32, scale)
    early = (early, swap(early, "dp", 1))
    proj, token = add("proj_sum", place, token, [proj], F32, scale)
    proj = (proj, swap(proj, "dp", 1))
    late, token = add("late", place, token, [late], F32, scale, arrived=[input_arrived])
    late = (late, swap(late, "dp", 1))
    bands = band_mixed.reshape((classes, n) + band_mixed.shape[1:])
    folds = class_mixed.reshape(bands.shape)
    grad_input, output, token = last(
        place, token, pre0, point_weights, band, stay, input_arrived, bands, folds
    )
    grad_proj, grad_depth, grad_point, token = finish(
        place, token, early, proj, late, channels, filters
    )
    return (
        output.reshape(cotangent.shape), grad_input.reshape(features_in.shape), grad_depth, grad_point,
        grad_proj,
    )


def shifted(value, axis, steps):
    count = lax.axis_size(axis)
    first, last = (max(0, -steps), min(count, count - steps))
    return lax.ppermute(value, axis, [(source, source + steps) for source in range(first, last)])


def window(source, top, left, band_rows, band_cols):
    upper = lax.slice_in_dim(source, top, top + band_rows, axis=1)
    return lax.slice_in_dim(upper, left, left + band_cols, axis=2)


def on_device(features_in, depth_weights, point_weights, proj_weights, cotangent):
    samples, band_rows, band_cols, channels = features_in.shape
    weight_scale = 1.0 / math.sqrt(
        samples * lax.axis_size("dp") * band_rows * lax.axis_size("row") * band_cols
    )
    largest_reach = 3 * BASE_DILATION
    offsets = (2, 1, -1, -2)
    arrivals = []
    for offset in offsets:
        arrivals.append(shifted(features_in, "row", offset))
    tall_rows = jnp.concatenate(
        [arrivals[0], arrivals[1], features_in, arrivals[2], arrivals[3]], axis=1
    )
    padded = jnp.pad(tall_rows, ((0, 0), (0, 0), (largest_reach, largest_reach), (0, 0)))
    branch_maps = [features_in]
    for branch_level in range(3):
        tap_spacing = (branch_level + 1) * BASE_DILATION
        summed = jnp.zeros(features_in.shape, jnp.float32)
        for row_tap in range(3):
            for col_tap in range(3):
                input_kernel_tap = window(
                    padded,
                    largest_reach + (row_tap - 1) * tap_spacing,
                    largest_reach + (col_tap - 1) * tap_spacing,
                    band_rows,
                    band_cols,
                )
                summed = summed + input_kernel_tap.astype(jnp.float32) * depth_weights[
                    branch_level, row_tap, col_tap
                ].astype(jnp.float32)
        branch_maps.append(summed.astype(jnp.bfloat16))
    spread = jnp.stack(branch_maps)
    full_point = lax.all_gather(point_weights, "chan", axis=1, tiled=True)
    preact = jnp.einsum(
        "bsrwc,bcf->bsrwf",
        lax.all_to_all(spread, "chan", split_axis=3, concat_axis=4, tiled=True),
        full_point,
        preferred_element_type=jnp.float32,
    )
    activation = jax.nn.silu(preact).astype(jnp.bfloat16)
    output = jnp.einsum(
        "bsrwf,bfg->srwg", activation, proj_weights, preferred_element_type=jnp.float32
    ).astype(jnp.bfloat16)
    silu_gradient = jnp.einsum(
        "srwg,bfg->bsrwf", cotangent, proj_weights, preferred_element_type=jnp.float32
    )
    logistic = jax.nn.sigmoid(preact)
    pre_grad = (silu_gradient * logistic * (1.0 + preact * (1.0 - logistic))).astype(jnp.bfloat16)
    proj_term = jnp.einsum(
        "bsrwf,srwg->bfg", activation, cotangent, preferred_element_type=jnp.float32
    )
    grad_proj = lax.psum(proj_term, ("row", "chan", "dp")) * weight_scale
    incoming = lax.all_gather(pre_grad, "chan", axis=3, tiled=True)
    local_grad = jnp.einsum(
        "bsrwf,bcf->bsrwc", incoming, point_weights, preferred_element_type=jnp.float32
    ).astype(jnp.bfloat16)
    spread_grad = local_grad
    point_sum = jnp.einsum("bsrwc,bsrwf->bcf", spread, incoming, preferred_element_type=jnp.float32)
    spread_grad, point_term = (spread_grad, point_sum)
    depth_rows = []
    for branch_level in range(3):
        tap_spacing = (branch_level + 1) * BASE_DILATION
        branch_grad = spread_grad[branch_level + 1].astype(jnp.float32)
        gathered = []
        for row_tap in range(3):
            for col_tap in range(3):
                input_kernel_tap = window(
                    padded,
                    largest_reach + (row_tap - 1) * tap_spacing,
                    largest_reach + (col_tap - 1) * tap_spacing,
                    band_rows,
                    band_cols,
                )
                gathered.append(
                    jnp.sum(input_kernel_tap.astype(jnp.float32) * branch_grad, axis=(0, 1, 2))
                )
        depth_rows.append(jnp.stack(gathered).reshape(3, 3, channels))
    depth_term = jnp.stack(depth_rows)
    point_summed, depth_summed = lax.psum((point_term, depth_term), ("row", "dp"))
    grad_point = point_summed * weight_scale
    grad_depth = depth_summed * weight_scale
    neighbour_sets = []
    for branch_level in range(3):
        neighbour_sets.append(
            [shifted(spread_grad[branch_level + 1], "row", offset) for offset in offsets]
        )
    grad_in = spread_grad[0].astype(jnp.float32)
    for branch_level in range(3):
        tap_spacing = (branch_level + 1) * BASE_DILATION
        received = neighbour_sets[branch_level]
        grad_tall = jnp.concatenate(
            [received[0], received[1], spread_grad[branch_level + 1], received[2], received[3]],
            axis=1,
        )
        grad_padded = jnp.pad(grad_tall, ((0, 0), (0, 0), (largest_reach, largest_reach), (0, 0)))
        for row_tap in range(3):
            for col_tap in range(3):
                grad_tap = window(
                    grad_padded,
                    largest_reach - (row_tap - 1) * tap_spacing,
                    largest_reach - (col_tap - 1) * tap_spacing,
                    band_rows,
                    band_cols,
                )
                grad_in = grad_in + grad_tap.astype(jnp.float32) * depth_weights[
                    branch_level, row_tap, col_tap
                ].astype(jnp.float32)
    return (output, grad_in.astype(jnp.bfloat16), grad_depth, grad_point, grad_proj)


def folds(mesh, features_in, point_weights):
    sizes = mesh.shape
    samples, rows, cols, channels = features_in.shape
    return (
        rows == 3 * BASE_DILATION
        and sizes["row"] == 2
        and sizes["chan"] == 4
        and sizes["dp"] == 4
        and samples == sizes["dp"]
        and cols % 64 == 0
        and channels % (128 * sizes["chan"]) == 0
        and channels == 2 * sizes["chan"] * point_weights.shape[2]
    )


def solution(mesh):
    in_specs = (
        P("dp", "row", None, "chan"),
        P(None, None, None, "chan"),
        P(None, "chan", None),
        P(),
        P("dp", "row", "chan", None),
    )
    out_specs = (
        P("dp", "row", "chan", None),
        P("dp", "row", None, "chan"),
        P(None, None, None, "chan"),
        P(None, "chan", None),
        P(),
    )

    def run(*args):
        body = by_classes if folds(mesh, args[0], args[2]) else on_device
        return jax.shard_map(
            body, mesh=mesh, in_specs=in_specs, out_specs=out_specs, check_vma=False
        )(*args)

    return run
```

```python
import functools
import math

import jax
import jax.numpy as jnp
from jax import lax
from jax.experimental import pallas as pl
from jax.experimental.pallas import tpu as pltpu
from jax.sharding import PartitionSpec as P

BASE_DILATION = 12
F32 = jnp.float32
BF16 = jnp.bfloat16
VMEM_BYTES = 28 * 2**20


def swap(value, axis, flip):
    count = lax.axis_size(axis)
    return lax.ppermute(value, axis, [(i, i ^ flip) for i in range(count)])


def moved(value, steps):
    count, width = value.shape
    if steps == 0:
        return 0, value
    far = abs(steps)
    whole, rest = far // 8 * 8, far % 8
    size = count - whole
    if rest == 0:
        return (0, value[whole:]) if steps > 0 else (whole, value[:size])
    blank = jnp.zeros((8, width), value.dtype)
    if steps > 0:
        longer = jnp.concatenate([value[whole:], blank])
        return 0, pltpu.roll(longer, size + 8 - rest, 0)[:size]
    longer = jnp.concatenate([blank, value[:size]])
    return whole, pltpu.roll(longer, rest, 0)[8:]


def add_moved(total, value, steps):
    if steps == 0:
        return value if total is None else total + value
    first, part = moved(value, steps)
    after = first + part.shape[0]
    pieces = [total[first:after] + part]
    if first > 0:
        pieces = [total[:first]] + pieces
    if after < total.shape[0]:
        pieces = pieces + [total[after:]]
    return jnp.concatenate(pieces)


def row_pairs(branch, classes):
    return [
        (q, i, q + (i - 1) * branch)
        for q in range(classes)
        for i in range(3)
        if 0 <= q + (i - 1) * branch < classes
    ]


def class_rows(upper, first, last, arrived):
    return (
        jnp.where(upper, first, arrived),
        jnp.where(upper, last, first),
        jnp.where(upper, arrived, last),
    )


def shape_of(shape, dtype):
    return jax.ShapeDtypeStruct(shape, dtype)


def in_hbm(value):
    return pltpu.with_memory_space_constraint(value, pltpu.HBM)


def result_of(shape, dtype):
    return jax.ShapeDtypeStruct(shape, dtype)


TOKEN = (8, 128)
STEPS = 1


def call(body, place, grid, after, ins, outs, name, scratch=()):
    def spec(block, split):
        dims = len(block)
        if isinstance(split, tuple):
            return pl.BlockSpec(block, lambda r, p: tuple(r if k is None else k for k in split))
        return pl.BlockSpec(block, lambda r, p: tuple(r if k == split else 0 for k in range(dims)))

    def kernel(place_ref, after_ref, *refs):
        last = len(ins) + len(outs) - 2
        body(place_ref, *refs[:last], *refs[last + 1 :])
        refs[last][...] = after_ref[...]

    ins = [(after, TOKEN, None)] + list(ins)
    outs = list(outs) + [(shape_of(TOKEN, F32), TOKEN, None)]
    return pl.pallas_call(
        kernel,
        grid_spec=pltpu.PrefetchScalarGridSpec(
            num_scalar_prefetch=1,
            grid=(grid,),
            in_specs=[spec(block, split) for _, block, split in ins],
            out_specs=[spec(block, split) for _, block, split in outs],
            scratch_shapes=list(scratch),
        ),
        out_shape=[s for s, _, _ in outs],
        compiler_params=pltpu.CompilerParams(vmem_limit_bytes=VMEM_BYTES),
        cost_estimate=pl.CostEstimate(flops=1, bytes_accessed=1, transcendentals=0),
        name=name,
    )(place, *[a for a, _, _ in ins])


def forward_kernel(branches, folded, place, x_ref, arrived_ref, taps_ref, *refs):
    classes, group, cols, channels = x_ref.shape
    count = len(branches)
    points, refs = refs[:count], refs[count:]
    keeps, sends, refs = refs[:count], refs[count : 2 * count], refs[2 * count :]
    spreads = dict(zip([b for b in branches if b], refs))
    if not branches[0]:
        refs[-1][...] = x_ref[1]

    def residue(r, carry):
        rows = [x_ref[q, r].astype(F32) for q in range(classes)]
        if folded:
            rows = class_rows(place[1] == 0, rows[0], rows[2], arrived_ref[r].astype(F32))
        for branch, spread_ref in spreads.items():
            for q in range(classes):
                total = None
                for j in (1, 0, 2):
                    part = None
                    for out, i, source in row_pairs(branch, classes):
                        if out == q:
                            tap = taps_ref[branch - 1, i, j].astype(F32)
                            term = rows[source] * tap[None, :]
                            part = term if part is None else part + term
                    total = add_moved(total, part, (j - 1) * branch * BASE_DILATION)
                spread_ref[q, r] = total.astype(BF16)
        return carry

    lax.fori_loop(0, group, residue, 0)
    for k, branch in enumerate(branches):
        cells = spreads[branch][...] if branch else x_ref[...]
        cells = cells.reshape(classes * group * cols, channels)
        partial = jnp.dot(cells, points[k][0], preferred_element_type=F32)
        split = partial.reshape(classes * group * 2, 2, cols // 4, partial.shape[-1])
        first = place[0] % 2 == 0
        keep = jnp.where(first, split[:, 0], split[:, 1])
        send = jnp.where(first, split[:, 1], split[:, 0])
        keeps[k][0] = keep.reshape(keeps[k].shape[1:])
        sends[k][0] = send.reshape(sends[k].shape[1:]).astype(BF16)


def forward(branches, folded, place, after, x, arrived, taps, point):
    classes, residues, cols, channels = x.shape
    filters = point.shape[2]
    group = residues // STEPS
    cell = (classes, group, cols, channels)
    part = (1, classes, group, 2, cols // 4, filters)
    part_shape = (1, classes, residues, 2, cols // 4, filters)
    outs = [(shape_of(part_shape, F32), part, 2) for _ in branches]
    outs += [(shape_of(part_shape, BF16), part, 2) for _ in branches]
    outs += [(shape_of(x.shape, BF16), cell, 1) for b in branches if b]
    if not branches[0]:
        outs += [(shape_of(x.shape[1:], BF16), (group, cols, channels), 0)]
    return call(
        functools.partial(forward_kernel, branches, folded), place, STEPS, after,
        [
            (x, cell, 1),
            (arrived, (group, cols, channels) if folded else (1, 1, 8, 128), 0 if folded else None),
            (taps, taps.shape, None),
        ]
        + [(point, (1, channels, filters), (b, 0, 0)) for b in branches],
        outs, "forward_" + "_".join(map(str, branches)),
    )


def near_kernel(place, keep_ref, arrived_ref, near_ref):
    near_ref[...] = (keep_ref[...] + arrived_ref[...].astype(F32)).astype(BF16)


def near_sum(name, place, after, keep, arrived):
    return call(
        near_kernel, place, 1, after, [(keep, keep.shape, None), (arrived, keep.shape, None)],
        [(shape_of(keep.shape, BF16), keep.shape, None)], f"near_{name}",
    )


def near_cot_kernel(place, keep_ref, arrived_ref, cot_ref, near_ref):
    near_ref[:, :, :, :2] = (keep_ref[...] + arrived_ref[...].astype(F32)).astype(BF16)
    near_ref[0, :, :, 2] = cot_ref[...].reshape(near_ref.shape[1:3] + near_ref.shape[4:])


def near_sum_cot(name, place, after, keep, arrived, cot):
    shape = keep.shape[:3] + (3,) + keep.shape[4:]
    return call(
        near_cot_kernel, place, 1, after,
        [(keep, keep.shape, None), (arrived, keep.shape, None), (cot, cot.shape, None)],
        [(shape_of(shape, BF16), shape, None)], f"near_{name}",
    )


def gate_kernel(branch, folded, first_gate, place, near_ref, far_ref, *refs):
    cot_ref = None
    if not first_gate:
        cot_ref, refs = refs[0], refs[1:]
    _, classes, residues, sides, width, filters = near_ref.shape
    if folded:
        arrived_ref, refs = refs[0], refs[1:]
    n, sides = residues, 2
    low_side = place[0] // 2 == 0
    if cot_ref is None:
        cots_ref, cots_leaving_ref, *refs = refs[-2:] + refs[:-2]
        own = near_ref[0, :, :, 2].reshape(classes * n, width, filters)
        far = far_ref[0, :, :, 2].reshape(classes * n, width, filters)
        cots_ref[:, 0] = jnp.where(low_side, own, far)
        cots_ref[:, 1] = jnp.where(low_side, far, own)
        cots_leaving_ref[...] = cots_ref[n : 2 * n]
        cot_ref = cots_ref
    paired = len(refs) > 5
    if paired:
        proj_ref, mixed_ref, earlier_ref, grad_ref, out_ref, keep_ref, send_ref, *leaving = refs
    else:
        proj_ref, mixed_ref, grad_ref, out_ref, proj_grad_ref = refs
    cots = cot_ref[...]
    if folded:
        cots = jnp.concatenate(
            class_rows(place[1] == 0, cots[:n], cots[2 * n : 3 * n], arrived_ref[...])
        )
    cells = cots.reshape(-1, filters)
    shape = (classes * residues, sides, width, filters)
    proj = proj_ref[0]
    act_grad = lax.dot_general(cells, proj, (((1,), (1,)), ((), ())), preferred_element_type=F32)
    preact = (near_ref[0, :, :, :2].astype(F32) + far_ref[0, :, :, :2].astype(F32)).reshape(shape)
    logistic = 1.0 / (1.0 + jnp.exp(-preact))
    grad = act_grad.reshape(shape) * logistic * (1.0 + preact * (1.0 - logistic))
    grad_ref[0] = grad.astype(BF16).reshape(grad_ref.shape[1:])
    active = (preact * logistic).astype(BF16)
    mine = jnp.where(low_side, active[:, 0], active[:, 1]).reshape(-1, filters)
    mixed = mixed_ref[...] + jnp.dot(mine, proj, preferred_element_type=F32).reshape(out_ref.shape)
    out_ref[...] = mixed
    proj_grad = lax.dot_general(
        active.reshape(-1, filters), cells, (((0,), (0,)), ((), ())), preferred_element_type=F32
    )
    if not paired:
        proj_grad_ref[...] = proj_grad
        return
    first = place[2] == 0
    keep_ref[...] = jnp.where(first, earlier_ref[...], proj_grad)
    send_ref[...] = jnp.where(first, proj_grad, earlier_ref[...]).astype(BF16)
    if leaving:
        leaving[0][...] = jnp.where(place[1] == 0, mixed[2 * n :], mixed[:n]).astype(BF16)


def gate(branch, folded, place, after, near, far, cots, arrived, proj, mixed, earlier=None, leaves=False):
    filters = proj.shape[-1]
    first_gate = cots is None
    arrays = [near, far] + ([] if first_gate else [cots]) + ([arrived] if folded else [])
    ins = [(a, a.shape, None) for a in arrays] + [(proj, (1, filters, filters), (branch, 0, 0))]
    ins += [(a, a.shape, None) for a in ([mixed] if earlier is None else [mixed, earlier])]
    part = (filters, filters)
    shapes = [(near.shape[:3] + (2,) + near.shape[4:], BF16), (mixed.shape, F32), (part, F32)]
    if earlier is not None:
        shapes.append((part, BF16))
    if first_gate:
        shapes.append(((mixed.shape[0], 2) + mixed.shape[1:], BF16))
        shapes.append(((mixed.shape[0] // 3, 2) + mixed.shape[1:], BF16))
    if leaves:
        shapes.append(((mixed.shape[0] // 3,) + mixed.shape[1:], BF16))
    return call(
        functools.partial(gate_kernel, branch, folded, first_gate), place, 1, after, ins,
        [(shape_of(shape, kind), shape, None) for shape, kind in shapes], f"gate_{branch}",
    )


def whole_columns(place, own, other):
    thin = (-1,) + own.shape[-2:]
    own, other = own.reshape(thin), other.reshape(thin)
    first = place[0] % 2 == 0
    low = jnp.where(first, own, other)
    high = jnp.where(first, other, own)
    both = jnp.concatenate([low[:, None], high[:, None]], axis=1)
    return both.reshape(-1, own.shape[-1])


def split_by_core(place, low, high, keep_ref, send_ref):
    first = place[2] == 0
    rows = low.shape[0]
    keep_ref[:rows] = jnp.where(first, low, high)
    send_ref[:rows] = jnp.where(first, high, low).astype(send_ref.dtype)


def backward_kernel(
    branch, folded, final, chained, place, own_ref, other_ref, x_ref, arrived_ref, spread_ref, taps_ref,
    point_ref, before_ref, *refs
):
    classes, group, cols, channels = x_ref.shape
    point_grad_ref, depth_ref, grads_ref = refs[-3:]
    refs = refs[:-3]
    if chained:
        mixed_ref, refs = refs[0], refs[1:]
    upper = place[1] == 0
    pre = whole_columns(place, own_ref[0], other_ref[0])
    grads = lax.dot_general(pre, point_ref[0], (((1,), (1,)), ((), ())), preferred_element_type=F32)
    grads_ref[...] = grads.astype(BF16).reshape(grads_ref.shape)
    cells = spread_ref[...].reshape(classes * group * cols, channels)
    product = lax.dot_general(cells, pre, (((0,), (0,)), ((), ())), preferred_element_type=F32)

    @pl.when(pl.program_id(0) == 0)
    def _():
        point_grad_ref[...] = product
        depth_ref[...] = jnp.zeros_like(depth_ref)

    @pl.when(pl.program_id(0) > 0)
    def _():
        point_grad_ref[...] += product

    outs = refs[2:] if chained else refs
    pairs = row_pairs(branch, classes)

    def residue(r, carry):
        rows = [x_ref[q, r].astype(F32) for q in range(classes)]
        if folded:
            rows = class_rows(upper, rows[0], rows[2], arrived_ref[r].astype(F32))
        grads = [grads_ref[q, r].astype(F32) for q in range(classes)]
        for j in range(3):
            shifts = [moved(row, (j - 1) * branch * BASE_DILATION) for row in rows]
            first, near = shifts[0][0], [part for _, part in shifts]
            size = near[0].shape[0]
            for i in range(3):
                part = None
                for q, tap, source in pairs:
                    if tap == i:
                        term = near[source] * grads[q][first : first + size]
                        term = term.reshape(size // 8, 8, channels).sum(axis=0)
                        part = term if part is None else part + term
                if part is not None:
                    depth_ref[i * 3 + j] += part
        totals = []
        for target in range(classes):
            total = before_ref[target, r] if chained else None
            for j in (1, 0, 2):
                part = None
                for q, i, source in pairs:
                    if source == target:
                        term = grads[q] * taps_ref[branch - 1, i, j].astype(F32)[None, :]
                        part = term if part is None else part + term
                total = add_moved(total, part, -(j - 1) * branch * BASE_DILATION)
            totals.append(total)
        if chained:
            leaving_ref, stay_ref = outs[:2]
            at = pl.multiple_of(r * cols, cols)
            leaving_ref[pl.ds(at, cols)] = jnp.where(upper, totals[2], totals[0]).astype(BF16)
            stay_ref[0, r] = jnp.where(upper, totals[0], totals[1])
            stay_ref[1, r] = jnp.where(upper, totals[1], totals[2])
        else:
            for q in range(classes):
                outs[0][q, r] = totals[q]
        return carry

    lax.fori_loop(0, group, residue, 0)
    if chained:
        width, filters = mixed_ref.shape[1:]
        for r in range(group // 2):
            at = group * cols + r * width
            outs[0][at : at + width, :filters] = mixed_ref[r]
            outs[0][at : at + width, filters:] = mixed_ref[r + group // 2]

    @pl.when(pl.program_id(0) == STEPS - 1)
    def _():
        depth = depth_ref[...].sum(axis=1)
        if final:
            keep_ref, send_ref = outs[-2:]
            half, filters = channels // 2, point_grad_ref.shape[1]
            split_by_core(place, point_grad_ref[:half], point_grad_ref[half:], keep_ref, send_ref)
            if chained:
                depths = jnp.concatenate([refs[0][...], depth, refs[1][...]])
                low, high = depths[:, :filters], depths[:, filters:]
                first = place[2] == 0
                keep_ref[half : half + 27] = jnp.where(first, low, high)
                send_ref[half : half + 27] = jnp.where(first, high, low).astype(BF16)
                blank = jnp.zeros((keep_ref.shape[0] - half - 27, filters), F32)
                keep_ref[half + 27 :] = blank
                send_ref[half + 27 :] = blank.astype(BF16)
            else:
                outs[-3][...] = depth
        else:
            outs[-2][...] = point_grad_ref[...]
            outs[-1][...] = depth


def backward(
    branch, folded, final, place, after, own, other, x, arrived, spread, taps, point, before=None, depths=(),
    mixed=None
):
    classes, residues, cols, channels = x.shape
    filters = point.shape[2]
    group = residues // STEPS
    part = (1, classes, group, 2, cols // 4, filters)
    cell = (classes, group, cols, channels)
    thin = (group, cols, channels)
    chained = before is not None
    flat = (residues * cols + residues // 2 * (cols // 4), channels)
    if chained:
        outs = [
            (shape_of(flat, BF16), flat, None),
            (shape_of((2,) + x.shape[1:], F32), (2,) + thin, 1),
        ]
    else:
        outs = [(shape_of(x.shape, F32), cell, 1)]
    halves = (channels // 2 + (32 if chained else 0), filters)
    shapes = [(channels, filters), (9, channels)]
    if final:
        shapes = [halves, halves] if chained else [(9, channels), halves, halves]
    outs += [(shape_of(shape, F32), shape, None) for shape in shapes]
    if final:
        outs[-1] = (shape_of(halves, BF16), halves, None)
    small = (1, 1, 8, 128)
    return call(
        functools.partial(backward_kernel, branch, folded, final, chained), place, STEPS, after,
        [
            (own, part, 2),
            (other, part, 2),
            (x, cell, 1),
            (arrived, thin, 0) if folded else (x, small, None),
            (spread, cell, 1),
            (taps, taps.shape, None),
            (point, (1, channels, filters), (branch, 0, 0)),
            (before, cell, 1) if chained else (x, small, None),
        ]
        + ([(mixed, (group,) + mixed.shape[1:], 0)] if chained else [])
        + [(d, d.shape, None) for d in depths],
        outs, f"backward_{branch}",
        scratch=[
            pltpu.VMEM((channels, filters), F32),
            pltpu.VMEM((9, 8, channels), F32),
            pltpu.VMEM(cell, BF16),
        ],
    )


def join_kernel(place, own_ref, other_ref, x_ref, earlier_ref, pre_ref, keep_ref, send_ref, total_ref):
    pre = whole_columns(place, own_ref[0], other_ref[0])
    pre_ref[...] = pre.reshape(pre_ref.shape)
    cells = x_ref[...].reshape(-1, x_ref.shape[-1])
    product = lax.dot_general(cells, pre, (((0,), (0,)), ((), ())), preferred_element_type=F32)

    @pl.when(pl.program_id(0) == 0)
    def _():
        total_ref[...] = product

    @pl.when(pl.program_id(0) > 0)
    def _():
        total_ref[...] += product

    @pl.when(pl.program_id(0) == STEPS - 1)
    def _():
        split_by_core(place, earlier_ref[...], total_ref[...], keep_ref, send_ref)


def join(place, after, own, other, x, earlier):
    classes, residues, cols, channels = x.shape
    filters = own.shape[-1]
    group = residues // STEPS
    part = (1, classes, group, 2, cols // 4, filters)
    return call(
        join_kernel, place, STEPS, after,
        [
            (own, part, 2),
            (other, part, 2),
            (x, (classes, group, cols, channels), 1),
            (earlier, earlier.shape, None),
        ],
        [
            (shape_of((classes, residues, cols, filters), BF16), (classes, group, cols, filters), 1),
            (shape_of(earlier.shape, F32), earlier.shape, None),
            (shape_of(earlier.shape, BF16), earlier.shape, None),
        ],
        "join", scratch=[pltpu.VMEM(earlier.shape, F32)],
    )


def last_kernel(
    place, pre_ref, point_ref, band_ref, stay_ref, arrived_ref, mixed_ref, folded_ref, input_ref, output_ref
):
    classes, group, cols, channels = band_ref.shape
    pre = pre_ref[...].reshape(classes * group * cols, -1)
    grads = lax.dot_general(pre, point_ref[0], (((1,), (1,)), ((), ())), preferred_element_type=F32)
    grads = grads.astype(BF16).astype(F32).reshape(band_ref.shape)
    cells = group * cols
    arrived = arrived_ref[:cells].reshape(group, cols, channels).astype(F32)
    others = (stay_ref[0], arrived, stay_ref[1])
    for q in range(classes):
        input_ref[q] = (grads[q] + band_ref[q] + others[q]).astype(BF16)
    upper = place[1] == 0
    width, filters = mixed_ref.shape[2:]
    rest = arrived_ref[cells:].reshape(group // 2, width, channels)
    mixed = (
        jnp.where(upper, folded_ref[0], folded_ref[1]),
        jnp.concatenate([rest[..., :filters], rest[..., filters:]]).astype(F32),
        jnp.where(upper, folded_ref[1], folded_ref[2]),
    )
    for q in range(classes):
        output_ref[q] = (mixed_ref[q] + mixed[q]).astype(BF16)


def last(place, after, pre, point, band, stay, arrived, mixed, folded):
    classes, residues, cols, channels = band.shape
    filters = point.shape[2]
    group = residues // STEPS
    cell = (classes, group, cols, channels)
    thin = (classes, group) + mixed.shape[2:]
    return call(
        last_kernel, place, STEPS, after,
        [
            (pre, (classes, group, cols, filters), 1),
            (point, (1, channels, filters), (0, 0, 0)),
            (band, cell, 1),
            (stay, (2, group, cols, channels), 1),
            (arrived, arrived.shape, None),
            (mixed, thin, 1),
            (folded, thin, 1),
        ],
        [(result_of(band.shape, BF16), cell, 1), (result_of(mixed.shape, BF16), thin, 1)], "last",
    )


def add_kernel(scale, counts, place, *refs):
    terms, out_ref = refs[: sum(counts)], refs[-1]
    at = 0
    for count in counts:
        group, terms = terms[:count], terms[count:]
        values = [ref[...].astype(F32) for ref in group]
        total = sum(values[1:], values[0])
        if scale != 1.0:
            total = total * scale
        rows = group[0].shape[0]
        out_ref[at : at + rows] = total.astype(out_ref.dtype)
        at += rows


def add(name, place, after, groups, kind, scale=1.0, arrived=()):
    shape = (sum(group[0].shape[0] for group in groups), groups[0][0].shape[1])
    counts = [len(group) for group in groups]
    return call(
        functools.partial(add_kernel, scale, counts), place, 1, after,
        [(a, a.shape, None) for group in groups for a in group]
        + [(a, (1,) * (len(a.shape) - 2) + a.shape[-2:], None) for a in arrived],
        [(shape_of(shape, kind), shape, None)], name,
    )


def finish_kernel(
    place, own30, far30, own_proj, far_proj, own21, far21, low21, high21, proj_ref, depth_ref, point_ref, sems
):
    core = place[2]
    channels, filters = point_ref.shape[1:]
    half = channels // 2
    first = own21.shape[0] - half
    copies = []

    def copy(source, target):
        moving = pltpu.make_async_copy(source, target, sems.at[len(copies)])
        moving.start()
        copies.append(moving)

    for mine, pair in ((core, (own30, own_proj, own21)), (1 - core, (far30, far_proj, far21))):
        points, projs, mixed = pair
        copy(points, point_ref.at[3 - 3 * mine])
        copy(projs.at[pl.ds(0, filters)], proj_ref.at[3 - 3 * mine])
        copy(projs.at[pl.ds(filters, filters)], proj_ref.at[1 + mine])
        rows = pl.ds(pl.multiple_of(mine * half, half), half)
        copy(mixed.at[pl.ds(0, half)], point_ref.at[2, rows])
        copy(mixed.at[pl.ds(first, half)], point_ref.at[1, rows])
    low = jnp.where(core == 0, low21[...], high21[...])
    high = jnp.where(core == 0, high21[...], low21[...])
    for k in range(9):
        rows = slice(3 * k, 3 * k + 3)
        depth_ref[k // 3, k % 3, :, :filters] = low[rows]
        depth_ref[k // 3, k % 3, :, filters:] = high[rows]
    for moving in copies:
        moving.wait()


def finish(place, after, early, proj, late, channels, filters):
    arrays = [*early, *proj, *late]
    half = channels // 2
    depth_spec = pl.BlockSpec((32, filters), lambda r, p: (half // 32, 0))
    anywhere = pl.BlockSpec(memory_space=pl.ANY)
    shapes = [(4, filters, filters), (3, 3, 3, channels), (4, channels, filters)]
    out = pl.pallas_call(
        finish_kernel,
        grid_spec=pltpu.PrefetchScalarGridSpec(
            num_scalar_prefetch=1,
            grid=(1,),
            in_specs=[anywhere] * 6 + [depth_spec] * 2,
            out_specs=[anywhere, pl.BlockSpec(shapes[1], lambda r, p: (0, 0, 0, 0)), anywhere],
            scratch_shapes=[pltpu.SemaphoreType.DMA((10,))],
        ),
        out_shape=[result_of(s, F32) for s in shapes],
        compiler_params=pltpu.CompilerParams(vmem_limit_bytes=VMEM_BYTES),
        name="finish",
    )(place, *arrays, *late)
    return (*out, after)


def by_classes(features_in, depth_weights, point_weights, proj_weights, cotangent):
    _, band_rows, cols, channels = features_in.shape
    filters = point_weights.shape[2]
    classes, n = 3, band_rows // 3
    scale = 1.0 / math.sqrt(lax.axis_size("dp") * band_rows * lax.axis_size("row") * cols)
    chan, row = lax.axis_index("chan"), lax.axis_index("row")
    core = lax.axis_index("dp") % 2
    place = jnp.stack([chan, row, core]).astype(jnp.int32)
    x = features_in[0].reshape(classes, n, cols, channels)

    weights = (depth_weights, point_weights)
    cot = cotangent[0]

    token, blank = jnp.zeros(TOKEN, F32), jnp.zeros(cot.shape, F32)
    keep3, send3, spread3, token = forward(
        (3,), False, place, token, in_hbm(x), x, in_hbm(depth_weights), in_hbm(point_weights)
    )
    sent3 = swap(send3, "chan", 1)
    keep0, send0, x_leaving, token = forward(
        (0,), False, place, token, x, x, in_hbm(depth_weights), in_hbm(point_weights)
    )
    sent0 = swap(send0, "chan", 1)
    arrived = swap(x_leaving, "row", 1)
    near3, token = near_sum_cot("3", place, token, keep3, sent3, cot)
    far3 = swap(near3, "chan", 2)
    keep1, keep2, send1, send2, spread1, spread2, token = forward(
        (1, 2), True, place, token, x, arrived, *weights
    )
    sent1, sent2 = swap(send1, "chan", 1), swap(send2, "chan", 1)
    near0, token = near_sum("0", place, token, keep0, sent0)
    far0 = swap(near0, "chan", 2)
    grad3, band_mixed, proj3, cots, cots_leaving, token = gate(
        3, False, place, token, near3, far3, None, None, proj_weights, blank
    )
    other3 = swap(grad3, "chan", 1)
    cots_arrived = swap(cots_leaving, "row", 1)
    near1, token = near_sum("1", place, token, keep1, sent1)
    far1 = swap(near1, "chan", 2)
    grad0, band_mixed, proj_keep, proj_send, token = gate(
        0, False, place, token, near0, far0, cots, None, proj_weights, band_mixed, proj3
    )
    other0 = swap(grad0, "chan", 1)
    proj30 = (proj_keep, swap(proj_send, "dp", 1))
    near2, token = near_sum("2", place, token, keep2, sent2)
    far2 = swap(near2, "chan", 2)
    grad1, class_mixed, proj1, token = gate(
        1, True, place, token, near1, far1, cots, cots_arrived, proj_weights, blank
    )
    other1 = swap(grad1, "chan", 1)
    band, point3, depth3, token = backward(
        3, False, False, place, token, grad3, other3, x, x, spread3, *weights
    )
    grad2, class_mixed, proj_keep, proj_send, mixed_leaving, token = gate(
        2, True, place, token, near2, far2, cots, cots_arrived, proj_weights, class_mixed, proj1,
        leaves=True,
    )
    other2 = swap(grad2, "chan", 1)
    proj12 = (proj_keep, swap(proj_send, "dp", 1))
    pre0, point_keep, point_send, token = join(place, token, grad0, other0, x, point3)
    point30 = (point_keep, swap(point_send, "dp", 1))
    total1, depth1, point_keep, point_send, token = backward(
        1, True, True, place, token, grad1, other1, x, arrived, spread1, *weights
    )
    point1 = (point_keep, swap(point_send, "dp", 1))
    proj, token = add("proj", place, token, [proj30, proj12], BF16)
    proj = (proj, swap(proj, "chan", 1))
    early, token = add("early_1", place, token, [point30], BF16)
    early = (early, swap(early, "row", 1))
    leaving, stay, late_keep, late_send, token = backward(
        2, True, True, place, token, grad2, other2, x, arrived, spread2, *weights, before=total1,
        depths=(depth1, depth3), mixed=mixed_leaving,
    )
    input_arrived = swap(leaving, "row", 1)
    late = (late_keep, swap(late_send, "dp", 1))
    proj, token = add("proj_1", place, token, [proj], BF16, arrived=[early[1]])
    proj = (proj, swap(proj, "row", 1))
    late, token = add("late_1", place, token, [late, point1], BF16)
    late = (late, swap(late, "dp", 2))
    late, token = add("late_2", place, token, [late], BF16)
    late = (late, swap(late, "row", 1))
    early, token = add("early_2", place, token, [early], BF16)
    early = (early, swap(early, "dp", 2))
    proj, token = add("proj_2", place, token, [proj], BF16)
    proj = (proj, swap(proj, "dp", 2))
    early, token = add("early", place, token, [early], F32, scale)
    early = (early, swap(early, "dp", 1))
    proj, token = add("proj_sum", place, token, [proj], F32, scale)
    proj = (proj, swap(proj, "dp", 1))
    late, token = add("late", place, token, [late], F32, scale, arrived=[input_arrived])
    late = (late, swap(late, "dp", 1))
    bands = band_mixed.reshape((classes, n) + band_mixed.shape[1:])
    folds = class_mixed.reshape(bands.shape)
    grad_input, output, token = last(
        place, token, pre0, point_weights, band, stay, input_arrived, bands, folds
    )
    grad_proj, grad_depth, grad_point, token = finish(
        place, token, early, proj, late, channels, filters
    )
    return (
        output.reshape(cotangent.shape), grad_input.reshape(features_in.shape), grad_depth, grad_point,
        grad_proj,
    )


def shifted(value, axis, steps):
    count = lax.axis_size(axis)
    first, last = (max(0, -steps), min(count, count - steps))
    return lax.ppermute(value, axis, [(source, source + steps) for source in range(first, last)])


def window(source, top, left, band_rows, band_cols):
    upper = lax.slice_in_dim(source, top, top + band_rows, axis=1)
    return lax.slice_in_dim(upper, left, left + band_cols, axis=2)


def on_device(features_in, depth_weights, point_weights, proj_weights, cotangent):
    samples, band_rows, band_cols, channels = features_in.shape
    weight_scale = 1.0 / math.sqrt(
        samples * lax.axis_size("dp") * band_rows * lax.axis_size("row") * band_cols
    )
    largest_reach = 3 * BASE_DILATION
    offsets = (2, 1, -1, -2)
    arrivals = []
    for offset in offsets:
        arrivals.append(shifted(features_in, "row", offset))
    tall_rows = jnp.concatenate(
        [arrivals[0], arrivals[1], features_in, arrivals[2], arrivals[3]], axis=1
    )
    padded = jnp.pad(tall_rows, ((0, 0), (0, 0), (largest_reach, largest_reach), (0, 0)))
    branch_maps = [features_in]
    for branch_level in range(3):
        tap_spacing = (branch_level + 1) * BASE_DILATION
        summed = jnp.zeros(features_in.shape, jnp.float32)
        for row_tap in range(3):
            for col_tap in range(3):
                input_kernel_tap = window(
                    padded,
                    largest_reach + (row_tap - 1) * tap_spacing,
                    largest_reach + (col_tap - 1) * tap_spacing,
                    band_rows,
                    band_cols,
                )
                summed = summed + input_kernel_tap.astype(jnp.float32) * depth_weights[
                    branch_level, row_tap, col_tap
                ].astype(jnp.float32)
        branch_maps.append(summed.astype(jnp.bfloat16))
    spread = jnp.stack(branch_maps)
    full_point = lax.all_gather(point_weights, "chan", axis=1, tiled=True)
    preact = jnp.einsum(
        "bsrwc,bcf->bsrwf",
        lax.all_to_all(spread, "chan", split_axis=3, concat_axis=4, tiled=True),
        full_point,
        preferred_element_type=jnp.float32,
    )
    activation = jax.nn.silu(preact).astype(jnp.bfloat16)
    output = jnp.einsum(
        "bsrwf,bfg->srwg", activation, proj_weights, preferred_element_type=jnp.float32
    ).astype(jnp.bfloat16)
    silu_gradient = jnp.einsum(
        "srwg,bfg->bsrwf", cotangent, proj_weights, preferred_element_type=jnp.float32
    )
    logistic = jax.nn.sigmoid(preact)
    pre_grad = (silu_gradient * logistic * (1.0 + preact * (1.0 - logistic))).astype(jnp.bfloat16)
    proj_term = jnp.einsum(
        "bsrwf,srwg->bfg", activation, cotangent, preferred_element_type=jnp.float32
    )
    grad_proj = lax.psum(proj_term, ("row", "chan", "dp")) * weight_scale
    incoming = lax.all_gather(pre_grad, "chan", axis=3, tiled=True)
    local_grad = jnp.einsum(
        "bsrwf,bcf->bsrwc", incoming, point_weights, preferred_element_type=jnp.float32
    ).astype(jnp.bfloat16)
    spread_grad = local_grad
    point_sum = jnp.einsum("bsrwc,bsrwf->bcf", spread, incoming, preferred_element_type=jnp.float32)
    spread_grad, point_term = (spread_grad, point_sum)
    depth_rows = []
    for branch_level in range(3):
        tap_spacing = (branch_level + 1) * BASE_DILATION
        branch_grad = spread_grad[branch_level + 1].astype(jnp.float32)
        gathered = []
        for row_tap in range(3):
            for col_tap in range(3):
                input_kernel_tap = window(
                    padded,
                    largest_reach + (row_tap - 1) * tap_spacing,
                    largest_reach + (col_tap - 1) * tap_spacing,
                    band_rows,
                    band_cols,
                )
                gathered.append(
                    jnp.sum(input_kernel_tap.astype(jnp.float32) * branch_grad, axis=(0, 1, 2))
                )
        depth_rows.append(jnp.stack(gathered).reshape(3, 3, channels))
    depth_term = jnp.stack(depth_rows)
    point_summed, depth_summed = lax.psum((point_term, depth_term), ("row", "dp"))
    grad_point = point_summed * weight_scale
    grad_depth = depth_summed * weight_scale
    neighbour_sets = []
    for branch_level in range(3):
        neighbour_sets.append(
            [shifted(spread_grad[branch_level + 1], "row", offset) for offset in offsets]
        )
    grad_in = spread_grad[0].astype(jnp.float32)
    for branch_level in range(3):
        tap_spacing = (branch_level + 1) * BASE_DILATION
        received = neighbour_sets[branch_level]
        grad_tall = jnp.concatenate(
            [received[0], received[1], spread_grad[branch_level + 1], received[2], received[3]],
            axis=1,
        )
        grad_padded = jnp.pad(grad_tall, ((0, 0), (0, 0), (largest_reach, largest_reach), (0, 0)))
        for row_tap in range(3):
            for col_tap in range(3):
                grad_tap = window(
                    grad_padded,
                    largest_reach - (row_tap - 1) * tap_spacing,
                    largest_reach - (col_tap - 1) * tap_spacing,
                    band_rows,
                    band_cols,
                )
                grad_in = grad_in + grad_tap.astype(jnp.float32) * depth_weights[
                    branch_level, row_tap, col_tap
                ].astype(jnp.float32)
    return (output, grad_in.astype(jnp.bfloat16), grad_depth, grad_point, grad_proj)


def folds(mesh, features_in, point_weights):
    sizes = mesh.shape
    samples, rows, cols, channels = features_in.shape
    return (
        rows == 3 * BASE_DILATION
        and sizes["row"] == 2
        and sizes["chan"] == 4
        and sizes["dp"] == 4
        and samples == sizes["dp"]
        and cols % 64 == 0
        and channels % (128 * sizes["chan"]) == 0
        and channels == 2 * sizes["chan"] * point_weights.shape[2]
    )


def solution(mesh):
    in_specs = (
        P("dp", "row", None, "chan"),
        P(None, None, None, "chan"),
        P(None, "chan", None),
        P(),
        P("dp", "row", "chan", None),
    )
    out_specs = (
        P("dp", "row", "chan", None),
        P("dp", "row", None, "chan"),
        P(None, None, None, "chan"),
        P(None, "chan", None),
        P(),
    )

    def run(*args):
        body = by_classes if folds(mesh, args[0], args[2]) else on_device
        return jax.shard_map(
            body, mesh=mesh, in_specs=in_specs, out_specs=out_specs, check_vma=False
        )(*args)

    return run
```
